256 devices in a mesh: seq: 64 (over y, z, x_hi), rep: 4 (over x_lo, core).
Axes of the slice: x: 4 (x_hi: 2, x_lo: 2; x = x_hi * 2 + x_lo), y: 4, z: 8, core: 2. Of those that a mesh axis runs over, the one named last changes fastest.
Arguments:
- queries: bfloat16 [4, 8192, 1024], P('rep', 'seq'), may hold values from -24 to 24
- keys: bfloat16 [4, 8192, 1024], P('rep', 'seq'), may hold values from -24 to 24
- values: bfloat16 [4, 8192, 1024], P('rep', 'seq'), may hold values from -6 to 6
- w_out: bfloat16 [1024, 2048], P('rep'), may hold values from -0.1875 to 0.1875
- d_out: bfloat16 [4, 8192, 2048], P('rep', 'seq'), may hold values from -6 to 6
- rand_slot: int32 [4, 64, 6], P('rep', 'seq'), may hold values from 0 to 1
- global_ids: int32 [4, 2], P('rep'), may hold values from 0 to 127
Outputs:
- layer_out: bfloat16 [4, 8192, 2048], P('rep', 'seq')
- query_grad: bfloat16 [4, 8192, 1024], P('rep', 'seq')
- key_grad: bfloat16 [4, 8192, 1024], P('rep', 'seq')
- value_grad: bfloat16 [4, 8192, 1024], P('rep', 'seq')
- weight_grad: float32 [1024, 2048], P(('seq', 'rep'))
The draws below stay inside these ranges and needn't reach their ends.
Inputs may be any that keep to these rules, and one draw needn't show every extreme that they name: `rand_slot`: entries name a block by its position 0 to 1 within its stretch.
All inputs are finite; a program needn't handle non-finite values.
Results may differ from the reference program's by a relative error of at most 0.014.
Values may be sent and summed in bfloat16 or wider, within the bound.
No kernel may reach another device: no remote copies, remote signals or barrier semaphores. Data moves between devices by JAX's collectives and lax.ppermute only.
A program may use at most 128 MiB of HBM per device.

```python
import jax
import jax.numpy as jnp
from jax import lax

D = 2048
HEADS = 8
HEAD_DIM = 128
BLK = 64
GLOB = 2
TOK_DEV = 128
BITS = 6
NBLK_DEV = 2
HD = 1024
SEQ_LEN = 8192
NBLK = 128
REPS = 4
N_SEQ = 64


def shared_dirs(key):
    return jax.random.normal(key, (REPS, SEQ_LEN, HEADS * HEAD_DIM), jnp.float32)


def draw_queries(key, part):
    directions = shared_dirs(key)
    key = jax.random.fold_in(key, 11)
    base = jax.random.normal(key, directions.shape, jnp.float32)
    return jnp.clip(base, -24.0, 24.0).astype(jnp.bfloat16)


def draw_keys(key, part):
    directions = shared_dirs(key)
    key = jax.random.fold_in(key, 23)
    base = jax.random.normal(key, directions.shape, jnp.float32)
    return jnp.clip(base, -24.0, 24.0).astype(jnp.bfloat16)


def place_ends(drawn, own_key, least, top_value):
    longest = drawn.shape.index(max(drawn.shape))
    spots = []
    for shift in (0, 1):
        where = [jax.random.randint(jax.random.fold_in(own_key, axis), (), 0, length) for axis, length in enumerate(drawn.shape)]
        where[longest] = (where[longest] + shift) % drawn.shape[longest]
        spots.append(tuple(where))
    return drawn.at[spots[0]].set(least).at[spots[1]].set(top_value)


def levels(own_key, shape, split, low, largest):
    factor_of = 1.0
    for dim, parts in split:
        draws = jax.random.uniform(jax.random.fold_in(jax.random.fold_in(own_key, 6), dim), (parts,), jnp.float32, low / len(split), largest / len(split))
        factor_of = factor_of * jnp.repeat(jnp.exp(draws), shape[dim] // parts).reshape((-1,) + (1,) * (len(shape) - 1 - dim))
    return factor_of


def scatter_about(key, extent, deviation, reach, split=(), kind=jnp.bfloat16):
    entries = deviation * jax.random.normal(key, extent, jnp.float32)
    if split:
        entries = entries * levels(key, extent, split, -0.22, 0.18)
    return jnp.clip(entries, -reach, reach).astype(kind)


def setup_inputs(seed: int = 0) -> dict:
    seeds = jax.random.split(jax.random.key(seed), 8)
    return {
        "queries": draw_queries(jax.random.fold_in(seeds[7], 71), 0),
        "keys": draw_keys(jax.random.fold_in(seeds[7], 71), 0),
        "values": scatter_about(seeds[2], (REPS, SEQ_LEN, HD), 1.0, 6.0, ((0, 4), (1, 64))),
        "w_out": scatter_about(seeds[3], (HD, D), HD ** -0.5, 0.1875, ((0, 4),)),
        "d_out": scatter_about(seeds[4], (REPS, SEQ_LEN, D), 1.0, 6.0, ((0, 4), (1, 64))),
        "rand_slot": place_ends(jax.random.randint(seeds[5], (REPS, N_SEQ, BITS), 0, NBLK_DEV), jax.random.fold_in(seeds[5], 1), 0, NBLK_DEV - 1).astype(jnp.int32),
        "global_ids": place_ends(jax.random.randint(seeds[6], (REPS, GLOB), 0, NBLK), jax.random.fold_in(seeds[6], 1), 0, NBLK - 1).astype(jnp.int32),
    }


def mult(form, left, right):
    return jnp.einsum(form, left.astype(jnp.float32), right.astype(jnp.float32))


def local_attention(q_dev, padded, global_kv, partner_kv, my_slots, d_attn):
    nblock = q_dev.shape[0] // BLK
    width = HEADS * HEAD_DIM
    scale = HEAD_DIM ** -0.5
    queries = q_dev.reshape(nblock, BLK, HEADS, HEAD_DIM)
    grads_in = d_attn.reshape(nblock, BLK, HEADS, HEAD_DIM)
    blocks = padded.reshape(2, nblock + 2, BLK, HEADS, HEAD_DIM)
    window = jnp.concatenate([blocks[:, 0:nblock], blocks[:, 1:nblock + 1], blocks[:, 2:nblock + 2]], axis=2)
    glob_heads = global_kv.reshape(2, -1, HEADS, HEAD_DIM)
    rand_heads = partner_kv.reshape(2, -1, HEADS, HEAD_DIM)
    wide = 3 * BLK
    gwide = glob_heads.shape[1]
    owned = my_slots[None, :] == jnp.arange(nblock, dtype=jnp.int32)[:, None]
    keep_rand = jnp.repeat(owned, BLK, axis=1)
    s_win = mult('nqhd,nkhd->nhqk', queries, window[0]) * scale
    s_glob = mult('nqhd,khd->nhqk', queries, glob_heads[0]) * scale
    s_rand = mult('nqhd,khd->nhqk', queries, rand_heads[0]) * scale
    s_rand = jnp.where(keep_rand[:, None, None, :], s_rand, jnp.float32(-1e30))
    scores = jnp.concatenate([s_win, s_glob, s_rand], axis=-1)
    top_score = jnp.max(scores, axis=-1, keepdims=True)
    expd = jnp.exp(scores - top_score)
    probs = expd / jnp.sum(expd, axis=-1, keepdims=True)
    probs_b = probs.astype(jnp.bfloat16)
    p_win = probs_b[..., :wide]
    p_glob = probs_b[..., wide:wide + gwide]
    p_rand = probs_b[..., wide + gwide:]
    output = mult('nhqk,nkhd->nqhd', p_win, window[1]) + mult('nhqk,khd->nqhd', p_glob, glob_heads[1]) + mult('nhqk,khd->nqhd', p_rand, rand_heads[1])
    attn = output.astype(jnp.bfloat16).reshape(nblock * BLK, width)
    dprob = jnp.concatenate([mult('nqhd,nkhd->nhqk', grads_in, window[1]), mult('nqhd,khd->nhqk', grads_in, glob_heads[1]), mult('nqhd,khd->nhqk', grads_in, rand_heads[1])], axis=-1)
    delta = jnp.sum(dprob * probs, axis=-1, keepdims=True)
    dscore = (probs * (dprob - delta) * scale).astype(jnp.bfloat16)
    d_win = dscore[..., :wide]
    d_glob = dscore[..., wide:wide + gwide]
    d_rand = dscore[..., wide + gwide:]
    query_grad = mult('nhqk,nkhd->nqhd', d_win, window[0]) + mult('nhqk,khd->nqhd', d_glob, glob_heads[0]) + mult('nhqk,khd->nqhd', d_rand, rand_heads[0])
    query_grad = query_grad.reshape(nblock * BLK, width)
    dk_win = mult('nhqk,nqhd->nkhd', d_win, queries)
    dv_win = mult('nhqk,nqhd->nkhd', p_win, grads_in)
    dkv_win = jnp.stack([dk_win, dv_win]).reshape(2, nblock, 3, BLK, width)
    zeros_one = jnp.zeros((2, 1, BLK, width), jnp.float32)
    dpad = jnp.concatenate([dkv_win[:, :, 0], zeros_one, zeros_one], axis=1)
    dpad = dpad + jnp.concatenate([zeros_one, dkv_win[:, :, 1], zeros_one], axis=1)
    dpad = dpad + jnp.concatenate([zeros_one, zeros_one, dkv_win[:, :, 2]], axis=1)
    dglob = jnp.stack([mult('nhqk,nqhd->khd', d_glob, queries), mult('nhqk,nqhd->khd', p_glob, grads_in)]).reshape(2, gwide, width)
    drand = jnp.stack([mult('nhqk,nqhd->khd', d_rand, queries), mult('nhqk,nqhd->khd', p_rand, grads_in)]).reshape(2, -1, width)
    return attn, query_grad, dpad, dglob, drand


def reference(queries, keys, values, w_out, d_out, rand_slot, global_ids):
    nseq = N_SEQ
    nblock = TOK_DEV // BLK
    width = HEADS * HEAD_DIM
    outs_y, outs_q, outs_k, outs_v = [], [], [], []
    weight_total = jnp.zeros((width, D), jnp.float32)
    stretch = jnp.arange(nseq, dtype=jnp.int32)
    bit_ids = jnp.arange(BITS, dtype=jnp.int32)
    partner = jnp.bitwise_xor(stretch[:, None], jnp.left_shift(jnp.int32(1), bit_ids)[None, :])
    block_ids = jnp.arange(nblock, dtype=jnp.int32)
    for replica in range(REPS):
        q_all = queries[replica].reshape(nseq, TOK_DEV, width)
        key_vals = jnp.stack([keys[replica], values[replica]]).reshape(2, nseq, TOK_DEV, width)
        before = jnp.roll(key_vals, 1, axis=1)[:, :, TOK_DEV - BLK:]
        after = jnp.roll(key_vals, -1, axis=1)[:, :, :BLK]
        padded = jnp.concatenate([before, key_vals, after], axis=2)
        kv_blocks = key_vals.reshape(2, nseq, nblock, BLK, width)
        slots = rand_slot[replica]
        partner_slot = slots[partner, bit_ids[None, :]]
        partner_kv = kv_blocks[:, partner, partner_slot]
        gids = global_ids[replica]
        global_kv = kv_blocks[:, gids // nblock, gids % nblock].reshape(2, GLOB * BLK, width)
        d_attn = jnp.dot(d_out[replica], w_out.T, preferred_element_type=jnp.float32).astype(jnp.bfloat16)

        def per_stretch(items):
            q_dev, pad_dev, rand_dev, slot_dev, grad_dev = items
            return local_attention(q_dev, pad_dev, global_kv, rand_dev.reshape(2, BITS * BLK, width), slot_dev, grad_dev)

        attn, query_grad, dpad, dglob, drand = lax.map(per_stretch, (q_all, jnp.moveaxis(padded, 1, 0), jnp.moveaxis(partner_kv, 1, 0), slots, d_attn.reshape(nseq, TOK_DEV, width)))
        own = dpad[:, :, 1:nblock + 1]
        from_right = jnp.roll(dpad[:, :, 0], -1, axis=0)
        from_left = jnp.roll(dpad[:, :, nblock + 1], 1, axis=0)
        own = own.at[:, :, nblock - 1].add(from_right)
        own = own.at[:, :, 0].add(from_left)
        drand_blocks = drand.reshape(nseq, 2, BITS, BLK, width)
        returned = drand_blocks[partner, :, bit_ids[None, :]]
        one_hot = (slots[:, :, None] == block_ids[None, None, :]).astype(jnp.float32)
        own = own + jnp.einsum('sbn,sbcxh->scnxh', one_hot, returned, precision=lax.Precision.HIGHEST)
        glob_total = jnp.sum(dglob, axis=0).reshape(2, GLOB, BLK, width)
        own_all = jnp.transpose(own, (1, 0, 2, 3, 4)).reshape(2, nseq * nblock, BLK, width)
        own_all = own_all.at[:, gids].add(glob_total)
        attn_flat = attn.reshape(SEQ_LEN, width)
        outs_y.append(jnp.dot(attn_flat, w_out, preferred_element_type=jnp.float32).astype(jnp.bfloat16))
        outs_q.append(query_grad.reshape(SEQ_LEN, width).astype(jnp.bfloat16))
        outs_k.append(own_all[0].reshape(SEQ_LEN, width).astype(jnp.bfloat16))
        outs_v.append(own_all[1].reshape(SEQ_LEN, width).astype(jnp.bfloat16))
        weight_total = weight_total + jnp.dot(attn_flat.T, d_out[replica], preferred_element_type=jnp.float32)
    return jnp.stack(outs_y), jnp.stack(outs_q), jnp.stack(outs_k), jnp.stack(outs_v), weight_total
```

```python
import jax
import jax.numpy as jnp
from jax import lax
from jax.sharding import PartitionSpec as P

HEADS = 8
HEAD_DIM = 128
BLK = 64
GLOB = 2


def shifted(value, axis, steps):
    count = lax.axis_size(axis)
    pairs = [(source, (source + steps) % count) for source in range(count)]
    return lax.ppermute(value, axis, pairs)


def padded_2(block, sides, width):
    for axis, dim in sides:
        count = lax.axis_size(axis)
        forward = [(i, i + 1) for i in range(count - 1)]
        forward.append((count - 1, 0))
        backward = [(target, source) for source, target in forward]
        low = lax.ppermute(
            lax.slice_in_dim(block, block.shape[dim] - width, None, axis=dim), axis, forward
        )
        high = lax.ppermute(lax.slice_in_dim(block, 0, width, axis=dim), axis, backward)
        block = jnp.concatenate([low, block, high], axis=dim)
    return block


def swapped(block, axis, stride):
    count = lax.axis_size(axis)
    route = []
    for low in range(count):
        high = low | 1 << stride
        if high != low and high < count:
            route += [(low, high), (high, low)]
    return lax.ppermute(block, axis, route)


def mult(form, left, right):
    return jnp.einsum(form, left, right, preferred_element_type=jnp.float32)


def local_attention(q_dev, padded, global_kv, partner_kv, my_slots, d_attn):
    nblock = q_dev.shape[0] // BLK
    width = HEADS * HEAD_DIM
    scale = HEAD_DIM ** (-0.5)
    queries = q_dev.reshape(nblock, BLK, HEADS, HEAD_DIM)
    grads_in = d_attn.reshape(nblock, BLK, HEADS, HEAD_DIM)
    blocks = padded.reshape(2, nblock + 2, BLK, HEADS, HEAD_DIM)
    window = jnp.concatenate(
        [blocks[:, 0:nblock], blocks[:, 1 : nblock + 1], blocks[:, 2 : nblock + 2]], axis=2
    )
    glob_heads = global_kv.reshape(2, -1, HEADS, HEAD_DIM)
    rand_heads = partner_kv.reshape(2, -1, HEADS, HEAD_DIM)
    wide = 3 * BLK
    gwide = glob_heads.shape[1]
    owned = my_slots[None, :] == jnp.arange(nblock, dtype=jnp.int32)[:, None]
    keep_rand = jnp.repeat(owned, BLK, axis=1)
    s_win = mult("nqhd,nkhd->nhqk", queries, window[0]) * scale
    s_glob = mult("nqhd,khd->nhqk", queries, glob_heads[0]) * scale
    s_rand = mult("nqhd,khd->nhqk", queries, rand_heads[0]) * scale
    s_rand = jnp.where(keep_rand[:, None, None, :], s_rand, jnp.float32(-1e30))
    scores = jnp.concatenate([s_win, s_glob, s_rand], axis=-1)
    top_score = jnp.max(scores, axis=-1, keepdims=True)
    expd = jnp.exp(scores - top_score)
    probs = expd / jnp.sum(expd, axis=-1, keepdims=True)
    probs_b = probs.astype(jnp.bfloat16)
    p_win = probs_b[..., :wide]
    p_glob = probs_b[..., wide : wide + gwide]
    p_rand = probs_b[..., wide + gwide :]
    output = (
        mult("nhqk,nkhd->nqhd", p_win, window[1])
        + mult("nhqk,khd->nqhd", p_glob, glob_heads[1])
        + mult("nhqk,khd->nqhd", p_rand, rand_heads[1])
    )
    attn = output.astype(jnp.bfloat16).reshape(nblock * BLK, width)
    dprob = jnp.concatenate(
        [
            mult("nqhd,nkhd->nhqk", grads_in, window[1]),
            mult("nqhd,khd->nhqk", grads_in, glob_heads[1]),
            mult("nqhd,khd->nhqk", grads_in, rand_heads[1]),
        ],
        axis=-1,
    )
    delta = jnp.sum(dprob * probs, axis=-1, keepdims=True)
    dscore = (probs * (dprob - delta) * scale).astype(jnp.bfloat16)
    d_win = dscore[..., :wide]
    d_glob = dscore[..., wide : wide + gwide]
    d_rand = dscore[..., wide + gwide :]
    query_grad = (
        mult("nhqk,nkhd->nqhd", d_win, window[0])
        + mult("nhqk,khd->nqhd", d_glob, glob_heads[0])
        + mult("nhqk,khd->nqhd", d_rand, rand_heads[0])
    )
    query_grad = query_grad.reshape(nblock * BLK, width)
    dk_win = mult("nhqk,nqhd->nkhd", d_win, queries)
    dv_win = mult("nhqk,nqhd->nkhd", p_win, grads_in)
    dkv_win = jnp.stack([dk_win, dv_win]).reshape(2, nblock, 3, BLK, width)
    zeros_one = jnp.zeros((2, 1, BLK, width), jnp.float32)
    dpad = jnp.concatenate([dkv_win[:, :, 0], zeros_one, zeros_one], axis=1)
    dpad = dpad + jnp.concatenate([zeros_one, dkv_win[:, :, 1], zeros_one], axis=1)
    dpad = dpad + jnp.concatenate([zeros_one, zeros_one, dkv_win[:, :, 2]], axis=1)
    dglob = jnp.stack(
        [mult("nhqk,nqhd->khd", d_glob, queries), mult("nhqk,nqhd->khd", p_glob, grads_in)]
    ).reshape(2, gwide, width)
    drand = jnp.stack(
        [mult("nhqk,nqhd->khd", d_rand, queries), mult("nhqk,nqhd->khd", p_rand, grads_in)]
    ).reshape(2, -1, width)
    return (attn, query_grad, dpad, dglob, drand)


def stretch_id(y, z, x):
    return y * 16 + z * 2 + x


Z_GROUPS = [[stretch_id(y, z, x) for z in range(8)] for y in range(4) for x in range(2)]
YX_GROUPS = [[stretch_id(y, z, x) for y in range(4) for x in range(2)] for z in range(8)]


def trade(value, groups):
    return lax.all_to_all(value, "seq", 0, 0, axis_index_groups=groups, tiled=True)


def summed(value):
    return jnp.sum(value.astype(jnp.float32), axis=0)


def spread_global(picked):
    chunks = picked.reshape(8, 32, 1024)
    mine = summed(trade(chunks, Z_GROUPS)).astype(jnp.bfloat16)
    mine = summed(trade(jnp.broadcast_to(mine, (8, 32, 1024)), YX_GROUPS)).astype(jnp.bfloat16)
    return trade(jnp.broadcast_to(mine, (8, 32, 1024)), Z_GROUPS).reshape(2, GLOB * BLK, 1024)


def reduce_global(dglob, weight_part, owner, my_index):
    slots = jnp.arange(8, dtype=jnp.int32)
    owner_z = (owner // 2) % 8
    owner_m = (owner // 16) * 2 + owner % 2
    my_m = (my_index // 16) * 2 + my_index % 2
    which = (my_m // 2) % 2
    chunks = dglob.reshape(8, 32, 1024).astype(jnp.bfloat16)
    mine = summed(trade(chunks, YX_GROUPS)).astype(jnp.bfloat16)
    routed = jnp.where((slots == owner_z[which])[:, None, None], mine[None], jnp.bfloat16(0))
    mine = summed(trade(routed, Z_GROUPS)).astype(jnp.bfloat16)
    routed = jnp.where((slots == owner_m[which])[:, None, None], mine[None], jnp.bfloat16(0))
    weight_rows = weight_part.astype(jnp.bfloat16).reshape(8, 8, 1024)
    both = trade(jnp.concatenate([routed, weight_rows], axis=1), YX_GROUPS)
    total = both[:, :32].astype(jnp.float32).reshape(2, GLOB, BLK, 1024)
    return total, summed(both[:, 32:]).reshape(4, 2048)


def feature_order():
    new = jnp.arange(1024, dtype=jnp.int32)
    r, z, y, x, j = new // 256, (new // 32) % 8, (new // 8) % 4, (new // 4) % 2, new % 4
    old = y * 256 + z * 32 + x * 16 + r * 4 + j
    return (jnp.arange(1024, dtype=jnp.int32)[:, None] == old[None, :]).astype(jnp.bfloat16)


def per_device(queries, keys, values, w_out, d_out, rand_slot, global_ids):
    q_dev = queries[0]
    tok_rows = q_dev.shape[0]
    width = q_dev.shape[1]
    nblock = tok_rows // BLK
    key_vals = jnp.stack([keys[0], values[0]])
    my_slots = rand_slot[0, 0]
    gids = global_ids[0]
    grad_out = d_out[0]
    my_index = lax.axis_index("seq")
    nbits = lax.axis_size("seq").bit_length() - 1
    block_ids = jnp.arange(nblock, dtype=jnp.int32)
    all_grads = lax.all_gather(grad_out, "rep", axis=0, tiled=False)
    all_w = lax.all_gather(w_out, "rep", axis=0, tiled=True)
    d_attn = lax.dot_general(
        grad_out, all_w, (((1,), (1,)), ((), ())), preferred_element_type=jnp.float32
    ).astype(jnp.bfloat16)
    padded = padded_2(key_vals, (("seq", 1),), BLK)
    received = []
    for bit_num in range(nbits):
        chosen = lax.dynamic_slice_in_dim(key_vals, my_slots[bit_num] * BLK, BLK, 1)
        received.append(swapped(chosen, "seq", bit_num))
    partner_kv = jnp.concatenate(received, axis=1)
    owner = gids // nblock
    position = gids % nblock
    place = (position[:, None] == block_ids[None, :]) & (owner[:, None] == my_index)
    blocks = key_vals.reshape(2, nblock, BLK, width)
    picked = jnp.stack(
        [
            jnp.where(
                owner[g] == my_index,
                jnp.where(position[g] == 0, blocks[:, 0], blocks[:, 1]),
                jnp.bfloat16(0),
            )
            for g in range(GLOB)
        ],
        axis=1,
    )
    global_kv = spread_global(picked)
    attn, query_grad, dpad, dglob, drand = local_attention(
        q_dev, padded, global_kv, partner_kv, my_slots, d_attn
    )
    ordered = jnp.dot(attn, feature_order(), preferred_element_type=jnp.float32)
    ordered = ordered.astype(jnp.bfloat16).reshape(tok_rows, 4, 256).transpose(1, 0, 2)
    columns = lax.all_to_all(ordered, "rep", 0, 0, tiled=True)
    weight_part = lax.psum_scatter(
        lax.dot_general(
            columns.reshape(4 * tok_rows, 256),
            all_grads.reshape(4 * tok_rows, 2048),
            (((0,), (0,)), ((), ())),
            preferred_element_type=jnp.float32,
        ),
        "seq",
        scatter_dimension=0,
        axis_index_groups=Z_GROUPS,
        tiled=True,
    )
    own = dpad[:, 1 : nblock + 1]
    from_right = shifted(dpad[:, 0].astype(jnp.bfloat16), "seq", -1).astype(jnp.float32)
    from_left = shifted(dpad[:, nblock + 1].astype(jnp.bfloat16), "seq", 1).astype(jnp.float32)
    own = own.at[:, nblock - 1].add(from_right)
    own = own.at[:, 0].add(from_left)
    for bit_num in range(nbits):
        back = drand[:, bit_num * BLK : (bit_num + 1) * BLK].astype(jnp.bfloat16)
        sent_back = swapped(back, "seq", bit_num).astype(jnp.float32)
        slot_mask = (block_ids == my_slots[bit_num]).astype(jnp.float32)
        own = own + slot_mask[None, :, None, None] * sent_back[:, None]
    glob_total, weight_grad = reduce_global(dglob, weight_part, owner, my_index)
    for g in range(GLOB):
        own = own + place[g].astype(jnp.float32)[None, :, None, None] * glob_total[:, g][:, None]
    layer_out = jnp.dot(attn, all_w, preferred_element_type=jnp.float32)
    return (
        layer_out.astype(jnp.bfloat16)[None],
        query_grad.astype(jnp.bfloat16)[None],
        own[0].reshape(tok_rows, width).astype(jnp.bfloat16)[None],
        own[1].reshape(tok_rows, width).astype(jnp.bfloat16)[None],
        weight_grad,
    )


def solution(mesh):
    return jax.shard_map(
        per_device,
        mesh=mesh,
        in_specs=(
            P("rep", "seq", None),
            P("rep", "seq", None),
            P("rep", "seq", None),
            P("rep", None),
            P("rep", "seq", None),
            P("rep", "seq", None),
            P("rep", None),
        ),
        out_specs=(
            P("rep", "seq", None),
            P("rep", "seq", None),
            P("rep", "seq", None),
            P("rep", "seq", None),
            P(("seq", "rep"), None),
        ),
        check_vma=False,
    )
```

```python
import jax
import jax.numpy as jnp
from jax import lax
from jax.experimental import pallas as pl
from jax.experimental.pallas import tpu as pltpu
from jax.sharding import PartitionSpec as P

HEADS = 8
HEAD_DIM = 128
BLK = 64
GLOB = 2
BITS = 6
TOK = 128
WIDTH = HEADS * HEAD_DIM
D = 2048
KEYS = 768
SCALE = HEAD_DIM ** (-0.5)
BF = jnp.bfloat16
F32 = jnp.float32
ROWS = (((1,), (1,)), ((), ()))
COLS = (((0,), (0,)), ((), ()))
PLAIN = (((1,), (0,)), ((), ()))
VMEM_LIMIT = 48 * 1024 * 1024


def stretch_id(y, z, x):
    return y * 16 + z * 2 + x


Z_GROUPS = [[stretch_id(y, z, x) for z in range(8)] for y in range(4) for x in range(2)]
YX_GROUPS = [[stretch_id(y, z, x) for y in range(4) for x in range(2)] for z in range(8)]


def mm(left, right, dims):
    return lax.dot_general(left, right, dims, preferred_element_type=F32)


def trade(value, groups):
    return lax.all_to_all(value, "seq", 0, 0, axis_index_groups=groups, tiled=True)


def shifted(value, steps):
    return lax.ppermute(value, "seq", [(s, (s + steps) % 64) for s in range(64)])


def swapped(value, bit):
    return lax.ppermute(value, "seq", [(s, s ^ (1 << bit)) for s in range(64)])


def smem():
    return pl.BlockSpec(memory_space=pltpu.SMEM)


def params(**kw):
    return pltpu.CompilerParams(vmem_limit_bytes=VMEM_LIMIT, **kw)


def where_of(rand_slot, global_ids):
    me = lax.axis_index("seq")
    owner = global_ids // 2
    here = jnp.where(owner == me, global_ids % 2, -1)
    my_m = (me // 16) * 2 + me % 2
    which = jnp.full((1,), (my_m // 2) % 2, jnp.int32)
    return jnp.concatenate(
        [rand_slot, here, (owner // 2) % 8, (owner // 16) * 2 + owner % 2, which]
    ).astype(jnp.int32)


def pick_kernel(where, k_ref, v_ref, *outs):
    for b in range(BITS):
        rows = pl.ds(pl.multiple_of(where[b] * BLK, BLK), BLK)
        outs[b][0] = k_ref[rows, :]
        outs[b][1] = v_ref[rows, :]
    first, last, picked = outs[BITS:]
    first[0] = k_ref[0:BLK, :]
    first[1] = v_ref[0:BLK, :]
    last[0] = k_ref[BLK : 2 * BLK, :]
    last[1] = v_ref[BLK : 2 * BLK, :]
    for g in range(GLOB):
        here = where[6 + g]

        @pl.when(here < 0)
        def _():
            picked[0, g] = jnp.zeros((BLK, WIDTH), BF)
            picked[1, g] = jnp.zeros((BLK, WIDTH), BF)

        @pl.when(here >= 0)
        def _():
            rows = pl.ds(pl.multiple_of(jnp.maximum(here, 0) * BLK, BLK), BLK)
            picked[0, g] = k_ref[rows, :]
            picked[1, g] = v_ref[rows, :]


def pick(where, keys, values):
    block = jax.ShapeDtypeStruct((2, BLK, WIDTH), BF)
    outs = [block] * (BITS + 2) + [jax.ShapeDtypeStruct((2, GLOB, BLK, WIDTH), BF)]
    vm = pl.BlockSpec(memory_space=pltpu.VMEM)
    return pl.pallas_call(
        pick_kernel,
        out_shape=outs,
        in_specs=[smem(), vm, vm],
        out_specs=[vm] * len(outs),
        compiler_params=params(),
        name="pick",
    )(where, keys, values)


def relay_kernel(x_ref, o_ref):
    total = jnp.sum(x_ref[...].astype(F32), axis=0).astype(BF)
    for j in range(8):
        o_ref[j] = total


def relay(x):
    return pl.pallas_call(
        relay_kernel,
        out_shape=jax.ShapeDtypeStruct(x.shape, BF),
        compiler_params=params(),
        name="relay",
    )(x)


def gather_heads(dst, c, own, lo, hi, rand, glob):
    dst[0:64, :] = lo[c]
    dst[64:192, :] = own[...]
    dst[192:256, :] = hi[c]
    dst[256:384, :] = glob[c]
    for b in range(BITS):
        dst[384 + 64 * b : 448 + 64 * b, :] = rand[b][c]


def fill_bias(where, bias):
    lane = lax.broadcasted_iota(jnp.int32, (BLK, TOK), 1) // BLK
    for kb in range(12):
        if kb < 4:
            keep = jnp.logical_and(lane <= kb, lane >= kb - 2)
        elif kb < 6:
            keep = lane >= 0
        else:
            keep = lane == where[kb - 6]
        bias[kb * BLK : (kb + 1) * BLK, :] = jnp.where(keep, 0.0, -1e30).astype(F32)


def forward_kernel(where, q, k, v, lo, hi, *rest):
    rand, (glob, perm, attn, stats, ordered, ks, vs, bias, acc) = rest[:BITS], rest[BITS:]
    head = pl.program_id(0)

    @pl.when(head == 0)
    def _():
        fill_bias(where, bias)
        acc[...] = jnp.zeros_like(acc)

    gather_heads(ks, 0, k, lo, hi, rand, glob)
    gather_heads(vs, 1, v, lo, hi, rand, glob)
    scores = mm(ks[...], q[...], ROWS) * SCALE + bias[...]
    top = jnp.max(scores, axis=0, keepdims=True)
    expd = jnp.exp(scores - top)
    inv = 1.0 / jnp.sum(expd, axis=0, keepdims=True)
    probs = (expd * inv).astype(BF)
    out = mm(probs, vs[...], COLS).astype(BF)
    attn[...] = out
    stats[0, 0:1, :] = top
    stats[0, 1:2, :] = inv
    acc[...] += mm(out, perm[...], PLAIN)

    @pl.when(head == HEADS - 1)
    def _():
        for r in range(4):
            ordered[r] = acc[:, r * 256 : (r + 1) * 256].astype(BF)


def head_specs():
    flat = pl.BlockSpec((TOK, HEAD_DIM), lambda h: (0, h))
    pair = pl.BlockSpec((2, BLK, HEAD_DIM), lambda h: (0, 0, h))
    both = pl.BlockSpec((2, TOK, HEAD_DIM), lambda h: (0, 0, h))
    return flat, pair, both


def forward(where, q, k, v, lo, hi, rand, glob, perm):
    flat, pair, both = head_specs()
    return pl.pallas_call(
        forward_kernel,
        grid=(HEADS,),
        in_specs=[smem(), flat, flat, flat, pair, pair]
        + [pair] * BITS
        + [both, pl.BlockSpec((HEAD_DIM, WIDTH), lambda h: (h, 0))],
        out_specs=[
            flat,
            pl.BlockSpec((1, 8, TOK), lambda h: (h, 0, 0)),
            pl.BlockSpec((4, TOK, 256), lambda h: (0, 0, 0)),
        ],
        out_shape=[
            jax.ShapeDtypeStruct((TOK, WIDTH), BF),
            jax.ShapeDtypeStruct((HEADS, 8, TOK), F32),
            jax.ShapeDtypeStruct((4, TOK, 256), BF),
        ],
        scratch_shapes=[
            pltpu.VMEM((KEYS, HEAD_DIM), BF),
            pltpu.VMEM((KEYS, HEAD_DIM), BF),
            pltpu.VMEM((KEYS, TOK), F32),
            pltpu.VMEM((TOK, WIDTH), F32),
        ],
        compiler_params=params(dimension_semantics=("arbitrary",)),
        name="forward",
    )(where, q, k, v, lo, hi, *rand, glob, perm)


def backward_kernel(where, q, k, v, lo, hi, *rest):
    rand, rest = rest[:BITS], rest[BITS:]
    glob, attn, stats, w, d_out = rest[:5]
    dq, down, dlo, dhi = rest[5:9]
    drand, rest = rest[9 : 9 + BITS], rest[9 + BITS :]
    dglob, layer, ks, vs, bias, acc = rest
    head = pl.program_id(0)

    @pl.when(head == 0)
    def _():
        fill_bias(where, bias)
        acc[...] = jnp.zeros_like(acc)

    gather_heads(ks, 0, k, lo, hi, rand, glob)
    gather_heads(vs, 1, v, lo, hi, rand, glob)
    d_attn = mm(d_out[...], w[...], ROWS).astype(BF)
    acc[...] += mm(attn[...], w[...], PLAIN)
    scores = mm(ks[...], q[...], ROWS) * SCALE + bias[...]
    probs = jnp.exp(scores - stats[0, 0:1, :]) * stats[0, 1:2, :]
    probs_b = probs.astype(BF)
    dprob = mm(vs[...], d_attn, ROWS)
    delta = jnp.sum(dprob * probs, axis=0, keepdims=True)
    dscore = (probs * (dprob - delta) * SCALE).astype(BF)
    dq[...] = mm(dscore, ks[...], COLS).astype(BF)
    for c, grad in ((0, mm(dscore, q[...], PLAIN)), (1, mm(probs_b, d_attn, PLAIN))):
        dlo[c] = grad[0:64].astype(BF)
        down[c] = grad[64:192]
        dhi[c] = grad[192:256].astype(BF)
        dglob[c] = grad[256:384].astype(BF)
        for b in range(BITS):
            drand[b][c] = grad[384 + 64 * b : 448 + 64 * b].astype(BF)

    @pl.when(head == HEADS - 1)
    def _():
        layer[...] = acc[...].astype(BF)


def backward(where, q, k, v, lo, hi, rand, glob, attn, stats, w, d_out):
    flat, pair, both = head_specs()
    whole = pl.BlockSpec((TOK, D), lambda h: (0, 0))
    block = jax.ShapeDtypeStruct((2, BLK, WIDTH), BF)
    outs = pl.pallas_call(
        backward_kernel,
        grid=(HEADS,),
        in_specs=[smem(), flat, flat, flat, pair, pair]
        + [pair] * BITS
        + [
            both,
            flat,
            pl.BlockSpec((1, 8, TOK), lambda h: (h, 0, 0)),
            pl.BlockSpec((HEAD_DIM, D), lambda h: (h, 0)),
            whole,
        ],
        out_specs=[flat, both, pair, pair] + [pair] * BITS + [both, whole],
        out_shape=[
            jax.ShapeDtypeStruct((TOK, WIDTH), BF),
            jax.ShapeDtypeStruct((2, TOK, WIDTH), F32),
            block,
            block,
        ]
        + [block] * BITS
        + [
            jax.ShapeDtypeStruct((2, TOK, WIDTH), BF),
            jax.ShapeDtypeStruct((TOK, D), BF),
        ],
        scratch_shapes=[
            pltpu.VMEM((KEYS, HEAD_DIM), BF),
            pltpu.VMEM((KEYS, HEAD_DIM), BF),
            pltpu.VMEM((KEYS, TOK), F32),
            pltpu.VMEM((TOK, D), F32),
        ],
        compiler_params=params(dimension_semantics=("arbitrary",)),
        name="backward",
    )(where, q, k, v, lo, hi, *rand, glob, attn, stats, w, d_out)
    return outs[:4], outs[4 : 4 + BITS], outs[4 + BITS], outs[5 + BITS]


def weight_kernel(cols, grads, dglob, out):
    step = pl.program_id(0)

    @pl.when(step == 0)
    def _():
        out[...] = dglob[...]

    @pl.when(step > 0)
    def _():
        out[...] = mm(cols[...], grads[...], COLS).astype(BF).reshape(8, 32, 1024)


def weight_payload(cols, grads, dglob):
    return pl.pallas_call(
        weight_kernel,
        grid=(3,),
        in_specs=[
            pl.BlockSpec((4 * TOK, 256), lambda i: (0, 0)),
            pl.BlockSpec((4 * TOK, 1024), lambda i: (0, jnp.maximum(i - 1, 0))),
            pl.BlockSpec((8, 32, 1024), lambda i: (0, 0, 0)),
        ],
        out_specs=pl.BlockSpec((8, 32, 1024), lambda i: (0, i, 0)),
        out_shape=jax.ShapeDtypeStruct((8, 96, 1024), BF),
        compiler_params=params(dimension_semantics=("arbitrary",)),
        name="weight",
    )(cols, grads, dglob)


def route_z_kernel(where, x, out, total, small):
    total[...] = jnp.sum(x[...].astype(F32), axis=0)
    which = where[12]
    target = jnp.where(which == 0, where[8], where[9])
    chunk = total[0:32, :]
    small[8:16, :] = jnp.zeros((8, 1024), F32)
    for j in range(8):
        out[j, 0:32] = jnp.where(target == j, chunk, 0.0).astype(BF)
        small[0:4, :] = total[32 + 4 * j : 36 + 4 * j, :]
        small[4:8, :] = total[64 + 4 * j : 68 + 4 * j, :]
        out[j, 32:48] = small[...].astype(BF)


def route_z(where, x):
    vm = pl.BlockSpec(memory_space=pltpu.VMEM)
    return pl.pallas_call(
        route_z_kernel,
        out_shape=jax.ShapeDtypeStruct((8, 48, 1024), BF),
        in_specs=[smem(), vm],
        out_specs=vm,
        scratch_shapes=[pltpu.VMEM((96, 1024), F32), pltpu.VMEM((16, 1024), F32)],
        compiler_params=params(),
        name="route_z",
    )(where, x)


def route_yx_kernel(where, x, out, weight, total):
    total[...] = jnp.sum(x[...].astype(F32), axis=0)
    which = where[12]
    target = jnp.where(which == 0, where[10], where[11])
    chunk = total[0:32, :]
    for j in range(8):
        out[j] = jnp.where(target == j, chunk, 0.0).astype(BF)
    weight[:, 0:1024] = total[32:36, :]
    weight[:, 1024:2048] = total[36:40, :]


def route_yx(where, x):
    vm = pl.BlockSpec(memory_space=pltpu.VMEM)
    return pl.pallas_call(
        route_yx_kernel,
        out_shape=[
            jax.ShapeDtypeStruct((8, 32, 1024), BF),
            jax.ShapeDtypeStruct((4, D), F32),
        ],
        in_specs=[smem(), vm],
        out_specs=[vm, vm],
        scratch_shapes=[pltpu.VMEM((48, 1024), F32)],
        compiler_params=params(),
        name="route_yx",
    )(where, x)


def finish_kernel(where, own, left, right, *rest):
    rand, (glob, dk, dv, acc) = rest[:BITS], rest[BITS:]
    acc[...] = own[...]
    acc[:, 0:BLK, :] += left[...].astype(F32)
    acc[:, BLK : 2 * BLK, :] += right[...].astype(F32)
    for b in range(BITS):
        rows = pl.ds(pl.multiple_of(where[b] * BLK, BLK), BLK)
        acc[:, rows, :] += rand[b][...].astype(F32)
    for g in range(GLOB):
        here = where[6 + g]

        @pl.when(here >= 0)
        def _():
            rows = pl.ds(pl.multiple_of(jnp.maximum(here, 0) * BLK, BLK), BLK)
            acc[:, rows, :] += glob[:, g].astype(F32)

    dk[...] = acc[0].astype(BF)
    dv[...] = acc[1].astype(BF)


def finish(where, own, left, right, rand, glob):
    wide = 256
    pair = pl.BlockSpec((2, BLK, wide), lambda i: (0, 0, i))
    flat = pl.BlockSpec((TOK, wide), lambda i: (0, i))
    return pl.pallas_call(
        finish_kernel,
        grid=(WIDTH // wide,),
        in_specs=[smem(), pl.BlockSpec((2, TOK, wide), lambda i: (0, 0, i)), pair, pair]
        + [pair] * BITS
        + [pl.BlockSpec((2, GLOB, BLK, wide), lambda i: (0, 0, 0, i))],
        out_specs=[flat, flat],
        out_shape=[jax.ShapeDtypeStruct((TOK, WIDTH), BF)] * 2,
        scratch_shapes=[pltpu.VMEM((2, TOK, wide), F32)],
        compiler_params=params(dimension_semantics=("arbitrary",)),
        name="finish",
    )(where, own, left, right, *rand, glob)


def feature_order():
    new = jnp.arange(WIDTH, dtype=jnp.int32)
    r, y, x, z, j = new // 256, (new // 64) % 4, (new // 32) % 2, (new // 4) % 8, new % 4
    old = y * 256 + z * 32 + x * 16 + r * 4 + j
    return (jnp.arange(WIDTH, dtype=jnp.int32)[:, None] == old[None, :]).astype(BF)


def per_device(queries, keys, values, w_out, d_out, rand_slot, global_ids):
    q, k, v, grad_out = queries[0], keys[0], values[0], d_out[0]
    where = where_of(rand_slot[0, 0], global_ids[0])
    all_grads = lax.all_gather(grad_out, "rep", axis=0, tiled=True)
    all_w = lax.all_gather(w_out, "rep", axis=0, tiled=True)
    *chosen, first, last, picked = pick(where, k, v)
    spread = trade(picked.reshape(8, 32, WIDTH), Z_GROUPS)
    lo = shifted(last, 1)
    hi = shifted(first, -1)
    rand = [swapped(chosen[b], b) for b in range(BITS)]
    spread = trade(relay(spread), YX_GROUPS)
    glob = trade(relay(spread), Z_GROUPS).reshape(2, GLOB * BLK, WIDTH)
    attn, stats, ordered = forward(where, q, k, v, lo, hi, rand, glob, feature_order())
    cols = lax.all_to_all(ordered, "rep", 0, 0, tiled=True).reshape(4 * TOK, 256)
    (dq, down, dlo, dhi), drand, dglob, layer = backward(
        where, q, k, v, lo, hi, rand, glob, attn, stats, all_w, grad_out
    )
    payload = weight_payload(cols, all_grads, dglob.reshape(8, 32, WIDTH))
    payload = route_z(where, trade(payload, YX_GROUPS))
    payload, weight_grad = route_yx(where, trade(payload, Z_GROUPS))
    glob_total = trade(payload, YX_GROUPS).reshape(2, GLOB, BLK, WIDTH)
    right = shifted(dlo, -1)
    left = shifted(dhi, 1)
    back = [swapped(drand[b], b) for b in range(BITS)]
    dk, dv = finish(where, down, left, right, back, glob_total)
    return (layer[None], dq[None], dk[None], dv[None], weight_grad)


def solution(mesh):
    return jax.shard_map(
        per_device,
        mesh=mesh,
        in_specs=(
            P("rep", "seq", None),
            P("rep", "seq", None),
            P("rep", "seq", None),
            P("rep", None),
            P("rep", "seq", None),
            P("rep", "seq", None),
            P("rep", None),
        ),
        out_specs=(
            P("rep", "seq", None),
            P("rep", "seq", None),
            P("rep", "seq", None),
            P("rep", "seq", None),
            P(("seq", "rep"), None),
        ),
        check_vma=False,
    )
```

```python
import jax
import jax.numpy as jnp
from jax import lax
from jax.experimental import pallas as pl
from jax.experimental.pallas import tpu as pltpu
from jax.sharding import PartitionSpec as P

HEADS = 8
HEAD_DIM = 128
BLK = 64
GLOB = 2
BITS = 6
TOK = 128
WIDTH = HEADS * HEAD_DIM
D = 2048
KEYS = 768
SCALE = HEAD_DIM ** (-0.5)
BF = jnp.bfloat16
F32 = jnp.float32
STEP = 4
WIDE = STEP * HEAD_DIM
ROWS = (((1,), (1,)), ((), ()))
COLS = (((0,), (0,)), ((), ()))
PLAIN = (((1,), (0,)), ((), ()))
VMEM_LIMIT = 20 * 1024 * 1024


def stretch_id(y, z, x):
    return y * 16 + z * 2 + x


Z_GROUPS = [[stretch_id(y, z, x) for z in range(8)] for y in range(4) for x in range(2)]
Y_GROUPS = [[stretch_id(y, z, x) for y in range(4)] for z in range(8) for x in range(2)]
YX_GROUPS = [[stretch_id(y, z, x) for y in range(4) for x in range(2)] for z in range(8)]


def mm(left, right, dims):
    return lax.dot_general(left, right, dims, preferred_element_type=F32)


def trade(value, groups):
    return lax.all_to_all(value, "seq", 0, 0, axis_index_groups=groups, tiled=True)


def shifted(value, steps):
    return lax.ppermute(value, "seq", [(s, (s + steps) % 64) for s in range(64)])


def swapped(value, bit):
    return lax.ppermute(value, "seq", [(s, s ^ (1 << bit)) for s in range(64)])


def across(value, flip):
    return lax.ppermute(value, "rep", [(r, r ^ flip) for r in range(4)])


def beside(value):
    pairs = [(s * 4 + r, (s ^ 1) * 4 + (r ^ 2)) for s in range(64) for r in range(4)]
    return lax.ppermute(value, ("seq", "rep"), pairs)


def far(shape, dtype=BF):
    return pltpu.HBM(shape, dtype)


def from_hbm(*values):
    return [pltpu.with_memory_space_constraint(x, pltpu.HBM) for x in values]


def smem():
    return pl.BlockSpec(memory_space=pltpu.SMEM)


def params(**kw):
    return pltpu.CompilerParams(vmem_limit_bytes=VMEM_LIMIT, **kw)


def where_of(rand_slot, global_ids):
    me = lax.axis_index("seq")
    owner = global_ids // 2
    here = jnp.where(owner == me, global_ids % 2, -1)
    my_m = (me // 16) * 2 + me % 2
    tail = jnp.stack([(my_m // 2) % 2, lax.axis_index("rep"), me % 2])
    return jnp.concatenate(
        [rand_slot, here, (owner // 2) % 8, (owner // 16) * 2 + owner % 2, tail]
    ).astype(jnp.int32)


def pick_kernel(where, k_ref, v_ref, *outs):
    for b in range(BITS):
        rows = pl.ds(pl.multiple_of(where[b] * BLK, BLK), BLK)
        outs[b][0] = k_ref[rows, :]
        outs[b][1] = v_ref[rows, :]
    first, last, picked = outs[BITS:]
    first[0] = k_ref[0:BLK, :]
    first[1] = v_ref[0:BLK, :]
    last[0] = k_ref[BLK : 2 * BLK, :]
    last[1] = v_ref[BLK : 2 * BLK, :]
    for g in range(GLOB):
        here = where[6 + g]

        @pl.when(here < 0)
        def _():
            picked[0, g] = jnp.zeros((BLK, WIDTH), BF)
            picked[1, g] = jnp.zeros((BLK, WIDTH), BF)

        @pl.when(here >= 0)
        def _():
            rows = pl.ds(pl.multiple_of(jnp.maximum(here, 0) * BLK, BLK), BLK)
            picked[0, g] = k_ref[rows, :]
            picked[1, g] = v_ref[rows, :]


def pick(where, keys, values):
    block = far((2, BLK, WIDTH))
    outs = [block] * (BITS + 2) + [far((2, GLOB, BLK, WIDTH))]
    vm = pl.BlockSpec(memory_space=pltpu.VMEM)
    return pl.pallas_call(
        pick_kernel,
        out_shape=outs,
        in_specs=[smem(), vm, vm],
        out_specs=[vm] * len(outs),
        compiler_params=params(),
        name="pick",
    )(where, keys, values)


def relay_kernel(x_ref, o_ref):
    total = jnp.sum(x_ref[...].astype(F32), axis=0).astype(BF)
    for j in range(8):
        o_ref[j] = total


def relay(x):
    return pl.pallas_call(
        relay_kernel,
        out_shape=far(x.shape),
        compiler_params=params(),
        name="relay",
    )(x)


def gather_heads(dst, c, cols, own, lo, hi, rand, glob):
    dst[0:64, :] = lo[c, :, cols]
    dst[64:192, :] = own[:, cols]
    dst[192:256, :] = hi[c, :, cols]
    dst[256:384, :] = glob[c, :, cols]
    for b in range(BITS):
        dst[384 + 64 * b : 448 + 64 * b, :] = rand[b][c, :, cols]


def fill_bias(where, bias):
    lane = lax.broadcasted_iota(jnp.int32, (BLK, TOK), 1) // BLK
    for kb in range(12):
        if kb < 4:
            keep = jnp.logical_and(lane <= kb, lane >= kb - 2)
        elif kb < 6:
            keep = lane >= 0
        else:
            keep = lane == where[kb - 6]
        bias[kb * BLK : (kb + 1) * BLK, :] = jnp.where(keep, 0.0, -1e30).astype(F32)


def forward_kernel(where, q, k, v, lo, hi, *rest):
    rand, rest = rest[:BITS], rest[BITS:]
    glob, perm, attn, stats, *ordered, ks, vs, bias, acc = rest
    step = pl.program_id(0)

    @pl.when(step == 0)
    def _():
        fill_bias(where, bias)

    for i in range(STEP):
        cols = slice(i * HEAD_DIM, (i + 1) * HEAD_DIM)
        gather_heads(ks.at[i], 0, cols, k, lo, hi, rand, glob)
        gather_heads(vs.at[i], 1, cols, v, lo, hi, rand, glob)
        scores = mm(ks[i], q[:, cols], ROWS) * SCALE + bias[...]
        top = jnp.max(scores, axis=0, keepdims=True)
        expd = jnp.exp(scores - top)
        inv = 1.0 / jnp.sum(expd, axis=0, keepdims=True)
        probs = (expd * inv).astype(BF)
        attn[:, cols] = mm(probs, vs[i], COLS).astype(BF)
        stats[i, 0:1, :] = top
        stats[i, 1:2, :] = inv

    part = mm(attn[...], perm[...], PLAIN)

    @pl.when(step == 0)
    def _():
        acc[...] = part

    @pl.when(step == HEADS // STEP - 1)
    def _():
        total = acc[...] + part
        for r in range(4):
            ordered[r][...] = total[:, r * 256 : (r + 1) * 256].astype(BF)


def head_specs():
    flat = pl.BlockSpec((TOK, WIDE), lambda h: (0, h))
    pair = pl.BlockSpec((2, BLK, WIDE), lambda h: (0, 0, h))
    both = pl.BlockSpec((2, TOK, WIDE), lambda h: (0, 0, h))
    return flat, pair, both


def forward(where, q, k, v, lo, hi, rand, glob, perm):
    flat, pair, both = head_specs()
    return pl.pallas_call(
        forward_kernel,
        grid=(HEADS // STEP,),
        in_specs=[smem(), flat, flat, flat, pair, pair]
        + [pair] * BITS
        + [both, pl.BlockSpec((WIDE, WIDTH), lambda h: (h, 0))],
        out_specs=[
            flat,
            pl.BlockSpec((STEP, 8, TOK), lambda h: (h, 0, 0)),
        ]
        + [pl.BlockSpec((TOK, 256), lambda h: (0, 0))] * 4,
        out_shape=[
            far((TOK, WIDTH)),
            far((HEADS, 8, TOK), F32),
        ]
        + [jax.ShapeDtypeStruct((TOK, 256), BF)] * 4,
        scratch_shapes=[
            pltpu.VMEM((STEP, KEYS, HEAD_DIM), BF),
            pltpu.VMEM((STEP, KEYS, HEAD_DIM), BF),
            pltpu.VMEM((KEYS, TOK), F32),
            pltpu.VMEM((TOK, WIDTH), F32),
        ],
        compiler_params=params(dimension_semantics=("arbitrary",)),
        name="forward",
    )(where, q, k, v, lo, hi, *rand, glob, perm)


def backward_kernel(where, q, k, v, lo, hi, *rest):
    rand, rest = rest[:BITS], rest[BITS:]
    glob, stats, d_attn_ref, dq, down, dlo, dhi = rest[:7]
    drand, rest = rest[7 : 7 + BITS], rest[7 + BITS :]
    dglob, ks, vs, bias = rest

    @pl.when(pl.program_id(0) == 0)
    def _():
        fill_bias(where, bias)

    for i in range(STEP):
        cols = slice(i * HEAD_DIM, (i + 1) * HEAD_DIM)
        gather_heads(ks.at[i], 0, cols, k, lo, hi, rand, glob)
        gather_heads(vs.at[i], 1, cols, v, lo, hi, rand, glob)
        d_attn = d_attn_ref[:, cols]
        scores = mm(ks[i], q[:, cols], ROWS) * SCALE + bias[...]
        probs = jnp.exp(scores - stats[i, 0:1, :]) * stats[i, 1:2, :]
        probs_b = probs.astype(BF)
        dprob = mm(vs[i], d_attn, ROWS)
        delta = jnp.sum(dprob * probs, axis=0, keepdims=True)
        dscore = (probs * (dprob - delta) * SCALE).astype(BF)
        dq[:, cols] = mm(dscore, ks[i], COLS).astype(BF)
        for c, grad in ((0, mm(dscore, q[:, cols], PLAIN)), (1, mm(probs_b, d_attn, PLAIN))):
            dlo[c, :, cols] = grad[0:64].astype(BF)
            down[c, :, cols] = grad[64:192]
            dhi[c, :, cols] = grad[192:256].astype(BF)
            dglob[c, :, cols] = grad[256:384].astype(BF)
            for b in range(BITS):
                drand[b][c, :, cols] = grad[384 + 64 * b : 448 + 64 * b].astype(BF)


def backward(where, q, k, v, lo, hi, rand, glob, stats, d_attn):
    flat, pair, both = head_specs()
    block = far((2, BLK, WIDTH))
    outs = pl.pallas_call(
        backward_kernel,
        grid=(HEADS // STEP,),
        in_specs=[smem(), flat, flat, flat, pair, pair]
        + [pair] * BITS
        + [both, pl.BlockSpec((STEP, 8, TOK), lambda h: (h, 0, 0)), flat],
        out_specs=[flat, both, pair, pair] + [pair] * BITS + [both],
        out_shape=[far((TOK, WIDTH)), far((2, TOK, WIDTH), F32), block, block]
        + [block] * BITS
        + [far((2, TOK, WIDTH))],
        scratch_shapes=[
            pltpu.VMEM((STEP, KEYS, HEAD_DIM), BF),
            pltpu.VMEM((STEP, KEYS, HEAD_DIM), BF),
            pltpu.VMEM((KEYS, TOK), F32),
        ],
        compiler_params=params(dimension_semantics=("arbitrary",)),
        name="backward",
    )(where, *from_hbm(q, k, v, lo, hi, *rand, glob, stats, d_attn))
    return outs[:4], outs[4 : 4 + BITS], outs[4 + BITS]


def head_of(i, where):
    return ((i // 2) ^ where[13]) * 2 + i % 2


def head_call(kernel, where, parts, extra, extra_spec, out_shape, out_spec, scratch, name):
    w_spec = pl.BlockSpec((HEAD_DIM, D), lambda i, at: (0, 0))
    return pl.pallas_call(
        kernel,
        grid_spec=pltpu.PrefetchScalarGridSpec(
            num_scalar_prefetch=1,
            grid=(HEADS,),
            in_specs=[w_spec] * HEADS + [extra_spec],
            out_specs=out_spec,
            scratch_shapes=scratch,
        ),
        out_shape=out_shape,
        compiler_params=params(dimension_semantics=("arbitrary",)),
        name=name,
    )(where, *parts, extra)


def project_kernel(where, *refs):
    w, (d_out, out) = refs[:HEADS], refs[HEADS:]
    for i in range(HEADS):

        @pl.when(pl.program_id(0) == i)
        def _():
            out[...] = mm(d_out[...], w[i][...], ROWS).astype(BF)


def project(where, parts, d_out):
    return head_call(
        project_kernel,
        where,
        parts,
        d_out,
        pl.BlockSpec((TOK, D), lambda i, at: (0, 0)),
        far((TOK, WIDTH)),
        pl.BlockSpec((TOK, HEAD_DIM), lambda i, at: (0, head_of(i, at))),
        [],
        "project",
    )


def layer_kernel(where, *refs):
    w, (attn, out, acc) = refs[:HEADS], refs[HEADS:]
    for i in range(HEADS):

        @pl.when(pl.program_id(0) == i)
        def _():
            part = mm(attn[...], w[i][...], PLAIN)
            if i == 0:
                acc[...] = part
            elif i < HEADS - 1:
                acc[...] += part
            else:
                out[...] = (acc[...] + part).astype(BF)


def layer_of(where, parts, attn):
    return head_call(
        layer_kernel,
        where,
        parts,
        attn,
        pl.BlockSpec((TOK, HEAD_DIM), lambda i, at: (0, head_of(i, at))),
        far((TOK, D)),
        pl.BlockSpec((TOK, D), lambda i, at: (0, 0)),
        [pltpu.VMEM((TOK, D), F32)],
        "layer",
    )


def weight_kernel(*refs):
    cols, grads, out = refs[:4], refs[4:8], refs[8]
    total = mm(cols[0][...], grads[0][...], COLS)
    for a in range(1, 4):
        total += mm(cols[a][...], grads[a][...], COLS)
    out[...] = total.astype(BF)


def weight_payload(cols, grads):
    return pl.pallas_call(
        weight_kernel,
        grid=(2,),
        in_specs=[pl.BlockSpec((TOK, 256), lambda i: (0, 0))] * 4
        + [pl.BlockSpec((TOK, 1024), lambda i: (0, i))]
        + [pl.BlockSpec((TOK, 1024), lambda i: (1, i))] * 3,
        out_specs=pl.BlockSpec((256, 1024), lambda i: (0, i)),
        out_shape=far((256, D)),
        compiler_params=params(dimension_semantics=("arbitrary",)),
        name="weight",
    )(*cols, *grads)


def route_z_kernel(where, x, w, out, rows, small):
    chunk = jnp.sum(x[...].astype(F32), axis=0)
    rows[...] = w[...].astype(F32)
    target = jnp.where(where[12] == 0, where[8], where[9])
    for j in range(8):
        out[j, 0:32] = jnp.where(target == j, chunk, 0.0).astype(BF)
        small[0:8, :] = rows[8 * j : 8 * j + 8, 0:1024]
        small[8:16, :] = rows[8 * j : 8 * j + 8, 1024:2048]
        out[j, 32:48] = small[...].astype(BF)


def route_z(where, x, w):
    vm = pl.BlockSpec(memory_space=pltpu.VMEM)
    return pl.pallas_call(
        route_z_kernel,
        out_shape=far((8, 48, 1024)),
        in_specs=[smem(), vm, vm],
        out_specs=vm,
        scratch_shapes=[pltpu.VMEM((64, D), F32), pltpu.VMEM((16, 1024), F32)],
        compiler_params=params(),
        name="route_z",
    )(where, x, w)


def route_yx_kernel(where, x, out, mine, other, total):
    total[...] = jnp.sum(x[...].astype(F32), axis=0)
    target = jnp.where(where[12] == 0, where[10], where[11])
    chunk = total[0:32, :]
    for j in range(8):
        out[j] = jnp.where(target == j, chunk, 0.0).astype(BF)
    left = where[14] == 0
    for half in range(2):
        cols = slice(half * 1024, (half + 1) * 1024)
        one = total[32 + 8 * half : 36 + 8 * half, :]
        two = total[36 + 8 * half : 40 + 8 * half, :]
        mine[:, cols] = jnp.where(left, one, two)
        other[:, cols] = jnp.where(left, two, one)


def route_yx(where, x):
    vm = pl.BlockSpec(memory_space=pltpu.VMEM)
    return pl.pallas_call(
        route_yx_kernel,
        out_shape=[far((8, 32, 1024)), far((4, D), F32), far((4, D), F32)],
        in_specs=[smem(), vm],
        out_specs=[vm] * 3,
        scratch_shapes=[pltpu.VMEM((48, 1024), F32)],
        compiler_params=params(),
        name="route_yx",
    )(where, x)


def finish_kernel(where, own, left, right, *rest):
    rand, (glob, mine, other, dk, dv, weight, acc) = rest[:BITS], rest[BITS:]
    weight[...] = mine[...] + other[...]
    acc[...] = own[...]
    acc[:, 0:BLK, :] += left[...].astype(F32)
    acc[:, BLK : 2 * BLK, :] += right[...].astype(F32)
    for b in range(BITS):
        rows = pl.ds(pl.multiple_of(where[b] * BLK, BLK), BLK)
        acc[:, rows, :] += rand[b][...].astype(F32)
    for g in range(GLOB):
        here = where[6 + g]

        @pl.when(here >= 0)
        def _():
            rows = pl.ds(pl.multiple_of(jnp.maximum(here, 0) * BLK, BLK), BLK)
            acc[:, rows, :] += glob[:, g].astype(F32)

    dk[...] = acc[0].astype(BF)
    dv[...] = acc[1].astype(BF)


def finish(where, own, left, right, rand, glob, mine, other):
    wide = 256
    pair = pl.BlockSpec((2, BLK, wide), lambda i: (0, 0, i))
    flat = pl.BlockSpec((TOK, wide), lambda i: (0, i))
    rows = pl.BlockSpec((4, 2 * wide), lambda i: (0, i))
    return pl.pallas_call(
        finish_kernel,
        grid=(WIDTH // wide,),
        in_specs=[smem(), pl.BlockSpec((2, TOK, wide), lambda i: (0, 0, i)), pair, pair]
        + [pair] * BITS
        + [pl.BlockSpec((2, GLOB, BLK, wide), lambda i: (0, 0, 0, i)), rows, rows],
        out_specs=[flat, flat, rows],
        out_shape=[far((TOK, WIDTH)), far((TOK, WIDTH)), far((4, D), F32)],
        scratch_shapes=[pltpu.VMEM((2, TOK, wide), F32)],
        compiler_params=params(dimension_semantics=("arbitrary",)),
        name="finish",
    )(where, *from_hbm(own), left, right, *rand, glob, mine, other)


def feature_order(rep):
    new = jnp.arange(WIDTH, dtype=jnp.int32)
    r, y, x, z, j = (new // 256) ^ rep, (new // 64) % 4, (new // 4) % 2, (new // 8) % 8, new % 4
    old = y * 256 + z * 32 + x * 16 + r * 4 + j
    return (jnp.arange(WIDTH, dtype=jnp.int32)[:, None] == old[None, :]).astype(BF)


def together(*values):
    return lax.optimization_barrier(values)


def per_device(queries, keys, values, w_out, d_out, rand_slot, global_ids):
    q, k, v, grad_out = queries[0], keys[0], values[0], d_out[0]
    where = where_of(rand_slot[0, 0], global_ids[0])
    *chosen, first, last, picked = pick(where, k, v)
    spread = trade(picked.reshape(8, 32, WIDTH), Z_GROUPS)
    mixed = jnp.concatenate([w_out[:HEAD_DIM], grad_out])
    upper = w_out[HEAD_DIM:]
    mixed2 = across(mixed, 2)
    upper2 = beside(upper)
    mixed1 = across(mixed, 1)
    upper1 = across(upper, 1)
    rand = [swapped(chosen[b], b) for b in range(BITS)]
    lo = shifted(last, 1)
    hi = shifted(first, -1)
    spread, rand[4], rand[1], mixed1, upper1 = together(spread, rand[4], rand[1], mixed1, upper1)
    spread = trade(relay(spread), YX_GROUPS)
    spread, rand[3], rand[5], mixed2, upper2 = together(spread, rand[3], rand[5], mixed2, upper2)
    mixed3 = across(mixed2, 1)
    upper3 = across(upper2, 1)
    glob = trade(relay(spread), Z_GROUPS).reshape(2, GLOB * BLK, WIDTH)
    parts = (w_out, upper, mixed1, upper1, mixed2, upper2, mixed3, upper3)
    d_attn = project(where, parts, grad_out)
    order = feature_order(lax.axis_index("rep"))
    glob, d_attn, order = together(glob, d_attn, order)
    early = from_hbm(rand[1], rand[3], rand[4], rand[5])
    mixed_rand = [rand[0], early[0], rand[2], early[1], early[2], early[3]]
    attn, stats, *ordered = forward(
        where, *from_hbm(q, k, v), lo, hi, mixed_rand, glob, *from_hbm(order)
    )
    cols = [ordered[0]] + [across(ordered[a], a) for a in range(1, 4)]
    layer = layer_of(where, parts, attn)
    layer, *cols = together(layer, *cols)
    weight = weight_payload(cols, (grad_out, mixed1, mixed2, mixed3))
    weight, d_attn = together(weight, d_attn)
    weight = lax.psum_scatter(
        weight, "seq", scatter_dimension=0, axis_index_groups=Y_GROUPS, tiled=True
    )
    (dq, down, dlo, dhi), drand, dglob = backward(
        where, q, k, v, lo, hi, rand, glob, stats, d_attn
    )
    payload = trade(dglob.reshape(8, 32, WIDTH), YX_GROUPS)
    back = [swapped(drand[b], b) for b in range(BITS)]
    right = shifted(dlo, -1)
    left = shifted(dhi, 1)
    payload, weight, back[3] = together(payload, weight, back[3])
    payload = trade(route_z(where, payload, weight), Z_GROUPS)
    payload, back[0], back[4], back[5], left = together(
        payload, back[0], back[4], back[5], left
    )
    payload, mine, other = route_yx(where, payload)
    glob_total = trade(payload, YX_GROUPS).reshape(2, GLOB, BLK, WIDTH)
    other = swapped(other, 0)
    dk, dv, weight_grad = finish(where, down, left, right, back, glob_total, mine, other)
    return (layer[None], dq[None], dk[None], dv[None], weight_grad)


def solution(mesh):
    return jax.shard_map(
        per_device,
        mesh=mesh,
        in_specs=(
            P("rep", "seq", None),
            P("rep", "seq", None),
            P("rep", "seq", None),
            P("rep", None),
            P("rep", "seq", None),
            P("rep", "seq", None),
            P("rep", None),
        ),
        out_specs=(
            P("rep", "seq", None),
            P("rep", "seq", None),
            P("rep", "seq", None),
            P("rep", "seq", None),
            P(("seq", "rep"), None),
        ),
        check_vma=False,
    )
```

```python
import jax
import jax.numpy as jnp
from jax import lax
from jax.experimental import pallas as pl
from jax.experimental.pallas import tpu as pltpu
from jax.sharding import PartitionSpec as P

HEADS = 8
HEAD_DIM = 128
BLK = 64
GLOB = 2
BITS = 6
TOK = 128
WIDTH = HEADS * HEAD_DIM
D = 2048
KEYS = 768
SCALE = HEAD_DIM ** (-0.5)
BF = jnp.bfloat16
F32 = jnp.float32
STEP = 4
WIDE = STEP * HEAD_DIM
ROWS = (((1,), (1,)), ((), ()))
COLS = (((0,), (0,)), ((), ()))
PLAIN = (((1,), (0,)), ((), ()))
VMEM_LIMIT = 20 * 1024 * 1024


def stretch_id(y, z, x):
    return y * 16 + z * 2 + x


YX_GROUPS = [[stretch_id(y, z, x) for y in range(4) for x in range(2)] for z in range(8)]
CHUNKS = 8
HALF = WIDTH // 2
Z_BITS = (1, 2, 3)
FIRST, SECOND, THIRD = (3, 4, 0), (5, 1), (2,)


def mm(left, right, dims):
    return lax.dot_general(left, right, dims, preferred_element_type=F32)


def trade(value):
    return lax.all_to_all(value, "seq", 0, 0, axis_index_groups=YX_GROUPS, tiled=True)


def shifted(value, steps):
    return lax.ppermute(value, "seq", [(s, (s + steps) % 64) for s in range(64)])


def swapped(value, bit):
    return lax.ppermute(value, "seq", [(s, s ^ (1 << bit)) for s in range(64)])


def across(value, flip):
    return lax.ppermute(value, "rep", [(r, r ^ flip) for r in range(4)])


def beside(value):
    pairs = [(s * 4 + r, (s ^ 1) * 4 + (r ^ 2)) for s in range(64) for r in range(4)]
    return lax.ppermute(value, ("seq", "rep"), pairs)


def far(shape, dtype=BF):
    return pltpu.HBM(shape, dtype)


def from_hbm(*values):
    return [pltpu.with_memory_space_constraint(x, pltpu.HBM) for x in values]


def smem():
    return pl.BlockSpec(memory_space=pltpu.SMEM)


def params(**kw):
    return pltpu.CompilerParams(vmem_limit_bytes=VMEM_LIMIT, **kw)


def where_of(rand_slot, global_ids):
    me = lax.axis_index("seq")
    rep = lax.axis_index("rep")
    owner = global_ids // 2
    here = jnp.where(owner == me, global_ids % 2, -1)
    tail = jnp.stack([me % 2, me, rep, rep])
    return jnp.concatenate([rand_slot, here, (owner // 16) * 2 + owner % 2, tail]).astype(
        jnp.int32
    )


def pick_kernel(where, k_ref, v_ref, *outs):
    for b in range(BITS):
        rows = pl.ds(pl.multiple_of(where[b] * BLK, BLK), BLK)
        outs[b][0] = k_ref[rows, :]
        outs[b][1] = v_ref[rows, :]
    first, last, picked = outs[BITS:]
    first[0] = k_ref[0:BLK, :]
    first[1] = v_ref[0:BLK, :]
    last[0] = k_ref[BLK : 2 * BLK, :]
    last[1] = v_ref[BLK : 2 * BLK, :]
    for g in range(GLOB):
        here = where[6 + g]
        rows = pl.ds(pl.multiple_of(jnp.maximum(here, 0) * BLK, BLK), BLK)
        for c, src in enumerate((k_ref, v_ref)):
            block = jnp.where(here >= 0, src[rows, :], jnp.zeros((BLK, WIDTH), BF))
            for half in range(2):
                picked[half * 4 + c * 2 + g] = block[:, half * HALF : (half + 1) * HALF]


def pick(where, keys, values):
    block = far((2, BLK, WIDTH))
    outs = [block] * (BITS + 2) + [far((CHUNKS, BLK, HALF))]
    vm = pl.BlockSpec(memory_space=pltpu.VMEM)
    return pl.pallas_call(
        pick_kernel,
        out_shape=outs,
        in_specs=[smem(), vm, vm],
        out_specs=[vm] * len(outs),
        compiler_params=params(),
        name="pick",
    )(where, keys, values)


def gathered_kernel(x_ref, o_ref):
    o_ref[...] = jnp.sum(x_ref[...].astype(F32), axis=0).astype(BF)


def gathered(x):
    return pl.pallas_call(
        gathered_kernel,
        out_shape=far((BLK, HALF)),
        compiler_params=params(),
        name="gathered",
    )(x)


def relay_kernel(mine, other, out):
    total = (mine[...].astype(F32) + other[...].astype(F32)).astype(BF)
    if len(out.shape) == 2:
        out[...] = total
    else:
        for j in range(CHUNKS):
            out[j] = total


def relay(mine, other, shape):
    return pl.pallas_call(
        relay_kernel,
        out_shape=far(shape),
        compiler_params=params(),
        name="relay",
    )(mine, other)


def gather_heads(dst, c, cols, own, lo, hi, rand, glob):
    dst[0:64, :] = lo[c, :, cols]
    dst[64:192, :] = own[:, cols]
    dst[192:256, :] = hi[c, :, cols]
    dst[256:384, :] = glob[0, c * TOK : (c + 1) * TOK, cols]
    for b in range(BITS):
        dst[384 + 64 * b : 448 + 64 * b, :] = rand[b][c, :, cols]


def fill_bias(where, bias):
    lane = lax.broadcasted_iota(jnp.int32, (BLK, TOK), 1) // BLK
    for kb in range(12):
        if kb < 4:
            keep = jnp.logical_and(lane <= kb, lane >= kb - 2)
        elif kb < 6:
            keep = lane >= 0
        else:
            keep = lane == where[kb - 6]
        bias[kb * BLK : (kb + 1) * BLK, :] = jnp.where(keep, 0.0, -1e30).astype(F32)


def forward_kernel(where, q, k, v, lo, hi, *rest):
    rand, rest = rest[:BITS], rest[BITS:]
    glob, perm, attn, stats, *ordered, ks, vs, bias, acc = rest
    step = pl.program_id(0)

    @pl.when(step == 0)
    def _():
        fill_bias(where, bias)

    for i in range(STEP):
        cols = slice(i * HEAD_DIM, (i + 1) * HEAD_DIM)
        gather_heads(ks.at[i], 0, cols, k, lo, hi, rand, glob)
        gather_heads(vs.at[i], 1, cols, v, lo, hi, rand, glob)
        scores = mm(ks[i], q[:, cols], ROWS) * SCALE + bias[...]
        top = jnp.max(scores, axis=0, keepdims=True)
        expd = jnp.exp(scores - top)
        inv = 1.0 / jnp.sum(expd, axis=0, keepdims=True)
        probs = (expd * inv).astype(BF)
        attn[:, cols] = mm(probs, vs[i], COLS).astype(BF)
        stats[i, 0:1, :] = top
        stats[i, 1:2, :] = inv

    part = mm(attn[...], perm[...], PLAIN)

    @pl.when(step == 0)
    def _():
        acc[...] = part

    @pl.when(step == HEADS // STEP - 1)
    def _():
        total = acc[...] + part
        for r in range(4):
            ordered[r][...] = total[:, r * 256 : (r + 1) * 256].astype(BF)


def head_specs():
    flat = pl.BlockSpec((TOK, WIDE), lambda h: (0, h))
    pair = pl.BlockSpec((2, BLK, WIDE), lambda h: (0, 0, h))
    both = pl.BlockSpec((2, TOK, WIDE), lambda h: (0, 0, h))
    half = pl.BlockSpec((1, 2 * TOK, WIDE), lambda h: (h, 0, 0))
    return flat, pair, both, half


def forward(where, q, k, v, lo, hi, rand, glob, perm):
    flat, pair, both, half = head_specs()
    return pl.pallas_call(
        forward_kernel,
        grid=(HEADS // STEP,),
        in_specs=[smem(), flat, flat, flat, pair, pair]
        + [pair] * BITS
        + [half, pl.BlockSpec((WIDE, WIDTH), lambda h: (h, 0))],
        out_specs=[
            flat,
            pl.BlockSpec((STEP, 8, TOK), lambda h: (h, 0, 0)),
        ]
        + [pl.BlockSpec((TOK, 256), lambda h: (0, 0))] * 4,
        out_shape=[
            far((TOK, WIDTH)),
            far((HEADS, 8, TOK), F32),
        ]
        + [jax.ShapeDtypeStruct((TOK, 256), BF)] * 4,
        scratch_shapes=[
            pltpu.VMEM((STEP, KEYS, HEAD_DIM), BF),
            pltpu.VMEM((STEP, KEYS, HEAD_DIM), BF),
            pltpu.VMEM((KEYS, TOK), F32),
            pltpu.VMEM((TOK, WIDTH), F32),
        ],
        compiler_params=params(dimension_semantics=("arbitrary",)),
        name="forward",
    )(where, q, k, v, lo, hi, *rand, glob, perm)


def backward_kernel(where, q, k, v, lo, hi, *rest):
    rand, rest = rest[:BITS], rest[BITS:]
    glob, stats, d_attn_ref, dq, down, dlo, dhi = rest[:7]
    drand, rest = rest[7 : 7 + BITS], rest[7 + BITS :]
    dglob, ks, vs, bias = rest

    @pl.when(pl.program_id(0) == 0)
    def _():
        fill_bias(where, bias)

    for i in range(STEP):
        cols = slice(i * HEAD_DIM, (i + 1) * HEAD_DIM)
        gather_heads(ks.at[i], 0, cols, k, lo, hi, rand, glob)
        gather_heads(vs.at[i], 1, cols, v, lo, hi, rand, glob)
        d_attn = d_attn_ref[:, cols]
        scores = mm(ks[i], q[:, cols], ROWS) * SCALE + bias[...]
        probs = jnp.exp(scores - stats[i, 0:1, :]) * stats[i, 1:2, :]
        probs_b = probs.astype(BF)
        dprob = mm(vs[i], d_attn, ROWS)
        delta = jnp.sum(dprob * probs, axis=0, keepdims=True)
        dscore = (probs * (dprob - delta) * SCALE).astype(BF)
        dq[:, cols] = mm(dscore, ks[i], COLS).astype(BF)
        for c, grad in ((0, mm(dscore, q[:, cols], PLAIN)), (1, mm(probs_b, d_attn, PLAIN))):
            dlo[c, :, cols] = grad[0:64].astype(BF)
            down[c, :, cols] = grad[64:192]
            dhi[c, :, cols] = grad[192:256].astype(BF)
            dglob[0, c * TOK : (c + 1) * TOK, cols] = grad[256:384].astype(BF)
            for b in range(BITS):
                drand[b][c, :, cols] = grad[384 + 64 * b : 448 + 64 * b].astype(BF)


def backward(where, q, k, v, lo, hi, rand, glob, stats, d_attn):
    flat, pair, both, half = head_specs()
    block = far((2, BLK, WIDTH))
    outs = pl.pallas_call(
        backward_kernel,
        grid=(HEADS // STEP,),
        in_specs=[smem(), flat, flat, flat, pair, pair]
        + [pair] * BITS
        + [half, pl.BlockSpec((STEP, 8, TOK), lambda h: (h, 0, 0)), flat],
        out_specs=[flat, both, pair, pair] + [pair] * BITS + [half],
        out_shape=[far((TOK, WIDTH)), far((2, TOK, WIDTH), F32), block, block]
        + [block] * BITS
        + [far((2, 2 * TOK, HALF))],
        scratch_shapes=[
            pltpu.VMEM((STEP, KEYS, HEAD_DIM), BF),
            pltpu.VMEM((STEP, KEYS, HEAD_DIM), BF),
            pltpu.VMEM((KEYS, TOK), F32),
        ],
        compiler_params=params(dimension_semantics=("arbitrary",)),
        name="backward",
    )(where, *from_hbm(q, k, v, lo, hi, *rand, glob, stats, d_attn))
    return outs[:4], outs[4 : 4 + BITS], outs[4 + BITS]


def head_of(i, where):
    return ((i // 2) ^ where[13]) * 2 + i % 2


def head_call(kernel, where, parts, extra, extra_spec, out_shape, out_spec, scratch, name):
    w_spec = pl.BlockSpec((HEAD_DIM, D), lambda i, at: (0, 0))
    return pl.pallas_call(
        kernel,
        grid_spec=pltpu.PrefetchScalarGridSpec(
            num_scalar_prefetch=1,
            grid=(HEADS,),
            in_specs=[w_spec] * HEADS + [extra_spec],
            out_specs=out_spec,
            scratch_shapes=scratch,
        ),
        out_shape=out_shape,
        compiler_params=params(dimension_semantics=("arbitrary",)),
        name=name,
    )(where, *from_hbm(*parts, extra))


def project_kernel(where, *refs):
    w, (d_out, out) = refs[:HEADS], refs[HEADS:]
    for i in range(HEADS):

        @pl.when(pl.program_id(0) == i)
        def _():
            out[...] = mm(d_out[...], w[i][...], ROWS).astype(BF)


def project(where, parts, d_out):
    return head_call(
        project_kernel,
        where,
        parts,
        d_out,
        pl.BlockSpec((TOK, D), lambda i, at: (0, 0)),
        far((TOK, WIDTH)),
        pl.BlockSpec((TOK, HEAD_DIM), lambda i, at: (0, head_of(i, at))),
        [],
        "project",
    )


def layer_kernel(where, *refs):
    w, (attn, out, acc) = refs[:HEADS], refs[HEADS:]
    for i in range(HEADS):

        @pl.when(pl.program_id(0) == i)
        def _():
            part = mm(attn[...], w[i][...], PLAIN)
            if i == 0:
                acc[...] = part
            elif i < HEADS - 1:
                acc[...] += part
            else:
                out[...] = (acc[...] + part).astype(BF)


def layer_of(where, parts, attn):
    return head_call(
        layer_kernel,
        where,
        parts,
        attn,
        pl.BlockSpec((TOK, HEAD_DIM), lambda i, at: (0, head_of(i, at))),
        far((TOK, D)),
        pl.BlockSpec((TOK, D), lambda i, at: (0, 0)),
        [pltpu.VMEM((TOK, D), F32)],
        "layer",
    )


def weight_kernel(*refs):
    cols, grads, (dglob, out) = refs[:4], refs[4:8], refs[8:]
    step = pl.program_id(0)

    @pl.when(step < 2)
    def _():
        out[...] = dglob[...]

    @pl.when(step >= 2)
    def _():
        part = mm(cols[0][...], grads[0][...], COLS)
        for a in range(1, 4):
            part += mm(cols[a][...], grads[a][...], COLS)
        out[...] = part.astype(BF).reshape(CHUNKS, 32, HALF)


def weight_payload(cols, grads, dglob):
    return pl.pallas_call(
        weight_kernel,
        grid=(6,),
        in_specs=[pl.BlockSpec((TOK, 256), lambda i: (0, 0))] * 4
        + [pl.BlockSpec((TOK, HALF), lambda i: (0, jnp.maximum(i - 2, 0)))]
        + [pl.BlockSpec((TOK, HALF), lambda i: (1, jnp.maximum(i - 2, 0)))] * 3
        + [pl.BlockSpec((CHUNKS, 32, HALF), lambda i: (0, jnp.minimum(i, 1), 0))],
        out_specs=pl.BlockSpec((CHUNKS, 32, HALF), lambda i: (0, i, 0)),
        out_shape=far((CHUNKS, 192, HALF)),
        compiler_params=params(dimension_semantics=("arbitrary",)),
        name="weight",
    )(*cols, *from_hbm(*grads, dglob))


def halve(where, bit, total, keep, stage):
    rows = keep.shape[0] // 4
    side = (where[11] // (1 << bit)) % 2
    for part in range(4):
        lower = total[2 * rows * part : 2 * rows * part + rows, :]
        upper = total[2 * rows * part + rows : 2 * rows * (part + 1), :]
        keep[rows * part : rows * (part + 1), :] = jnp.where(side == 0, lower, upper)
        stage[rows * part : rows * (part + 1), :] = jnp.where(side == 0, upper, lower)


def first_kernel(bit, where, x, glob, keep, send, total, stage):
    added = jnp.sum(x[...].astype(F32), axis=0)
    glob[...] = added[0:BLK]
    send[0:BLK, :] = added[0:BLK].astype(BF)
    total[...] = added[BLK:]
    halve(where, bit, total, keep, stage)
    send[BLK:, :] = stage[...].astype(BF)


def fold_kernel(bit, where, glob, kept, came, glob_out, keep, send, total, stage):
    added = came[...].astype(F32)
    glob_out[...] = glob[...] + added[0:BLK]
    send[0:BLK, :] = glob_out[...].astype(BF)
    total[...] = kept[...] + added[BLK:]
    halve(where, bit, total, keep, stage)
    send[BLK:, :] = stage[...].astype(BF)


def last_kernel(where, glob, kept, came, out, weight, total):
    added = came[...].astype(F32)
    chunk = (glob[...] + added[0:BLK]).astype(BF)
    target = jnp.where(where[10] == 0, where[8], where[9])
    for j in range(CHUNKS):
        out[j] = jnp.where(target == j, chunk, jnp.zeros_like(chunk))
    total[...] = kept[...] + added[BLK:]
    for part in range(4):
        weight[:, part * HALF : (part + 1) * HALF] = total[4 * part : 4 * part + 4, :]


def fold_call(kernel, where, args, rows, name):
    vm = pl.BlockSpec(memory_space=pltpu.VMEM)
    return pl.pallas_call(
        kernel,
        out_shape=[far((BLK, HALF), F32), far((rows, HALF), F32), far((BLK + rows, HALF))],
        in_specs=[smem()] + [vm] * len(args),
        out_specs=[vm] * 3,
        scratch_shapes=[pltpu.VMEM((2 * rows, HALF), F32), pltpu.VMEM((rows, HALF), F32)],
        compiler_params=params(),
        name=name,
    )(where, *args)


def first(where, x):
    return fold_call(lambda *refs: first_kernel(Z_BITS[0], *refs), where, (x,), 64, "first")


def fold(where, bit, glob, kept, came):
    rows = kept.shape[0] // 2
    return fold_call(lambda *refs: fold_kernel(bit, *refs), where, (glob, kept, came), rows, "fold")


def last(where, glob, kept, came):
    vm = pl.BlockSpec(memory_space=pltpu.VMEM)
    return pl.pallas_call(
        last_kernel,
        out_shape=[far((CHUNKS, BLK, HALF)), far((4, D), F32)],
        in_specs=[smem()] + [vm] * 3,
        out_specs=[vm] * 2,
        scratch_shapes=[pltpu.VMEM((16, HALF), F32)],
        compiler_params=params(),
        name="last",
    )(where, glob, kept, came)


def finish_kernel(where, own, left, right, *rest):
    rand, (glob, dk, dv, acc) = rest[:BITS], rest[BITS:]
    acc[...] = own[...]
    acc[:, 0:BLK, :] += left[...].astype(F32)
    acc[:, BLK : 2 * BLK, :] += right[...].astype(F32)
    for b in range(BITS):
        rows = pl.ds(pl.multiple_of(where[b] * BLK, BLK), BLK)
        acc[:, rows, :] += rand[b][...].astype(F32)
    for g in range(GLOB):
        here = where[6 + g]

        @pl.when(here >= 0)
        def _():
            rows = pl.ds(pl.multiple_of(jnp.maximum(here, 0) * BLK, BLK), BLK)
            acc[:, rows, :] += glob[0, :, g].astype(F32)

    dk[...] = acc[0].astype(BF)
    dv[...] = acc[1].astype(BF)


def finish(where, own, left, right, rand, glob):
    wide = 256
    pair = pl.BlockSpec((2, BLK, wide), lambda i: (0, 0, i))
    flat = pl.BlockSpec((TOK, wide), lambda i: (0, i))
    return pl.pallas_call(
        finish_kernel,
        grid=(WIDTH // wide,),
        in_specs=[smem(), pl.BlockSpec((2, TOK, wide), lambda i: (0, 0, i)), pair, pair]
        + [pair] * BITS
        + [pl.BlockSpec((1, 2, GLOB, BLK, wide), lambda i: (i // 2, 0, 0, 0, i % 2))],
        out_specs=[flat, flat],
        out_shape=[far((TOK, WIDTH)), far((TOK, WIDTH))],
        scratch_shapes=[pltpu.VMEM((2, TOK, wide), F32)],
        compiler_params=params(dimension_semantics=("arbitrary",)),
        name="finish",
    )(where, *from_hbm(own, left, right, *rand), glob)


def feature_order(rep):
    new = jnp.arange(WIDTH, dtype=jnp.int32)
    stretch = ((new // 64) % 4) * 16 + (new // 32) % 2
    for i, bit in enumerate(Z_BITS):
        stretch = stretch + ((new // (16 >> i)) % 2) * (1 << bit)
    old = stretch * 16 + ((new // 256) ^ rep) * 4 + new % 4
    return (jnp.arange(WIDTH, dtype=jnp.int32)[:, None] == old[None, :]).astype(BF)


def together(*values):
    return lax.optimization_barrier(values)


def per_device(queries, keys, values, w_out, d_out, rand_slot, global_ids):
    q, k, v, grad_out = queries[0], keys[0], values[0], d_out[0]
    where = where_of(rand_slot[0, 0], global_ids[0])
    *chosen, low_edge, high_edge, picked = pick(where, k, v)
    spread = trade(picked)
    mixed = jnp.concatenate([w_out[:HEAD_DIM], grad_out])
    upper = w_out[HEAD_DIM:]
    mixed2 = across(mixed, 2)
    upper2 = beside(upper)
    rand = [None] * BITS
    for b in FIRST:
        rand[b] = swapped(chosen[b], b)
    tied = together(spread, *[rand[b] for b in FIRST], low_edge, high_edge, *chosen)
    spread, tied = tied[0], tied[1:]
    for b in FIRST:
        rand[b], tied = tied[0], tied[1:]
    low_edge, high_edge, *chosen = tied
    mine = gathered(spread)
    for b in SECOND:
        rand[b] = swapped(chosen[b], b)
    for b in Z_BITS[:2]:
        mine = relay(mine, swapped(mine, b), (BLK, HALF))
    other = swapped(mine, Z_BITS[2])
    tied = together(
        mine, other, mixed2, upper2, *[rand[b] for b in SECOND], low_edge, high_edge, *chosen
    )
    mine, other, mixed2, upper2, *tied = tied
    for b in SECOND:
        rand[b], tied = tied[0], tied[1:]
    low_edge, high_edge, *chosen = tied
    glob = trade(relay(mine, other, (CHUNKS, BLK, HALF))).reshape(2, 2 * TOK, HALF)
    mixed3 = across(mixed2, 1)
    upper3 = across(upper2, 1)
    mixed1 = across(mixed, 1)
    upper1 = across(upper, 1)
    for b in THIRD:
        rand[b] = swapped(chosen[b], b)
    lo = shifted(high_edge, 1)
    hi = shifted(low_edge, -1)
    parts = (w_out, upper, mixed1, upper1, mixed2, upper2, mixed3, upper3)
    d_attn = project(where, parts, grad_out)
    order = feature_order(lax.axis_index("rep"))
    glob, lo, hi, d_attn, order, *tied = together(
        glob, lo, hi, d_attn, order, *[rand[b] for b in THIRD]
    )
    for b in THIRD:
        rand[b], tied = tied[0], tied[1:]
    lo, hi, *rand = from_hbm(lo, hi, *rand)
    attn, stats, *ordered = forward(
        where, *from_hbm(q, k, v), lo, hi, rand, glob, *from_hbm(order)
    )
    cols = [ordered[0]] + [across(ordered[a], a) for a in range(1, 4)]
    (dq, down, dlo, dhi), drand, dglob = backward(
        where, q, k, v, lo, hi, rand, glob, stats, d_attn
    )
    cols[1], cols[2], cols[3], dglob = together(cols[1], cols[2], cols[3], dglob)
    payload = weight_payload(
        cols, (grad_out, mixed1, mixed2, mixed3), dglob.reshape(CHUNKS, BLK, HALF)
    )
    payload = trade(payload)
    back = [None] * BITS
    for b in FIRST:
        back[b] = swapped(drand[b], b)
    payload, attn, dlo, dhi, *tied = together(
        payload, attn, dlo, dhi, *[back[b] for b in FIRST], *drand
    )
    for b in FIRST:
        back[b], tied = tied[0], tied[1:]
    drand = tied
    for b in SECOND:
        back[b] = swapped(drand[b], b)
    glob_sum, keep, send = first(where, payload)
    for step, bit in enumerate(Z_BITS[1:]):
        came = swapped(send, Z_BITS[step])
        glob_sum, keep, send = fold(where, bit, glob_sum, keep, came)
    came = swapped(send, Z_BITS[2])
    came, attn, dlo, dhi, *tied = together(
        came, attn, dlo, dhi, *[back[b] for b in SECOND], *drand
    )
    for b in SECOND:
        back[b], tied = tied[0], tied[1:]
    drand = tied
    routed, weight_grad = last(where, glob_sum, keep, came)
    glob_total = trade(routed).reshape(2, 2, GLOB, BLK, HALF)
    for b in THIRD:
        back[b] = swapped(drand[b], b)
    right = shifted(dlo, -1)
    left = shifted(dhi, 1)
    layer = layer_of(where, parts, attn)
    glob_total, layer = together(glob_total, layer)
    dk, dv = finish(where, down, left, right, back, glob_total)
    return (layer[None], dq[None], dk[None], dv[None], weight_grad)


def solution(mesh):
    return jax.shard_map(
        per_device,
        mesh=mesh,
        in_specs=(
            P("rep", "seq", None),
            P("rep", "seq", None),
            P("rep", "seq", None),
            P("rep", None),
            P("rep", "seq", None),
            P("rep", "seq", None),
            P("rep", None),
        ),
        out_specs=(
            P("rep", "seq", None),
            P("rep", "seq", None),
            P("rep", "seq", None),
            P("rep", "seq", None),
            P(("seq", "rep"), None),
        ),
        check_vma=False,
    )
```

```python
import jax
import jax.numpy as jnp
from jax import lax
from jax.experimental import pallas as pl
from jax.experimental.pallas import tpu as pltpu
from jax.sharding import PartitionSpec as P

HEADS = 8
HEAD_DIM = 128
BLK = 64
GLOB = 2
BITS = 6
TOK = 128
WIDTH = HEADS * HEAD_DIM
D = 2048
KEYS = 768
SCALE = HEAD_DIM ** (-0.5)
BF = jnp.bfloat16
F32 = jnp.float32
STEP = 4
WIDE = STEP * HEAD_DIM
ROWS = (((1,), (1,)), ((), ()))
COLS = (((0,), (0,)), ((), ()))
PLAIN = (((1,), (0,)), ((), ()))
VMEM_LIMIT = 20 * 1024 * 1024


def stretch_id(y, z, x):
    return y * 16 + z * 2 + x


YX_GROUPS = [[stretch_id(y, z, x) for y in range(4) for x in range(2)] for z in range(8)]
CHUNKS = 8
HALF = WIDTH // 2
Z_BITS = (1, 2, 3)
FIRST, SECOND, THIRD = (3, 4, 1), (5, 0), (2,)


def mm(left, right, dims):
    return lax.dot_general(left, right, dims, preferred_element_type=F32)


def trade(value):
    return lax.all_to_all(value, "seq", 0, 0, axis_index_groups=YX_GROUPS, tiled=True)


def shifted(value, steps):
    return lax.ppermute(value, "seq", [(s, (s + steps) % 64) for s in range(64)])


def swapped(value, bit):
    return lax.ppermute(value, "seq", [(s, s ^ (1 << bit)) for s in range(64)])


def along_z(value, steps):
    pairs = [(s, s // 16 * 16 + (s // 2 + steps) % 8 * 2 + s % 2) for s in range(64)]
    return lax.ppermute(value, "seq", pairs)


def across(value, flip):
    return lax.ppermute(value, "rep", [(r, r ^ flip) for r in range(4)])


def beside(value):
    pairs = [(s * 4 + r, (s ^ 1) * 4 + (r ^ 2)) for s in range(64) for r in range(4)]
    return lax.ppermute(value, ("seq", "rep"), pairs)


def far(shape, dtype=BF):
    return pltpu.HBM(shape, dtype)


def from_hbm(*values):
    return [pltpu.with_memory_space_constraint(x, pltpu.HBM) for x in values]


def smem():
    return pl.BlockSpec(memory_space=pltpu.SMEM)


def params(**kw):
    return pltpu.CompilerParams(vmem_limit_bytes=VMEM_LIMIT, **kw)


def where_of(rand_slot, global_ids):
    me = lax.axis_index("seq")
    rep = lax.axis_index("rep")
    owner = global_ids // 2
    here = jnp.where(owner == me, global_ids % 2, -1)
    tail = jnp.stack([me % 2, me, rep, rep])
    return jnp.concatenate([rand_slot, here, (owner // 16) * 2 + owner % 2, tail]).astype(
        jnp.int32
    )


def pick_kernel(where, k_ref, v_ref, *outs):
    for b in range(BITS):
        rows = pl.ds(pl.multiple_of(where[b] * BLK, BLK), BLK)
        outs[b][0] = k_ref[rows, :]
        outs[b][1] = v_ref[rows, :]
    first, last, picked = outs[BITS:]
    first[0] = k_ref[0:BLK, :]
    first[1] = v_ref[0:BLK, :]
    last[0] = k_ref[BLK : 2 * BLK, :]
    last[1] = v_ref[BLK : 2 * BLK, :]
    for g in range(GLOB):
        here = where[6 + g]
        rows = pl.ds(pl.multiple_of(jnp.maximum(here, 0) * BLK, BLK), BLK)
        for c, src in enumerate((k_ref, v_ref)):
            block = jnp.where(here >= 0, src[rows, :], jnp.zeros((BLK, WIDTH), BF))
            for half in range(2):
                picked[half * 4 + c * 2 + g] = block[:, half * HALF : (half + 1) * HALF]


def pick(where, keys, values):
    block = far((2, BLK, WIDTH))
    outs = [block] * (BITS + 2) + [far((CHUNKS, BLK, HALF))]
    vm = pl.BlockSpec(memory_space=pltpu.VMEM)
    return pl.pallas_call(
        pick_kernel,
        out_shape=outs,
        in_specs=[smem(), vm, vm],
        out_specs=[vm] * len(outs),
        compiler_params=params(),
        name="pick",
    )(where, keys, values)


def gathered_kernel(x_ref, o_ref):
    o_ref[...] = jnp.sum(x_ref[...].astype(F32), axis=0).astype(BF)


def gathered(x):
    return pl.pallas_call(
        gathered_kernel,
        out_shape=jax.ShapeDtypeStruct((BLK, HALF), BF),
        compiler_params=params(),
        name="gathered",
    )(x)


def near_kernel(mine, below, above, two, three):
    added = mine[...].astype(F32) + below[...].astype(F32)
    two[...] = added.astype(BF)
    three[...] = (added + above[...].astype(F32)).astype(BF)


def near(mine, below, above):
    return pl.pallas_call(
        near_kernel,
        out_shape=[jax.ShapeDtypeStruct((BLK, HALF), BF)] * 2,
        compiler_params=params(),
        name="near",
    )(mine, below, above)


def relay_kernel(mine, below, above, out):
    total = (mine[...].astype(F32) + below[...].astype(F32) + above[...].astype(F32)).astype(BF)
    for j in range(CHUNKS):
        out[j] = total


def relay(mine, below, above):
    return pl.pallas_call(
        relay_kernel,
        out_shape=far((CHUNKS, BLK, HALF)),
        compiler_params=params(),
        name="relay",
    )(mine, below, above)


def gather_heads(dst, c, cols, own, lo, hi, rand, glob):
    dst[0:64, :] = lo[c, :, cols]
    dst[64:192, :] = own[:, cols]
    dst[192:256, :] = hi[c, :, cols]
    dst[256:384, :] = glob[0, c * TOK : (c + 1) * TOK, cols]
    for b in range(BITS):
        dst[384 + 64 * b : 448 + 64 * b, :] = rand[b][c, :, cols]


def fill_bias(where, bias):
    lane = lax.broadcasted_iota(jnp.int32, (BLK, TOK), 1) // BLK
    for kb in range(12):
        if kb < 4:
            keep = jnp.logical_and(lane <= kb, lane >= kb - 2)
        elif kb < 6:
            keep = lane >= 0
        else:
            keep = lane == where[kb - 6]
        bias[kb * BLK : (kb + 1) * BLK, :] = jnp.where(keep, 0.0, -1e30).astype(F32)


def forward_kernel(where, q, k, v, lo, hi, *rest):
    rand, rest = rest[:BITS], rest[BITS:]
    glob, perm, attn, stats, *ordered, ks, vs, bias, acc = rest
    step = pl.program_id(0)

    @pl.when(step == 0)
    def _():
        fill_bias(where, bias)

    for i in range(STEP):
        cols = slice(i * HEAD_DIM, (i + 1) * HEAD_DIM)
        gather_heads(ks.at[i], 0, cols, k, lo, hi, rand, glob)
        gather_heads(vs.at[i], 1, cols, v, lo, hi, rand, glob)
        scores = mm(ks[i], q[:, cols], ROWS) * SCALE + bias[...]
        top = jnp.max(scores, axis=0, keepdims=True)
        expd = jnp.exp(scores - top)
        inv = 1.0 / jnp.sum(expd, axis=0, keepdims=True)
        probs = (expd * inv).astype(BF)
        attn[:, cols] = mm(probs, vs[i], COLS).astype(BF)
        stats[i, 0:1, :] = top
        stats[i, 1:2, :] = inv

    part = mm(attn[...], perm[...], PLAIN)

    @pl.when(step == 0)
    def _():
        acc[...] = part

    @pl.when(step == HEADS // STEP - 1)
    def _():
        total = acc[...] + part
        for r in range(4):
            ordered[r][...] = total[:, r * 256 : (r + 1) * 256].astype(BF)


def head_specs():
    flat = pl.BlockSpec((TOK, WIDE), lambda h: (0, h))
    pair = pl.BlockSpec((2, BLK, WIDE), lambda h: (0, 0, h))
    both = pl.BlockSpec((2, TOK, WIDE), lambda h: (0, 0, h))
    half = pl.BlockSpec((1, 2 * TOK, WIDE), lambda h: (h, 0, 0))
    return flat, pair, both, half


def forward(where, q, k, v, lo, hi, rand, glob, perm):
    flat, pair, both, half = head_specs()
    return pl.pallas_call(
        forward_kernel,
        grid=(HEADS // STEP,),
        in_specs=[smem(), flat, flat, flat, pair, pair]
        + [pair] * BITS
        + [half, pl.BlockSpec((WIDE, WIDTH), lambda h: (h, 0))],
        out_specs=[
            flat,
            pl.BlockSpec((STEP, 8, TOK), lambda h: (h, 0, 0)),
        ]
        + [pl.BlockSpec((TOK, 256), lambda h: (0, 0))] * 4,
        out_shape=[
            far((TOK, WIDTH)),
            far((HEADS, 8, TOK), F32),
        ]
        + [jax.ShapeDtypeStruct((TOK, 256), BF)] * 4,
        scratch_shapes=[
            pltpu.VMEM((STEP, KEYS, HEAD_DIM), BF),
            pltpu.VMEM((STEP, KEYS, HEAD_DIM), BF),
            pltpu.VMEM((KEYS, TOK), F32),
            pltpu.VMEM((TOK, WIDTH), F32),
        ],
        compiler_params=params(dimension_semantics=("arbitrary",)),
        name="forward",
    )(where, q, k, v, lo, hi, *rand, glob, perm)


def backward_kernel(where, q, k, v, lo, hi, *rest):
    rand, rest = rest[:BITS], rest[BITS:]
    glob, stats, d_attn_ref, dq, down, dlo, dhi = rest[:7]
    drand, rest = rest[7 : 7 + BITS], rest[7 + BITS :]
    dglob, ks, vs, bias = rest

    @pl.when(pl.program_id(0) == 0)
    def _():
        fill_bias(where, bias)

    for i in range(STEP):
        cols = slice(i * HEAD_DIM, (i + 1) * HEAD_DIM)
        gather_heads(ks.at[i], 0, cols, k, lo, hi, rand, glob)
        gather_heads(vs.at[i], 1, cols, v, lo, hi, rand, glob)
        d_attn = d_attn_ref[:, cols]
        scores = mm(ks[i], q[:, cols], ROWS) * SCALE + bias[...]
        probs = jnp.exp(scores - stats[i, 0:1, :]) * stats[i, 1:2, :]
        probs_b = probs.astype(BF)
        dprob = mm(vs[i], d_attn, ROWS)
        delta = jnp.sum(dprob * probs, axis=0, keepdims=True)
        dscore = (probs * (dprob - delta) * SCALE).astype(BF)
        dq[:, cols] = mm(dscore, ks[i], COLS).astype(BF)
        for c, grad in ((0, mm(dscore, q[:, cols], PLAIN)), (1, mm(probs_b, d_attn, PLAIN))):
            dlo[c, :, cols] = grad[0:64].astype(BF)
            down[c, :, cols] = grad[64:192]
            dhi[c, :, cols] = grad[192:256].astype(BF)
            dglob[0, c * TOK : (c + 1) * TOK, cols] = grad[256:384].astype(BF)
            for b in range(BITS):
                drand[b][c, :, cols] = grad[384 + 64 * b : 448 + 64 * b].astype(BF)


def backward(where, q, k, v, lo, hi, rand, glob, stats, d_attn):
    flat, pair, both, half = head_specs()
    block = far((2, BLK, WIDTH))
    outs = pl.pallas_call(
        backward_kernel,
        grid=(HEADS // STEP,),
        in_specs=[smem(), flat, flat, flat, pair, pair]
        + [pair] * BITS
        + [half, pl.BlockSpec((STEP, 8, TOK), lambda h: (h, 0, 0)), flat],
        out_specs=[flat, both, pair, pair] + [pair] * BITS + [half],
        out_shape=[far((TOK, WIDTH)), far((2, TOK, WIDTH), F32), block, block]
        + [block] * BITS
        + [far((2, 2 * TOK, HALF))],
        scratch_shapes=[
            pltpu.VMEM((STEP, KEYS, HEAD_DIM), BF),
            pltpu.VMEM((STEP, KEYS, HEAD_DIM), BF),
            pltpu.VMEM((KEYS, TOK), F32),
        ],
        compiler_params=params(dimension_semantics=("arbitrary",)),
        name="backward",
    )(where, *from_hbm(q, k, v, lo, hi, *rand, glob, stats, d_attn))
    return outs[:4], outs[4 : 4 + BITS], outs[4 + BITS]


def head_of(i, where):
    return ((i // 2) ^ where[13]) * 2 + i % 2


def head_call(kernel, where, parts, extra, extra_spec, out_shape, out_spec, scratch, name):
    w_spec = pl.BlockSpec((HEAD_DIM, D), lambda i, at: (0, 0))
    return pl.pallas_call(
        kernel,
        grid_spec=pltpu.PrefetchScalarGridSpec(
            num_scalar_prefetch=1,
            grid=(HEADS,),
            in_specs=[w_spec] * HEADS + [extra_spec],
            out_specs=out_spec,
            scratch_shapes=scratch,
        ),
        out_shape=out_shape,
        compiler_params=params(dimension_semantics=("arbitrary",)),
        name=name,
    )(where, *from_hbm(*parts, extra))


def project_kernel(where, *refs):
    w, (d_out, out) = refs[:HEADS], refs[HEADS:]
    for i in range(HEADS):

        @pl.when(pl.program_id(0) == i)
        def _():
            out[...] = mm(d_out[...], w[i][...], ROWS).astype(BF)


def project(where, parts, d_out):
    return head_call(
        project_kernel,
        where,
        parts,
        d_out,
        pl.BlockSpec((TOK, D), lambda i, at: (0, 0)),
        far((TOK, WIDTH)),
        pl.BlockSpec((TOK, HEAD_DIM), lambda i, at: (0, head_of(i, at))),
        [],
        "project",
    )


def layer_kernel(where, *refs):
    w, (attn, out, acc) = refs[:HEADS], refs[HEADS:]
    for i in range(HEADS):

        @pl.when(pl.program_id(0) == i)
        def _():
            part = mm(attn[...], w[i][...], PLAIN)
            if i == 0:
                acc[...] = part
            elif i < HEADS - 1:
                acc[...] += part
            else:
                out[...] = (acc[...] + part).astype(BF)


def layer_of(where, parts, attn):
    return head_call(
        layer_kernel,
        where,
        parts,
        attn,
        pl.BlockSpec((TOK, HEAD_DIM), lambda i, at: (0, head_of(i, at))),
        far((TOK, D)),
        pl.BlockSpec((TOK, D), lambda i, at: (0, 0)),
        [pltpu.VMEM((TOK, D), F32)],
        "layer",
    )


def weight_kernel(*refs):
    cols, grads, (dglob, out) = refs[:4], refs[4:8], refs[8:]
    step = pl.program_id(0)

    @pl.when(step == 0)
    def _():
        out[...] = dglob[...]

    @pl.when(step > 0)
    def _():
        part = mm(cols[0][...], grads[0][...], COLS)
        for a in range(1, 4):
            part += mm(cols[a][...], grads[a][...], COLS)
        part = part.astype(BF)
        for i in range(2):
            out[:, 32 * i : 32 * i + 32, :] = part[:, HALF * i : HALF * (i + 1)].reshape(
                CHUNKS, 32, HALF
            )


def weight_payload(cols, grads, dglob):
    return pl.pallas_call(
        weight_kernel,
        grid=(3,),
        in_specs=[pl.BlockSpec((TOK, 256), lambda i: (0, 0))] * 4
        + [pl.BlockSpec((TOK, WIDTH), lambda i: (0, jnp.maximum(i - 1, 0)))]
        + [pl.BlockSpec((TOK, WIDTH), lambda i: (1, jnp.maximum(i - 1, 0)))] * 3
        + [pl.BlockSpec((CHUNKS, BLK, HALF), lambda i: (0, 0, 0))],
        out_specs=pl.BlockSpec((CHUNKS, BLK, HALF), lambda i: (0, i, 0)),
        out_shape=far((CHUNKS, 192, HALF)),
        compiler_params=params(dimension_semantics=("arbitrary",)),
        name="weight",
    )(*cols, *from_hbm(*grads, dglob))


def halve(where, bit, total, keep, stage):
    rows = keep.shape[0] // 4
    side = (where[11] // (1 << bit)) % 2
    for part in range(4):
        lower = total[2 * rows * part : 2 * rows * part + rows, :]
        upper = total[2 * rows * part + rows : 2 * rows * (part + 1), :]
        keep[rows * part : rows * (part + 1), :] = jnp.where(side == 0, lower, upper)
        stage[rows * part : rows * (part + 1), :] = jnp.where(side == 0, upper, lower)


def first_kernel(bit, where, x, glob, keep, send, total, stage):
    added = jnp.sum(x[...].astype(F32), axis=0)
    glob[...] = added[0:BLK]
    send[0:BLK, :] = added[0:BLK].astype(BF)
    total[...] = added[BLK:]
    halve(where, bit, total, keep, stage)
    send[BLK:, :] = stage[...].astype(BF)


def fold_kernel(bit, where, glob, kept, came, glob_out, keep, send, total, stage):
    added = came[...].astype(F32)
    glob_out[...] = glob[...] + added[0:BLK]
    send[0:BLK, :] = glob_out[...].astype(BF)
    total[...] = kept[...] + added[BLK:]
    halve(where, bit, total, keep, stage)
    send[BLK:, :] = stage[...].astype(BF)


def last_kernel(where, glob, kept, came, out, weight, total):
    added = came[...].astype(F32)
    chunk = (glob[...] + added[0:BLK]).astype(BF)
    target = jnp.where(where[10] == 0, where[8], where[9])
    for j in range(CHUNKS):
        out[j] = jnp.where(target == j, chunk, jnp.zeros_like(chunk))
    total[...] = kept[...] + added[BLK:]
    for part in range(4):
        weight[:, part * HALF : (part + 1) * HALF] = total[4 * part : 4 * part + 4, :]


def fold_call(kernel, where, args, rows, name):
    vm = pl.BlockSpec(memory_space=pltpu.VMEM)
    return pl.pallas_call(
        kernel,
        out_shape=[
            jax.ShapeDtypeStruct((BLK, HALF), F32),
            jax.ShapeDtypeStruct((rows, HALF), F32),
            jax.ShapeDtypeStruct((BLK + rows, HALF), BF),
        ],
        in_specs=[smem()] + [vm] * len(args),
        out_specs=[vm] * 3,
        scratch_shapes=[pltpu.VMEM((2 * rows, HALF), F32), pltpu.VMEM((rows, HALF), F32)],
        compiler_params=params(),
        name=name,
    )(where, *args)


def first(where, x):
    return fold_call(lambda *refs: first_kernel(Z_BITS[0], *refs), where, (x,), 64, "first")


def fold(where, bit, glob, kept, came):
    rows = kept.shape[0] // 2
    return fold_call(lambda *refs: fold_kernel(bit, *refs), where, (glob, kept, came), rows, "fold")


def last(where, glob, kept, came):
    vm = pl.BlockSpec(memory_space=pltpu.VMEM)
    return pl.pallas_call(
        last_kernel,
        out_shape=[far((CHUNKS, BLK, HALF)), far((4, D), F32)],
        in_specs=[smem()] + [vm] * 3,
        out_specs=[vm] * 2,
        scratch_shapes=[pltpu.VMEM((16, HALF), F32)],
        compiler_params=params(),
        name="last",
    )(where, glob, kept, came)


def finish_kernel(where, own, left, right, *rest):
    rand, (glob, dk, dv, acc) = rest[:BITS], rest[BITS:]
    acc[...] = own[...]
    acc[:, 0:BLK, :] += left[...].astype(F32)
    acc[:, BLK : 2 * BLK, :] += right[...].astype(F32)
    for b in range(BITS):
        rows = pl.ds(pl.multiple_of(where[b] * BLK, BLK), BLK)
        acc[:, rows, :] += rand[b][...].astype(F32)
    for g in range(GLOB):
        here = where[6 + g]

        @pl.when(here >= 0)
        def _():
            rows = pl.ds(pl.multiple_of(jnp.maximum(here, 0) * BLK, BLK), BLK)
            acc[:, rows, :] += glob[0, :, g].astype(F32)

    dk[...] = acc[0].astype(BF)
    dv[...] = acc[1].astype(BF)


def finish(where, own, left, right, rand, glob):
    wide = 256
    pair = pl.BlockSpec((2, BLK, wide), lambda i: (0, 0, i))
    flat = pl.BlockSpec((TOK, wide), lambda i: (0, i))
    return pl.pallas_call(
        finish_kernel,
        grid=(WIDTH // wide,),
        in_specs=[smem(), pl.BlockSpec((2, TOK, wide), lambda i: (0, 0, i)), pair, pair]
        + [pair] * BITS
        + [pl.BlockSpec((1, 2, GLOB, BLK, wide), lambda i: (i // 2, 0, 0, 0, i % 2))],
        out_specs=[flat, flat],
        out_shape=[far((TOK, WIDTH)), far((TOK, WIDTH))],
        scratch_shapes=[pltpu.VMEM((2, TOK, wide), F32)],
        compiler_params=params(dimension_semantics=("arbitrary",)),
        name="finish",
    )(where, *from_hbm(own, left, right, *rand), glob)


def feature_order(rep):
    new = jnp.arange(WIDTH, dtype=jnp.int32)
    stretch = ((new // 64) % 4) * 16 + (new // 32) % 2
    for i, bit in enumerate(Z_BITS):
        stretch = stretch + ((new // (16 >> i)) % 2) * (1 << bit)
    old = stretch * 16 + ((new // 256) ^ rep) * 4 + new % 4
    return (jnp.arange(WIDTH, dtype=jnp.int32)[:, None] == old[None, :]).astype(BF)


def together(*values):
    return lax.optimization_barrier(values)


def per_device(queries, keys, values, w_out, d_out, rand_slot, global_ids):
    q, k, v, grad_out = queries[0], keys[0], values[0], d_out[0]
    where = where_of(rand_slot[0, 0], global_ids[0])
    *chosen, low_edge, high_edge, picked = pick(where, k, v)
    spread = trade(picked)
    mixed = jnp.concatenate([w_out[:HEAD_DIM], grad_out])
    upper = w_out[HEAD_DIM:]
    mixed2 = across(mixed, 2)
    upper2 = beside(upper)
    order = feature_order(lax.axis_index("rep"))
    rand = [None] * BITS
    for b in FIRST:
        rand[b] = swapped(chosen[b], b)
    spread, mixed, upper, mixed2, upper2, order, *tied = together(
        spread,
        mixed,
        upper,
        mixed2,
        upper2,
        order,
        *[rand[b] for b in FIRST],
        low_edge,
        high_edge,
        *chosen,
    )
    for b in FIRST:
        rand[b], tied = tied[0], tied[1:]
    low_edge, high_edge, *chosen = tied
    mine = gathered(spread)
    mixed1 = across(mixed, 1)
    upper1 = across(upper, 1)
    mixed3 = across(mixed2, 1)
    upper3 = across(upper2, 1)
    for b in SECOND:
        rand[b] = swapped(chosen[b], b)
    two, three = near(mine, along_z(mine, 1), along_z(mine, -1))
    below, above = along_z(three, 3), along_z(two, -3)
    parts = (w_out, upper, mixed1, upper1, mixed2, upper2, mixed3, upper3)
    d_attn = project(where, parts, grad_out)
    below, above, d_attn, *tied = together(
        below, above, d_attn, *[rand[b] for b in SECOND], low_edge, high_edge, *chosen
    )
    for b in SECOND:
        rand[b], tied = tied[0], tied[1:]
    low_edge, high_edge, *chosen = tied
    glob = trade(relay(three, below, above)).reshape(2, 2 * TOK, HALF)
    for b in THIRD:
        rand[b] = swapped(chosen[b], b)
    lo = shifted(high_edge, 1)
    hi = shifted(low_edge, -1)
    glob, lo, hi, *tied = together(glob, lo, hi, *[rand[b] for b in THIRD])
    for b in THIRD:
        rand[b], tied = tied[0], tied[1:]
    lo, hi, *rand = from_hbm(lo, hi, *rand)
    attn, stats, *ordered = forward(
        where, *from_hbm(q, k, v), lo, hi, rand, glob, *from_hbm(order)
    )
    cols = [ordered[0]] + [across(ordered[a], a) for a in range(1, 4)]
    (dq, down, dlo, dhi), drand, dglob = backward(
        where, q, k, v, lo, hi, rand, glob, stats, d_attn
    )
    cols[1], cols[2], cols[3], dglob = together(cols[1], cols[2], cols[3], dglob)
    payload = weight_payload(
        cols, (grad_out, mixed1, mixed2, mixed3), dglob.reshape(CHUNKS, BLK, HALF)
    )
    payload = trade(payload)
    back = [None] * BITS
    for b in FIRST:
        back[b] = swapped(drand[b], b)
    layer = layer_of(where, parts, attn)
    payload, layer, dlo, dhi, *tied = together(
        payload, layer, dlo, dhi, *[back[b] for b in FIRST], *drand
    )
    for b in FIRST:
        back[b], tied = tied[0], tied[1:]
    drand = tied
    for b in SECOND:
        back[b] = swapped(drand[b], b)
    glob_sum, keep, send = first(where, payload)
    for step, bit in enumerate(Z_BITS[1:]):
        came = swapped(send, Z_BITS[step])
        glob_sum, keep, send = fold(where, bit, glob_sum, keep, came)
    came = swapped(send, Z_BITS[2])
    came, dlo, dhi, *tied = together(came, dlo, dhi, *[back[b] for b in SECOND], *drand)
    for b in SECOND:
        back[b], tied = tied[0], tied[1:]
    drand = tied
    routed, weight_grad = last(where, glob_sum, keep, came)
    glob_total = trade(routed).reshape(2, 2, GLOB, BLK, HALF)
    for b in THIRD:
        back[b] = swapped(drand[b], b)
    right = shifted(dlo, -1)
    left = shifted(dhi, 1)
    dk, dv = finish(where, down, left, right, back, glob_total)
    return (layer[None], dq[None], dk[None], dv[None], weight_grad)


def solution(mesh):
    return jax.shard_map(
        per_device,
        mesh=mesh,
        in_specs=(
            P("rep", "seq", None),
            P("rep", "seq", None),
            P("rep", "seq", None),
            P("rep", None),
            P("rep", "seq", None),
            P("rep", "seq", None),
            P("rep", None),
        ),
        out_specs=(
            P("rep", "seq", None),
            P("rep", "seq", None),
            P("rep", "seq", None),
            P("rep", "seq", None),
            P(("seq", "rep"), None),
        ),
        check_vma=False,
    )
```

```python
import jax
import jax.numpy as jnp
from jax import lax
from jax.experimental import pallas as pl
from jax.experimental.pallas import tpu as pltpu
from jax.sharding import PartitionSpec as P

HEADS = 8
HEAD_DIM = 128
BLK = 64
GLOB = 2
BITS = 6
TOK = 128
WIDTH = HEADS * HEAD_DIM
D = 2048
KEYS = 768
SCALE = HEAD_DIM ** (-0.5)
BF = jnp.bfloat16
F32 = jnp.float32
STEP = 4
WIDE = STEP * HEAD_DIM
ROWS = (((1,), (1,)), ((), ()))
COLS = (((0,), (0,)), ((), ()))
PLAIN = (((1,), (0,)), ((), ()))
VMEM_LIMIT = 20 * 1024 * 1024


def stretch_id(y, z, x):
    return y * 16 + z * 2 + x


YX_GROUPS = [[stretch_id(y, z, x) for y in range(4) for x in range(2)] for z in range(8)]
CHUNKS = 8
PARTS = 4
HALF = WIDTH // 2
Z_BITS = (1, 2, 3)
FIRST, THIRD = (3, 4), (2, 1, 5)


def mm(left, right, dims):
    return lax.dot_general(left, right, dims, preferred_element_type=F32)


def trade(value):
    return lax.all_to_all(value, "seq", 0, 0, axis_index_groups=YX_GROUPS, tiled=True)


def swapped(value, bit):
    return lax.ppermute(value, "seq", [(s, s ^ (1 << bit)) for s in range(64)])


def along_z(value, steps):
    pairs = [(s, s // 16 * 16 + (s // 2 + steps) % 8 * 2 + s % 2) for s in range(64)]
    return lax.ppermute(value, "seq", pairs)


def across(value, flip):
    return lax.ppermute(value, "rep", [(r, r ^ flip) for r in range(4)])


def far(shape, dtype=BF):
    return pltpu.HBM(shape, dtype)


def from_hbm(*values):
    return [pltpu.with_memory_space_constraint(x, pltpu.HBM) for x in values]


def smem():
    return pl.BlockSpec(memory_space=pltpu.SMEM)


def params(**kw):
    return pltpu.CompilerParams(vmem_limit_bytes=VMEM_LIMIT, **kw)


def where_of(rand_slot, global_ids):
    me = lax.axis_index("seq")
    rep = lax.axis_index("rep")
    owner = global_ids // 2
    here = jnp.where(owner == me, global_ids % 2, -1)
    tail = jnp.stack([me % 2, me, rep, rep])
    return jnp.concatenate([rand_slot, here, (owner // 16) * 2 + owner % 2, tail]).astype(
        jnp.int32
    )


def paired(value):
    return swapped(value, 0)


def neighboured(value):
    return lax.ppermute(value, "seq", [(s, (s - 1 + s % 2 * 2) % 64) for s in range(64)])


def inner_block(where):
    return 1 - where[11] % 2


def pick_kernel(where, k_ref, v_ref, pair, outer, *outs):
    def block(index):
        return pl.ds(pl.multiple_of(index * BLK, BLK), BLK)

    inner = inner_block(where)
    for c, src in enumerate((k_ref, v_ref)):
        pair[0, c] = src[block(where[0]), :]
        pair[1, c] = src[block(inner), :]
        outer[c] = src[block(1 - inner), :]
        for b in range(1, BITS):
            outs[b - 1][c] = src[block(where[b]), :]
    picked = outs[BITS - 1]
    for g in range(GLOB):
        here = where[6 + g]
        rows = pl.ds(pl.multiple_of(jnp.maximum(here, 0) * BLK, BLK), BLK)
        for c, src in enumerate((k_ref, v_ref)):
            block = jnp.where(here >= 0, src[rows, :], jnp.zeros((BLK, WIDTH), BF))
            for half in range(2):
                picked[half * 4 + c * 2 + g] = block[:, half * HALF : (half + 1) * HALF]


def pick(where, keys, values):
    block = far((2, BLK, WIDTH))
    outs = [far((2, 2, BLK, WIDTH))] + [block] * BITS + [far((CHUNKS, BLK, HALF))]
    vm = pl.BlockSpec(memory_space=pltpu.VMEM)
    return pl.pallas_call(
        pick_kernel,
        out_shape=outs,
        in_specs=[smem(), vm, vm],
        out_specs=[vm] * len(outs),
        compiler_params=params(),
        name="pick",
    )(where, *from_hbm(keys, values))


def gathered_kernel(x_ref, o_ref):
    o_ref[...] = jnp.sum(x_ref[...].astype(F32), axis=0).astype(BF)


def gathered(x):
    return pl.pallas_call(
        gathered_kernel,
        out_shape=jax.ShapeDtypeStruct((BLK, HALF), BF),
        compiler_params=params(),
        name="gathered",
    )(x)


def near_kernel(mine, below, above, two, three):
    added = mine[...].astype(F32) + below[...].astype(F32)
    two[...] = added.astype(BF)
    three[...] = (added + above[...].astype(F32)).astype(BF)


def near(mine, below, above):
    return pl.pallas_call(
        near_kernel,
        out_shape=[jax.ShapeDtypeStruct((BLK, HALF), BF)] * 2,
        compiler_params=params(),
        name="near",
    )(mine, below, above)


def relay_kernel(mine, below, above, out):
    total = (mine[...].astype(F32) + below[...].astype(F32) + above[...].astype(F32)).astype(BF)
    for j in range(CHUNKS):
        out[j] = total


def relay(mine, below, above):
    return pl.pallas_call(
        relay_kernel,
        out_shape=far((CHUNKS, BLK, HALF)),
        compiler_params=params(),
        name="relay",
    )(mine, below, above)


def gather_heads(where, dst, c, cols, own, pair, outer, rand, glob):
    inner = inner_block(where)
    dst[pl.ds(pl.multiple_of(inner * 192, 64), BLK), :] = pair[1, c, :, cols]
    dst[pl.ds(pl.multiple_of((1 - inner) * 192, 64), BLK), :] = outer[c, :, cols]
    dst[64:192, :] = own[:, cols]
    dst[256:384, :] = glob[0, c * TOK : (c + 1) * TOK, cols]
    dst[384:448, :] = pair[0, c, :, cols]
    for b in range(1, BITS):
        dst[384 + 64 * b : 448 + 64 * b, :] = rand[b - 1][c, :, cols]


def fill_bias(where, bias):
    lane = lax.broadcasted_iota(jnp.int32, (BLK, TOK), 1) // BLK
    for kb in range(12):
        if kb < 4:
            keep = jnp.logical_and(lane <= kb, lane >= kb - 2)
        elif kb < 6:
            keep = lane >= 0
        else:
            keep = lane == where[kb - 6]
        bias[kb * BLK : (kb + 1) * BLK, :] = jnp.where(keep, 0.0, -1e30).astype(F32)


def forward_kernel(where, q, k, v, pair, outer, *rest):
    rand, rest = rest[: BITS - 1], rest[BITS - 1 :]
    glob, perm, attn, stats, *ordered, ks, vs, bias, acc = rest
    step = pl.program_id(0)

    @pl.when(step == 0)
    def _():
        fill_bias(where, bias)

    for i in range(STEP):
        cols = slice(i * HEAD_DIM, (i + 1) * HEAD_DIM)
        gather_heads(where, ks.at[i], 0, cols, k, pair, outer, rand, glob)
        gather_heads(where, vs.at[i], 1, cols, v, pair, outer, rand, glob)
        scores = mm(ks[i], q[:, cols], ROWS) * SCALE + bias[...]
        top = jnp.max(scores, axis=0, keepdims=True)
        expd = jnp.exp(scores - top)
        inv = 1.0 / jnp.sum(expd, axis=0, keepdims=True)
        probs = (expd * inv).astype(BF)
        attn[:, cols] = mm(probs, vs[i], COLS).astype(BF)
        stats[i, 0:1, :] = top
        stats[i, 1:2, :] = inv

    part = mm(attn[...], perm[...], PLAIN)

    @pl.when(step == 0)
    def _():
        acc[...] = part

    @pl.when(step == HEADS // STEP - 1)
    def _():
        total = acc[...] + part
        for r in range(4):
            ordered[r][...] = total[:, r * 256 : (r + 1) * 256].astype(BF)


def head_specs():
    flat = pl.BlockSpec((TOK, WIDE), lambda h: (0, h))
    pair = pl.BlockSpec((2, BLK, WIDE), lambda h: (0, 0, h))
    both = pl.BlockSpec((2, TOK, WIDE), lambda h: (0, 0, h))
    half = pl.BlockSpec((1, 2 * TOK, WIDE), lambda h: (h, 0, 0))
    two = pl.BlockSpec((2, 2, BLK, WIDE), lambda h: (0, 0, 0, h))
    return flat, pair, both, half, two


def forward(where, q, k, v, pair, outer, rand, glob, perm):
    flat, block, both, half, two = head_specs()
    return pl.pallas_call(
        forward_kernel,
        grid=(HEADS // STEP,),
        in_specs=[smem(), flat, flat, flat, two]
        + [block] * BITS
        + [half, pl.BlockSpec((WIDE, WIDTH), lambda h: (h, 0))],
        out_specs=[
            flat,
            pl.BlockSpec((STEP, 8, TOK), lambda h: (h, 0, 0)),
        ]
        + [pl.BlockSpec((TOK, 256), lambda h: (0, 0))] * 4,
        out_shape=[
            far((TOK, WIDTH)),
            far((HEADS, 8, TOK), F32),
        ]
        + [jax.ShapeDtypeStruct((TOK, 256), BF)] * 4,
        scratch_shapes=[
            pltpu.VMEM((STEP, KEYS, HEAD_DIM), BF),
            pltpu.VMEM((STEP, KEYS, HEAD_DIM), BF),
            pltpu.VMEM((KEYS, TOK), F32),
            pltpu.VMEM((TOK, WIDTH), F32),
        ],
        compiler_params=params(dimension_semantics=("arbitrary",)),
        name="forward",
    )(where, q, k, v, pair, outer, *rand, glob, perm)


def backward_kernel(where, q, k, v, pair, outer, *rest):
    rand, rest = rest[: BITS - 1], rest[BITS - 1 :]
    low = inner_block(where) == 0
    glob, stats, d_attn_ref, dq, down, dpair, douter = rest[:7]
    drand, rest = rest[7 : 6 + BITS], rest[6 + BITS :]
    dglob, ks, vs, bias = rest

    @pl.when(pl.program_id(0) == 0)
    def _():
        fill_bias(where, bias)

    for i in range(STEP):
        cols = slice(i * HEAD_DIM, (i + 1) * HEAD_DIM)
        gather_heads(where, ks.at[i], 0, cols, k, pair, outer, rand, glob)
        gather_heads(where, vs.at[i], 1, cols, v, pair, outer, rand, glob)
        d_attn = d_attn_ref[:, cols]
        scores = mm(ks[i], q[:, cols], ROWS) * SCALE + bias[...]
        probs = jnp.exp(scores - stats[i, 0:1, :]) * stats[i, 1:2, :]
        probs_b = probs.astype(BF)
        dprob = mm(vs[i], d_attn, ROWS)
        delta = jnp.sum(dprob * probs, axis=0, keepdims=True)
        dscore = (probs * (dprob - delta) * SCALE).astype(BF)
        dq[:, cols] = mm(dscore, ks[i], COLS).astype(BF)
        for c, grad in ((0, mm(dscore, q[:, cols], PLAIN)), (1, mm(probs_b, d_attn, PLAIN))):
            before, after = grad[0:64], grad[192:256]
            dpair[0, c, :, cols] = grad[384:448].astype(BF)
            dpair[1, c, :, cols] = jnp.where(low, before, after).astype(BF)
            douter[c, :, cols] = jnp.where(low, after, before).astype(BF)
            down[c, :, cols] = grad[64:192]
            dglob[0, c * TOK : (c + 1) * TOK, cols] = grad[256:384].astype(BF)
            for b in range(1, BITS):
                drand[b - 1][c, :, cols] = grad[384 + 64 * b : 448 + 64 * b].astype(BF)


def backward(where, q, k, v, pair, outer, rand, glob, stats, d_attn):
    flat, block, both, half, two = head_specs()
    out = far((2, BLK, WIDTH))
    outs = pl.pallas_call(
        backward_kernel,
        grid=(HEADS // STEP,),
        in_specs=[smem(), flat, flat, flat, two]
        + [block] * BITS
        + [half, pl.BlockSpec((STEP, 8, TOK), lambda h: (h, 0, 0)), flat],
        out_specs=[flat, both, two] + [block] * BITS + [half],
        out_shape=[far((TOK, WIDTH)), far((2, TOK, WIDTH), F32), far((2, 2, BLK, WIDTH))]
        + [out] * BITS
        + [far((2, 2 * TOK, HALF))],
        scratch_shapes=[
            pltpu.VMEM((STEP, KEYS, HEAD_DIM), BF),
            pltpu.VMEM((STEP, KEYS, HEAD_DIM), BF),
            pltpu.VMEM((KEYS, TOK), F32),
        ],
        compiler_params=params(dimension_semantics=("arbitrary",)),
        name="backward",
    )(where, *from_hbm(q, k, v, pair, outer, *rand, glob, stats, d_attn))
    return outs[:4], outs[4 : 3 + BITS], outs[3 + BITS]


def place_weights(where, parts, w, sems):
    copies = []
    for i in range(PARTS):
        rows = pl.ds(pl.multiple_of((i ^ where[13]) * 256, 256), 256)
        copies.append(pltpu.make_async_copy(parts[i], w.at[rows, :], sems.at[i]))
    for copy in copies:
        copy.start()
    for copy in copies:
        copy.wait()


def project_kernel(where, *refs):
    parts, (d_out, out, w, sems) = refs[:PARTS], refs[PARTS:]
    place_weights(where, parts, w, sems)
    out[...] = mm(d_out[...], w[...], ROWS).astype(BF)


def layer_kernel(where, *refs):
    parts, (attn, out, w, sems) = refs[:PARTS], refs[PARTS:]
    place_weights(where, parts, w, sems)
    out[...] = mm(attn[...], w[...], PLAIN).astype(BF)


def weights_call(kernel, where, parts, rows, width, name):
    vm = pl.BlockSpec(memory_space=pltpu.VMEM)
    return pl.pallas_call(
        kernel,
        out_shape=far((TOK, width)),
        in_specs=[smem()] + [pl.BlockSpec(memory_space=pl.ANY)] * PARTS + [vm],
        out_specs=vm,
        scratch_shapes=[pltpu.VMEM((WIDTH, D), BF), pltpu.SemaphoreType.DMA((PARTS,))],
        compiler_params=params(),
        name=name,
    )(where, *from_hbm(*parts), rows)


def project(where, parts, d_out):
    return weights_call(project_kernel, where, parts, d_out, WIDTH, "project")


def layer_of(where, parts, attn):
    return weights_call(layer_kernel, where, parts, attn, D, "layer")


def weight_kernel(*refs):
    cols, grads, (dglob, out) = refs[:4], refs[4:8], refs[8:]
    step = pl.program_id(0)

    @pl.when(step == 0)
    def _():
        out[...] = dglob[...]

    @pl.when(step > 0)
    def _():
        part = mm(cols[0][...], grads[0][...], COLS)
        for a in range(1, 4):
            part += mm(cols[a][...], grads[a][...], COLS)
        part = part.astype(BF)
        for i in range(2):
            out[:, 32 * i : 32 * i + 32, :] = part[:, HALF * i : HALF * (i + 1)].reshape(
                CHUNKS, 32, HALF
            )


def weight_payload(cols, grads, dglob):
    return pl.pallas_call(
        weight_kernel,
        grid=(3,),
        in_specs=[pl.BlockSpec((TOK, 256), lambda i: (0, 0))] * 4
        + [pl.BlockSpec((TOK, WIDTH), lambda i: (0, jnp.maximum(i - 1, 0)))] * 4
        + [pl.BlockSpec((CHUNKS, BLK, HALF), lambda i: (0, 0, 0))],
        out_specs=pl.BlockSpec((CHUNKS, BLK, HALF), lambda i: (0, i, 0)),
        out_shape=far((CHUNKS, 192, HALF)),
        compiler_params=params(dimension_semantics=("arbitrary",)),
        name="weight",
    )(*cols, *from_hbm(*grads, dglob))


def halve(where, bit, total, keep, stage):
    rows = keep.shape[0] // 4
    side = (where[11] // (1 << bit)) % 2
    for part in range(4):
        lower = total[2 * rows * part : 2 * rows * part + rows, :]
        upper = total[2 * rows * part + rows : 2 * rows * (part + 1), :]
        keep[rows * part : rows * (part + 1), :] = jnp.where(side == 0, lower, upper)
        stage[rows * part : rows * (part + 1), :] = jnp.where(side == 0, upper, lower)


def first_kernel(bit, where, x, glob, keep, send, total, stage):
    added = jnp.sum(x[...].astype(F32), axis=0)
    glob[...] = added[0:BLK]
    send[0:BLK, :] = added[0:BLK].astype(BF)
    total[...] = added[BLK:]
    halve(where, bit, total, keep, stage)
    send[BLK:, :] = stage[...].astype(BF)


def fold_kernel(bit, where, glob, kept, came, glob_out, keep, send, total, stage):
    added = came[...].astype(F32)
    glob_out[...] = glob[...] + added[0:BLK]
    send[0:BLK, :] = glob_out[...].astype(BF)
    total[...] = kept[...] + added[BLK:]
    halve(where, bit, total, keep, stage)
    send[BLK:, :] = stage[...].astype(BF)


def last_kernel(where, glob, kept, came, out, weight, total):
    added = came[...].astype(F32)
    chunk = (glob[...] + added[0:BLK]).astype(BF)
    target = jnp.where(where[10] == 0, where[8], where[9])
    for j in range(CHUNKS):
        out[j] = jnp.where(target == j, chunk, jnp.zeros_like(chunk))
    total[...] = kept[...] + added[BLK:]
    for part in range(4):
        weight[:, part * HALF : (part + 1) * HALF] = total[4 * part : 4 * part + 4, :]


def fold_call(kernel, where, args, rows, name):
    vm = pl.BlockSpec(memory_space=pltpu.VMEM)
    return pl.pallas_call(
        kernel,
        out_shape=[
            jax.ShapeDtypeStruct((BLK, HALF), F32),
            jax.ShapeDtypeStruct((rows, HALF), F32),
            jax.ShapeDtypeStruct((BLK + rows, HALF), BF),
        ],
        in_specs=[smem()] + [vm] * len(args),
        out_specs=[vm] * 3,
        scratch_shapes=[pltpu.VMEM((2 * rows, HALF), F32), pltpu.VMEM((rows, HALF), F32)],
        compiler_params=params(),
        name=name,
    )(where, *args)


def first(where, x):
    return fold_call(lambda *refs: first_kernel(Z_BITS[0], *refs), where, (x,), 64, "first")


def fold(where, bit, glob, kept, came):
    rows = kept.shape[0] // 2
    return fold_call(lambda *refs: fold_kernel(bit, *refs), where, (glob, kept, came), rows, "fold")


def last(where, glob, kept, came):
    vm = pl.BlockSpec(memory_space=pltpu.VMEM)
    return pl.pallas_call(
        last_kernel,
        out_shape=[far((CHUNKS, BLK, HALF)), far((4, D), F32)],
        in_specs=[smem()] + [vm] * 3,
        out_specs=[vm] * 2,
        scratch_shapes=[pltpu.VMEM((16, HALF), F32)],
        compiler_params=params(),
        name="last",
    )(where, glob, kept, came)


def finish_kernel(where, own, pair, outer, *rest):
    rand, (glob, dk, dv, acc) = rest[: BITS - 1], rest[BITS - 1 :]

    def block(index):
        return pl.ds(pl.multiple_of(index * BLK, BLK), BLK)

    inner = inner_block(where)
    acc[...] = own[...]
    acc[:, block(inner), :] += pair[1].astype(F32)
    acc[:, block(1 - inner), :] += outer[...].astype(F32)
    acc[:, block(where[0]), :] += pair[0].astype(F32)
    for b in range(1, BITS):
        acc[:, block(where[b]), :] += rand[b - 1][...].astype(F32)
    for g in range(GLOB):
        here = where[6 + g]

        @pl.when(here >= 0)
        def _():
            rows = pl.ds(pl.multiple_of(jnp.maximum(here, 0) * BLK, BLK), BLK)
            acc[:, rows, :] += glob[0, :, g].astype(F32)

    dk[...] = acc[0].astype(BF)
    dv[...] = acc[1].astype(BF)


def finish(where, own, pair, outer, rand, glob):
    wide = 512
    block = pl.BlockSpec((2, BLK, wide), lambda i: (0, 0, i))
    two = pl.BlockSpec((2, 2, BLK, wide), lambda i: (0, 0, 0, i))
    flat = pl.BlockSpec((TOK, wide), lambda i: (0, i))
    return pl.pallas_call(
        finish_kernel,
        grid=(WIDTH // wide,),
        in_specs=[smem(), pl.BlockSpec((2, TOK, wide), lambda i: (0, 0, i)), two]
        + [block] * BITS
        + [pl.BlockSpec((1, 2, GLOB, BLK, wide), lambda i: (i, 0, 0, 0, 0))],
        out_specs=[flat, flat],
        out_shape=[far((TOK, WIDTH)), far((TOK, WIDTH))],
        scratch_shapes=[pltpu.VMEM((2, TOK, wide), F32)],
        compiler_params=params(dimension_semantics=("arbitrary",)),
        name="finish",
    )(where, *from_hbm(own, pair, outer, *rand), glob)


def feature_order(rep):
    new = jnp.arange(WIDTH, dtype=jnp.int32)
    stretch = ((new // 64) % 4) * 16 + (new // 32) % 2
    for i, bit in enumerate(Z_BITS):
        stretch = stretch + ((new // (16 >> i)) % 2) * (1 << bit)
    old = stretch * 16 + ((new // 256) ^ rep) * 4 + new % 4
    return (jnp.arange(WIDTH, dtype=jnp.int32)[:, None] == old[None, :]).astype(BF)


def together(*values):
    return lax.optimization_barrier(values)


def per_device(queries, keys, values, w_out, d_out, rand_slot, global_ids):
    q, k, v, grad_out = queries[0], keys[0], values[0], d_out[0]
    where = where_of(rand_slot[0, 0], global_ids[0])
    pair, outer, *chosen, picked = pick(where, k, v)
    rand = dict(zip(range(1, BITS), chosen))
    spread = trade(picked)
    picked, rows = together(picked, w_out)
    parts = [w_out, across(rows, 1), across(rows, 2)]
    order = feature_order(lax.axis_index("rep"))
    for b in FIRST:
        rand[b] = swapped(rand[b], b)
    spread, order, parts[1], own_grad, pair, outer, rand = together(
        spread, order, parts[1], grad_out, pair, outer, rand
    )
    mine = gathered(spread)
    pair = paired(pair)
    outer = neighboured(outer)
    two, three = near(mine, along_z(mine, 1), along_z(mine, -1))
    below, above = along_z(three, 3), along_z(two, -3)
    below, above, pair, outer, parts[2], own_grad, rand = together(
        below, above, pair, outer, parts[2], own_grad, rand
    )
    glob = trade(relay(three, below, above)).reshape(2, 2 * TOK, HALF)
    parts.append(across(parts[2], 1))
    grads = [grad_out, across(own_grad, 1), across(own_grad, 2)]
    for b in THIRD:
        rand[b] = swapped(rand[b], b)
    d_attn = project(where, parts, grad_out)
    glob, d_attn, rand = together(glob, d_attn, rand)
    rand = [rand[b] for b in range(1, BITS)]
    pair, outer, *rand = from_hbm(pair, outer, *rand)
    attn, stats, *ordered = forward(
        where, *from_hbm(q, k, v), pair, outer, rand, glob, *from_hbm(order)
    )
    cols = [ordered[0]] + [across(ordered[a], a) for a in range(1, 4)]
    grads.append(across(grads[2], 1))
    (dq, down, pair, outer), drand, dglob = backward(
        where, q, k, v, pair, outer, rand, glob, stats, d_attn
    )
    back = dict(zip(range(1, BITS), drand))
    cols[1], cols[2], cols[3], grads[1], grads[2], grads[3], dglob = together(
        cols[1], cols[2], cols[3], grads[1], grads[2], grads[3], dglob
    )
    payload = weight_payload(cols, grads, dglob.reshape(CHUNKS, BLK, HALF))
    payload = trade(payload)
    for b in FIRST:
        back[b] = swapped(back[b], b)
    layer = layer_of(where, parts, attn)
    payload, layer, pair, outer, back = together(payload, layer, pair, outer, back)
    pair = paired(pair)
    outer = neighboured(outer)
    glob_sum, keep, send = first(where, payload)
    for step, bit in enumerate(Z_BITS[1:]):
        came = swapped(send, Z_BITS[step])
        glob_sum, keep, send = fold(where, bit, glob_sum, keep, came)
    came = swapped(send, Z_BITS[2])
    came, pair, outer, back = together(came, pair, outer, back)
    routed, weight_grad = last(where, glob_sum, keep, came)
    glob_total = trade(routed).reshape(2, 2, GLOB, BLK, HALF)
    for b in THIRD:
        back[b] = swapped(back[b], b)
    back = [back[b] for b in range(1, BITS)]
    dk, dv = finish(where, down, pair, outer, back, glob_total)
    return (layer[None], dq[None], dk[None], dv[None], weight_grad)


def solution(mesh):
    return jax.shard_map(
        per_device,
        mesh=mesh,
        in_specs=(
            P("rep", "seq", None),
            P("rep", "seq", None),
            P("rep", "seq", None),
            P("rep", None),
            P("rep", "seq", None),
            P("rep", "seq", None),
            P("rep", None),
        ),
        out_specs=(
            P("rep", "seq", None),
            P("rep", "seq", None),
            P("rep", "seq", None),
            P("rep", "seq", None),
            P(("seq", "rep"), None),
        ),
        check_vma=False,
    )
```

```python
import jax
import jax.numpy as jnp
from jax import lax
from jax.experimental import pallas as pl
from jax.experimental.pallas import tpu as pltpu
from jax.sharding import PartitionSpec as P

HEADS = 8
HEAD_DIM = 128
BLK = 64
GLOB = 2
BITS = 6
TOK = 128
WIDTH = HEADS * HEAD_DIM
D = 2048
KEYS = 768
SCALE = HEAD_DIM ** (-0.5)
BF = jnp.bfloat16
F32 = jnp.float32
STEP = 4
WIDE = STEP * HEAD_DIM
ROWS = (((1,), (1,)), ((), ()))
COLS = (((0,), (0,)), ((), ()))
PLAIN = (((1,), (0,)), ((), ()))
VMEM_LIMIT = 20 * 1024 * 1024


def stretch_id(y, z, x):
    return y * 16 + z * 2 + x


YX_GROUPS = [[stretch_id(y, z, x) for y in range(4) for x in range(2)] for z in range(8)]
CHUNKS = 8
PARTS = 6
HALF = WIDTH // 2
Z_BITS = (1, 2, 3)
FIRST, THIRD = (3, 4), (2, 1, 5)


def mm(left, right, dims):
    return lax.dot_general(left, right, dims, preferred_element_type=F32)


def trade(value):
    return lax.all_to_all(value, "seq", 0, 0, axis_index_groups=YX_GROUPS, tiled=True)


def swapped(value, bit):
    return lax.ppermute(value, "seq", [(s, s ^ (1 << bit)) for s in range(64)])


def along_z(value, steps):
    pairs = [(s, s // 16 * 16 + (s // 2 + steps) % 8 * 2 + s % 2) for s in range(64)]
    return lax.ppermute(value, "seq", pairs)


def across(value, flip):
    return lax.ppermute(value, "rep", [(r, r ^ flip) for r in range(4)])


def beside(value):
    pairs = [(s * 4 + r, (s ^ 1) * 4 + (r ^ 2)) for s in range(64) for r in range(4)]
    return lax.ppermute(value, ("seq", "rep"), pairs)


def far(shape, dtype=BF):
    return pltpu.HBM(shape, dtype)


def from_hbm(*values):
    return [pltpu.with_memory_space_constraint(x, pltpu.HBM) for x in values]


def smem():
    return pl.BlockSpec(memory_space=pltpu.SMEM)


def params(**kw):
    return pltpu.CompilerParams(vmem_limit_bytes=VMEM_LIMIT, **kw)


def where_of(rand_slot, global_ids):
    me = lax.axis_index("seq")
    rep = lax.axis_index("rep")
    owner = global_ids // 2
    here = jnp.where(owner == me, global_ids % 2, -1)
    tail = jnp.stack([me % 2, me, rep, rep])
    return jnp.concatenate([rand_slot, here, (owner // 16) * 2 + owner % 2, tail]).astype(
        jnp.int32
    )


def paired(value):
    return swapped(value, 0)


def neighboured(value):
    return lax.ppermute(value, "seq", [(s, (s - 1 + s % 2 * 2) % 64) for s in range(64)])


def inner_block(where):
    return 1 - where[11] % 2


def pick_kernel(where, k_ref, v_ref, pair, outer, *outs):
    def block(index):
        return pl.ds(pl.multiple_of(index * BLK, BLK), BLK)

    inner = inner_block(where)
    for c, src in enumerate((k_ref, v_ref)):
        pair[0, c] = src[block(where[0]), :]
        pair[1, c] = src[block(inner), :]
        outer[c] = src[block(1 - inner), :]
        for b in range(1, BITS):
            outs[b - 1][c] = src[block(where[b]), :]
    picked = outs[BITS - 1]
    for g in range(GLOB):
        here = where[6 + g]
        rows = pl.ds(pl.multiple_of(jnp.maximum(here, 0) * BLK, BLK), BLK)
        for c, src in enumerate((k_ref, v_ref)):
            block = jnp.where(here >= 0, src[rows, :], jnp.zeros((BLK, WIDTH), BF))
            for half in range(2):
                picked[half * 4 + c * 2 + g] = block[:, half * HALF : (half + 1) * HALF]


def pick(where, keys, values):
    block = far((2, BLK, WIDTH))
    outs = [far((2, 2, BLK, WIDTH))] + [block] * BITS + [far((CHUNKS, BLK, HALF))]
    vm = pl.BlockSpec(memory_space=pltpu.VMEM)
    return pl.pallas_call(
        pick_kernel,
        out_shape=outs,
        in_specs=[smem(), vm, vm],
        out_specs=[vm] * len(outs),
        compiler_params=params(),
        name="pick",
    )(where, *from_hbm(keys, values))


def gathered_kernel(x_ref, o_ref):
    o_ref[...] = jnp.sum(x_ref[...].astype(F32), axis=0).astype(BF)


def gathered(x):
    return pl.pallas_call(
        gathered_kernel,
        out_shape=jax.ShapeDtypeStruct((BLK, HALF), BF),
        compiler_params=params(),
        name="gathered",
    )(x)


def near_kernel(mine, below, above, two, three):
    added = mine[...].astype(F32) + below[...].astype(F32)
    two[...] = added.astype(BF)
    three[...] = (added + above[...].astype(F32)).astype(BF)


def near(mine, below, above):
    return pl.pallas_call(
        near_kernel,
        out_shape=[jax.ShapeDtypeStruct((BLK, HALF), BF)] * 2,
        compiler_params=params(),
        name="near",
    )(mine, below, above)


def relay_kernel(mine, below, above, out):
    total = (mine[...].astype(F32) + below[...].astype(F32) + above[...].astype(F32)).astype(BF)
    for j in range(CHUNKS):
        out[j] = total


def relay(mine, below, above):
    return pl.pallas_call(
        relay_kernel,
        out_shape=far((CHUNKS, BLK, HALF)),
        compiler_params=params(),
        name="relay",
    )(mine, below, above)


def gather_heads(where, dst, c, cols, own, pair, outer, rand, glob):
    inner = inner_block(where)
    dst[pl.ds(pl.multiple_of(inner * 192, 64), BLK), :] = pair[1, c, :, cols]
    dst[pl.ds(pl.multiple_of((1 - inner) * 192, 64), BLK), :] = outer[c, :, cols]
    dst[64:192, :] = own[:, cols]
    dst[256:384, :] = glob[0, c * TOK : (c + 1) * TOK, cols]
    dst[384:448, :] = pair[0, c, :, cols]
    for b in range(1, BITS):
        dst[384 + 64 * b : 448 + 64 * b, :] = rand[b - 1][c, :, cols]


def fill_bias(where, bias):
    lane = lax.broadcasted_iota(jnp.int32, (BLK, TOK), 1) // BLK
    for kb in range(12):
        if kb < 4:
            keep = jnp.logical_and(lane <= kb, lane >= kb - 2)
        elif kb < 6:
            keep = lane >= 0
        else:
            keep = lane == where[kb - 6]
        bias[kb * BLK : (kb + 1) * BLK, :] = jnp.where(keep, 0.0, -1e30).astype(F32)


def forward_kernel(where, q, k, v, pair, outer, *rest):
    rand, rest = rest[: BITS - 1], rest[BITS - 1 :]
    glob, perm, attn, stats, *ordered, ks, vs, bias, acc = rest
    step = pl.program_id(0)

    @pl.when(step == 0)
    def _():
        fill_bias(where, bias)

    for i in range(STEP):
        cols = slice(i * HEAD_DIM, (i + 1) * HEAD_DIM)
        gather_heads(where, ks.at[i], 0, cols, k, pair, outer, rand, glob)
        gather_heads(where, vs.at[i], 1, cols, v, pair, outer, rand, glob)
        scores = mm(ks[i], q[:, cols], ROWS) * SCALE + bias[...]
        top = jnp.max(scores, axis=0, keepdims=True)
        expd = jnp.exp(scores - top)
        inv = 1.0 / jnp.sum(expd, axis=0, keepdims=True)
        probs = (expd * inv).astype(BF)
        attn[:, cols] = mm(probs, vs[i], COLS).astype(BF)
        stats[i, 0:1, :] = top
        stats[i, 1:2, :] = inv

    part = mm(attn[...], perm[...], PLAIN)

    @pl.when(step == 0)
    def _():
        acc[...] = part

    @pl.when(step == HEADS // STEP - 1)
    def _():
        total = acc[...] + part
        for r in range(4):
            ordered[r][...] = total[:, r * 256 : (r + 1) * 256].astype(BF)


def head_specs():
    flat = pl.BlockSpec((TOK, WIDE), lambda h: (0, h))
    pair = pl.BlockSpec((2, BLK, WIDE), lambda h: (0, 0, h))
    both = pl.BlockSpec((2, TOK, WIDE), lambda h: (0, 0, h))
    half = pl.BlockSpec((1, 2 * TOK, WIDE), lambda h: (h, 0, 0))
    two = pl.BlockSpec((2, 2, BLK, WIDE), lambda h: (0, 0, 0, h))
    return flat, pair, both, half, two


def forward(where, q, k, v, pair, outer, rand, glob, perm):
    flat, block, both, half, two = head_specs()
    return pl.pallas_call(
        forward_kernel,
        grid=(HEADS // STEP,),
        in_specs=[smem(), flat, flat, flat, two]
        + [block] * BITS
        + [half, pl.BlockSpec((WIDE, WIDTH), lambda h: (h, 0))],
        out_specs=[
            flat,
            pl.BlockSpec((STEP, 8, TOK), lambda h: (h, 0, 0)),
        ]
        + [pl.BlockSpec((TOK, 256), lambda h: (0, 0))] * 4,
        out_shape=[
            far((TOK, WIDTH)),
            far((HEADS, 8, TOK), F32),
        ]
        + [jax.ShapeDtypeStruct((TOK, 256), BF)] * 4,
        scratch_shapes=[
            pltpu.VMEM((STEP, KEYS, HEAD_DIM), BF),
            pltpu.VMEM((STEP, KEYS, HEAD_DIM), BF),
            pltpu.VMEM((KEYS, TOK), F32),
            pltpu.VMEM((TOK, WIDTH), F32),
        ],
        compiler_params=params(dimension_semantics=("arbitrary",)),
        name="forward",
    )(where, q, k, v, pair, outer, *rand, glob, perm)


def backward_kernel(where, q, k, v, pair, outer, *rest):
    rand, rest = rest[: BITS - 1], rest[BITS - 1 :]
    low = inner_block(where) == 0
    glob, stats, *pieces, dq, down, dpair, douter = rest[:10]
    drand, rest = rest[10 : 9 + BITS], rest[9 + BITS :]
    dglob, ks, vs, bias, d_attns = rest

    step = pl.program_id(0)

    @pl.when(step == 0)
    def _():
        fill_bias(where, bias)
        for i in range(4):
            d_attns[i ^ where[13]] = pieces[i][...]

    for i in range(STEP):
        cols = slice(i * HEAD_DIM, (i + 1) * HEAD_DIM)
        gather_heads(where, ks.at[i], 0, cols, k, pair, outer, rand, glob)
        gather_heads(where, vs.at[i], 1, cols, v, pair, outer, rand, glob)
        d_attn = d_attns[step * (STEP // 2) + i // 2, :, i % 2 * HEAD_DIM : (i % 2 + 1) * HEAD_DIM]
        scores = mm(ks[i], q[:, cols], ROWS) * SCALE + bias[...]
        probs = jnp.exp(scores - stats[i, 0:1, :]) * stats[i, 1:2, :]
        probs_b = probs.astype(BF)
        dprob = mm(vs[i], d_attn, ROWS)
        delta = jnp.sum(dprob * probs, axis=0, keepdims=True)
        dscore = (probs * (dprob - delta) * SCALE).astype(BF)
        dq[:, cols] = mm(dscore, ks[i], COLS).astype(BF)
        for c, grad in ((0, mm(dscore, q[:, cols], PLAIN)), (1, mm(probs_b, d_attn, PLAIN))):
            before, after = grad[0:64], grad[192:256]
            dpair[0, c, :, cols] = grad[384:448].astype(BF)
            dpair[1, c, :, cols] = jnp.where(low, before, after).astype(BF)
            douter[c, :, cols] = jnp.where(low, after, before).astype(BF)
            down[c, :, cols] = grad[64:192]
            dglob[0, c * TOK : (c + 1) * TOK, cols] = grad[256:384].astype(BF)
            for b in range(1, BITS):
                drand[b - 1][c, :, cols] = grad[384 + 64 * b : 448 + 64 * b].astype(BF)


def backward(where, q, k, v, pair, outer, rand, glob, stats, pieces):
    flat, block, both, half, two = head_specs()
    out = far((2, BLK, WIDTH))
    outs = pl.pallas_call(
        backward_kernel,
        grid=(HEADS // STEP,),
        in_specs=[smem(), flat, flat, flat, two]
        + [block] * BITS
        + [half, pl.BlockSpec((STEP, 8, TOK), lambda h: (h, 0, 0))]
        + [pl.BlockSpec((TOK, 256), lambda h: (0, 0))] * 4,
        out_specs=[flat, both, two] + [block] * BITS + [half],
        out_shape=[far((TOK, WIDTH)), far((2, TOK, WIDTH), F32), far((2, 2, BLK, WIDTH))]
        + [out] * BITS
        + [far((2, 2 * TOK, HALF))],
        scratch_shapes=[
            pltpu.VMEM((STEP, KEYS, HEAD_DIM), BF),
            pltpu.VMEM((STEP, KEYS, HEAD_DIM), BF),
            pltpu.VMEM((KEYS, TOK), F32),
            pltpu.VMEM((4, TOK, 256), BF),
        ],
        compiler_params=params(dimension_semantics=("arbitrary",)),
        name="backward",
    )(where, *from_hbm(q, k, v, pair, outer, *rand, glob, stats), *pieces)
    return outs[:4], outs[4 : 3 + BITS], outs[3 + BITS]


def place_weights(where, parts, w, sems):
    copies = []
    for i, (rep, half) in enumerate([(0, 0), (1, 0), (2, 0), (2, 1), (3, 0), (3, 1)]):
        head = (rep ^ where[13]) * 2 + half
        rows = pl.ds(pl.multiple_of(head * HEAD_DIM, HEAD_DIM), parts[i].shape[0])
        copies.append(pltpu.make_async_copy(parts[i], w.at[rows, :], sems.at[i]))
    for copy in copies:
        copy.start()
    for copy in copies:
        copy.wait()


def project_kernel(w, *refs):
    for i in range(4):
        refs[4 + i][...] = mm(refs[i][...], w[...], ROWS).astype(BF)


def project(w, grads):
    return pl.pallas_call(
        project_kernel,
        out_shape=[jax.ShapeDtypeStruct((TOK, 256), BF)] * 4,
        compiler_params=params(),
        name="project",
    )(*from_hbm(w, *grads))


def layer_kernel(where, *refs):
    parts, (attn, out, w, sems) = refs[:PARTS], refs[PARTS:]
    place_weights(where, parts, w, sems)
    out[...] = mm(attn[...], w[...], PLAIN).astype(BF)


def weights_call(kernel, where, parts, rows, width, name):
    vm = pl.BlockSpec(memory_space=pltpu.VMEM)
    return pl.pallas_call(
        kernel,
        out_shape=far((TOK, width)),
        in_specs=[smem()] + [pl.BlockSpec(memory_space=pl.ANY)] * PARTS + [vm],
        out_specs=vm,
        scratch_shapes=[pltpu.VMEM((WIDTH, D), BF), pltpu.SemaphoreType.DMA((PARTS,))],
        compiler_params=params(),
        name=name,
    )(where, *from_hbm(*parts), rows)


def layer_of(where, parts, attn):
    return weights_call(layer_kernel, where, parts, attn, D, "layer")


def weight_kernel(*refs):
    cols, grads, (dglob, out) = refs[:4], refs[4:8], refs[8:]
    step = pl.program_id(0)

    @pl.when(step == 0)
    def _():
        out[...] = dglob[...]

    @pl.when(step > 0)
    def _():
        part = mm(cols[0][...], grads[0][...], COLS)
        for a in range(1, 4):
            part += mm(cols[a][...], grads[a][...], COLS)
        part = part.astype(BF)
        for i in range(2):
            out[:, 32 * i : 32 * i + 32, :] = part[:, HALF * i : HALF * (i + 1)].reshape(
                CHUNKS, 32, HALF
            )


def weight_payload(cols, grads, dglob):
    return pl.pallas_call(
        weight_kernel,
        grid=(3,),
        in_specs=[pl.BlockSpec((TOK, 256), lambda i: (0, 0))] * 4
        + [pl.BlockSpec((TOK, WIDTH), lambda i: (0, jnp.maximum(i - 1, 0)))] * 4
        + [pl.BlockSpec((CHUNKS, BLK, HALF), lambda i: (0, 0, 0))],
        out_specs=pl.BlockSpec((CHUNKS, BLK, HALF), lambda i: (0, i, 0)),
        out_shape=far((CHUNKS, 192, HALF)),
        compiler_params=params(dimension_semantics=("arbitrary",)),
        name="weight",
    )(*cols, *from_hbm(*grads, dglob))


def halve(where, bit, total, keep, stage):
    rows = keep.shape[0] // 4
    side = (where[11] // (1 << bit)) % 2
    for part in range(4):
        lower = total[2 * rows * part : 2 * rows * part + rows, :]
        upper = total[2 * rows * part + rows : 2 * rows * (part + 1), :]
        keep[rows * part : rows * (part + 1), :] = jnp.where(side == 0, lower, upper)
        stage[rows * part : rows * (part + 1), :] = jnp.where(side == 0, upper, lower)


def first_kernel(bit, where, x, glob, keep, send, total, stage):
    added = jnp.sum(x[...].astype(F32), axis=0)
    glob[...] = added[0:BLK]
    send[0:BLK, :] = added[0:BLK].astype(BF)
    total[...] = added[BLK:]
    halve(where, bit, total, keep, stage)
    send[BLK:, :] = stage[...].astype(BF)


def fold_kernel(bit, where, glob, kept, came, glob_out, keep, send, total, stage):
    added = came[...].astype(F32)
    glob_out[...] = glob[...] + added[0:BLK]
    send[0:BLK, :] = glob_out[...].astype(BF)
    total[...] = kept[...] + added[BLK:]
    halve(where, bit, total, keep, stage)
    send[BLK:, :] = stage[...].astype(BF)


def last_kernel(where, glob, kept, came, out, weight, total):
    added = came[...].astype(F32)
    chunk = (glob[...] + added[0:BLK]).astype(BF)
    target = jnp.where(where[10] == 0, where[8], where[9])
    for j in range(CHUNKS):
        out[j] = jnp.where(target == j, chunk, jnp.zeros_like(chunk))
    total[...] = kept[...] + added[BLK:]
    for part in range(4):
        weight[:, part * HALF : (part + 1) * HALF] = total[4 * part : 4 * part + 4, :]


def fold_call(kernel, where, args, rows, name):
    vm = pl.BlockSpec(memory_space=pltpu.VMEM)
    return pl.pallas_call(
        kernel,
        out_shape=[
            jax.ShapeDtypeStruct((BLK, HALF), F32),
            jax.ShapeDtypeStruct((rows, HALF), F32),
            jax.ShapeDtypeStruct((BLK + rows, HALF), BF),
        ],
        in_specs=[smem()] + [vm] * len(args),
        out_specs=[vm] * 3,
        scratch_shapes=[pltpu.VMEM((2 * rows, HALF), F32), pltpu.VMEM((rows, HALF), F32)],
        compiler_params=params(),
        name=name,
    )(where, *args)


def first(where, x):
    return fold_call(lambda *refs: first_kernel(Z_BITS[0], *refs), where, (x,), 64, "first")


def fold(where, bit, glob, kept, came):
    rows = kept.shape[0] // 2
    return fold_call(lambda *refs: fold_kernel(bit, *refs), where, (glob, kept, came), rows, "fold")


def last(where, glob, kept, came):
    vm = pl.BlockSpec(memory_space=pltpu.VMEM)
    return pl.pallas_call(
        last_kernel,
        out_shape=[far((CHUNKS, BLK, HALF)), far((4, D), F32)],
        in_specs=[smem()] + [vm] * 3,
        out_specs=[vm] * 2,
        scratch_shapes=[pltpu.VMEM((16, HALF), F32)],
        compiler_params=params(),
        name="last",
    )(where, glob, kept, came)


def finish_kernel(where, own, pair, outer, *rest):
    rand, (glob, dk, dv, acc) = rest[: BITS - 1], rest[BITS - 1 :]

    def block(index):
        return pl.ds(pl.multiple_of(index * BLK, BLK), BLK)

    inner = inner_block(where)
    acc[...] = own[...]
    acc[:, block(inner), :] += pair[1].astype(F32)
    acc[:, block(1 - inner), :] += outer[...].astype(F32)
    acc[:, block(where[0]), :] += pair[0].astype(F32)
    for b in range(1, BITS):
        acc[:, block(where[b]), :] += rand[b - 1][...].astype(F32)
    for g in range(GLOB):
        here = where[6 + g]

        @pl.when(here >= 0)
        def _():
            rows = pl.ds(pl.multiple_of(jnp.maximum(here, 0) * BLK, BLK), BLK)
            acc[:, rows, :] += glob[0, :, g].astype(F32)

    dk[...] = acc[0].astype(BF)
    dv[...] = acc[1].astype(BF)


def finish(where, own, pair, outer, rand, glob):
    wide = 512
    block = pl.BlockSpec((2, BLK, wide), lambda i: (0, 0, i))
    two = pl.BlockSpec((2, 2, BLK, wide), lambda i: (0, 0, 0, i))
    flat = pl.BlockSpec((TOK, wide), lambda i: (0, i))
    return pl.pallas_call(
        finish_kernel,
        grid=(WIDTH // wide,),
        in_specs=[smem(), pl.BlockSpec((2, TOK, wide), lambda i: (0, 0, i)), two]
        + [block] * BITS
        + [pl.BlockSpec((1, 2, GLOB, BLK, wide), lambda i: (i, 0, 0, 0, 0))],
        out_specs=[flat, flat],
        out_shape=[far((TOK, WIDTH)), far((TOK, WIDTH))],
        scratch_shapes=[pltpu.VMEM((2, TOK, wide), F32)],
        compiler_params=params(dimension_semantics=("arbitrary",)),
        name="finish",
    )(where, *from_hbm(own, pair, outer, *rand), glob)


def feature_order(rep):
    new = jnp.arange(WIDTH, dtype=jnp.int32)
    stretch = ((new // 64) % 4) * 16 + (new // 32) % 2
    for i, bit in enumerate(Z_BITS):
        stretch = stretch + ((new // (16 >> i)) % 2) * (1 << bit)
    old = stretch * 16 + ((new // 256) ^ rep) * 4 + new % 4
    return (jnp.arange(WIDTH, dtype=jnp.int32)[:, None] == old[None, :]).astype(BF)


def together(*values):
    return lax.optimization_barrier(values)


def per_device(queries, keys, values, w_out, d_out, rand_slot, global_ids):
    q, k, v, grad_out = queries[0], keys[0], values[0], d_out[0]
    where = where_of(rand_slot[0, 0], global_ids[0])
    pair, outer, *chosen, picked = pick(where, k, v)
    rand = dict(zip(range(1, BITS), chosen))
    spread = trade(picked)
    picked, own_grad = together(picked, grad_out)
    grads = [grad_out, across(own_grad, 1), across(own_grad, 2)]
    order = feature_order(lax.axis_index("rep"))
    for b in FIRST:
        rand[b] = swapped(rand[b], b)
    spread, order, grads, pair, outer, rand, lower, upper = together(
        spread, order, grads, pair, outer, rand, w_out[:HEAD_DIM], w_out[HEAD_DIM:]
    )
    mine = gathered(spread)
    two, three = near(mine, along_z(mine, 1), along_z(mine, -1))
    two, three, outer = together(two, three, outer)
    below, above = along_z(three, 3), along_z(two, -3)
    outer = neighboured(outer)
    below, above, pair, grads, rand = together(below, above, pair, grads, rand)
    glob = trade(relay(three, below, above)).reshape(2, 2 * TOK, HALF)
    grads.append(across(grads[2], 1))
    pair = paired(pair)
    for b in THIRD:
        rand[b] = swapped(rand[b], b)
    pieces = project(w_out, grads)
    glob, pieces, pair, outer, rand = together(glob, pieces, pair, outer, rand)
    pieces = [pieces[0]] + [across(pieces[a], a) for a in range(1, 4)]
    rand = [rand[b] for b in range(1, BITS)]
    pair, outer, *rand = from_hbm(pair, outer, *rand)
    attn, stats, *ordered = forward(
        where, *from_hbm(q, k, v), pair, outer, rand, glob, *from_hbm(order)
    )
    cols = [ordered[0]] + [across(ordered[a], a) for a in range(1, 4)]
    (dq, down, pair, outer), drand, dglob = backward(
        where, q, k, v, pair, outer, rand, glob, stats, pieces
    )
    back = dict(zip(range(1, BITS), drand))
    cols, dglob = together(cols, dglob)
    payload = weight_payload(cols, grads, dglob.reshape(CHUNKS, BLK, HALF))
    payload = trade(payload)
    back[3] = swapped(back[3], 3)
    payload, pair, outer, back, lower, upper, w_own = together(
        payload, pair, outer, back, lower, upper, w_out
    )
    parts = [w_out, across(w_own, 1), across(lower, 2), beside(upper)]
    back[4] = swapped(back[4], 4)
    outer = neighboured(outer)
    glob_sum, keep, send = first(where, payload)
    for step, bit in enumerate(Z_BITS[1:]):
        came = swapped(send, Z_BITS[step])
        glob_sum, keep, send = fold(where, bit, glob_sum, keep, came)
    came = swapped(send, Z_BITS[2])
    came, pair, outer, back, parts = together(came, pair, outer, back, parts)
    parts += [across(parts[2], 1), across(parts[3], 1)]
    routed, weight_grad = last(where, glob_sum, keep, came)
    glob_total = trade(routed).reshape(2, 2, GLOB, BLK, HALF)
    pair = paired(pair)
    for b in THIRD:
        back[b] = swapped(back[b], b)
    back = [back[b] for b in range(1, BITS)]
    layer = layer_of(where, parts, attn)
    glob_total, layer = together(glob_total, layer)
    dk, dv = finish(where, down, pair, outer, back, glob_total)
    return (layer[None], dq[None], dk[None], dv[None], weight_grad)


def solution(mesh):
    return jax.shard_map(
        per_device,
        mesh=mesh,
        in_specs=(
            P("rep", "seq", None),
            P("rep", "seq", None),
            P("rep", "seq", None),
            P("rep", None),
            P("rep", "seq", None),
            P("rep", "seq", None),
            P("rep", None),
        ),
        out_specs=(
            P("rep", "seq", None),
            P("rep", "seq", None),
            P("rep", "seq", None),
            P("rep", "seq", None),
            P(("seq", "rep"), None),
        ),
        check_vma=False,
    )
```

```python
import jax
import jax.numpy as jnp
from jax import lax
from jax.experimental import pallas as pl
from jax.experimental.pallas import tpu as pltpu
from jax.sharding import PartitionSpec as P

HEADS = 8
HEAD_DIM = 128
BLK = 64
GLOB = 2
BITS = 6
TOK = 128
WIDTH = HEADS * HEAD_DIM
D = 2048
KEYS = 768
SCALE = HEAD_DIM ** (-0.5)
BF = jnp.bfloat16
F32 = jnp.float32
STEP = 4
WIDE = STEP * HEAD_DIM
ROWS = (((1,), (1,)), ((), ()))
COLS = (((0,), (0,)), ((), ()))
PLAIN = (((1,), (0,)), ((), ()))
VMEM_LIMIT = 20 * 1024 * 1024


def stretch_id(y, z, x):
    return y * 16 + z * 2 + x


YX_GROUPS = [[stretch_id(y, z, x) for y in range(4) for x in range(2)] for z in range(8)]
CHUNKS = 8
PARTS = 6
HALF = WIDTH // 2
Z_BITS = (1, 2, 3)
FIRST, THIRD = (3, 4), (2, 1, 5)


def mm(left, right, dims):
    return lax.dot_general(left, right, dims, preferred_element_type=F32)


def trade(value):
    return lax.all_to_all(value, "seq", 0, 0, axis_index_groups=YX_GROUPS, tiled=True)


def swapped(value, bit):
    return lax.ppermute(value, "seq", [(s, s ^ (1 << bit)) for s in range(64)])


def along_z(value, steps):
    pairs = [(s, s // 16 * 16 + (s // 2 + steps) % 8 * 2 + s % 2) for s in range(64)]
    return lax.ppermute(value, "seq", pairs)


def across(value, flip):
    return lax.ppermute(value, "rep", [(r, r ^ flip) for r in range(4)])


def beside(value):
    pairs = [(s * 4 + r, (s ^ 1) * 4 + (r ^ 2)) for s in range(64) for r in range(4)]
    return lax.ppermute(value, ("seq", "rep"), pairs)


def far(shape, dtype=BF):
    return pltpu.HBM(shape, dtype)


def from_hbm(*values):
    return [pltpu.with_memory_space_constraint(x, pltpu.HBM) for x in values]


def smem():
    return pl.BlockSpec(memory_space=pltpu.SMEM)


def params(**kw):
    return pltpu.CompilerParams(vmem_limit_bytes=VMEM_LIMIT, **kw)


def where_of(rand_slot, global_ids):
    me = lax.axis_index("seq")
    rep = lax.axis_index("rep")
    owner = global_ids // 2
    here = jnp.where(owner == me, global_ids % 2, -1)
    tail = jnp.stack([me % 2, me, rep, rep])
    return jnp.concatenate([rand_slot, here, (owner // 16) * 2 + owner % 2, tail]).astype(
        jnp.int32
    )


def paired(value):
    return swapped(value, 0)


def neighboured(value):
    return lax.ppermute(value, "seq", [(s, (s - 1 + s % 2 * 2) % 64) for s in range(64)])


def inner_block(where):
    return 1 - where[11] % 2


def pick_kernel(me_ref, slots, gids, k_ref, v_ref, pair, outer, *outs):
    def block(index):
        return pl.ds(pl.multiple_of(index * BLK, BLK), BLK)

    me = me_ref[0]
    inner = 1 - me % 2
    for c, src in enumerate((k_ref, v_ref)):
        pair[0, c] = src[block(slots[0]), :]
        pair[1, c] = src[block(inner), :]
        outer[c] = src[block(1 - inner), :]
        for b in range(1, BITS):
            outs[b - 1][c] = src[block(slots[b]), :]
    picked = outs[BITS - 1]
    for g in range(GLOB):
        here = jnp.where(gids[g] // 2 == me, gids[g] % 2, -1)
        rows = pl.ds(pl.multiple_of(jnp.maximum(here, 0) * BLK, BLK), BLK)
        for c, src in enumerate((k_ref, v_ref)):
            block = jnp.where(here >= 0, src[rows, :], jnp.zeros((BLK, WIDTH), BF))
            for half in range(2):
                picked[half * 4 + c * 2 + g] = block[:, half * HALF : (half + 1) * HALF]


def pick(me, slots, gids, keys, values):
    block = far((2, BLK, WIDTH))
    outs = [far((2, 2, BLK, WIDTH))] + [block] * BITS + [far((CHUNKS, BLK, HALF))]
    vm = pl.BlockSpec(memory_space=pltpu.VMEM)
    return pl.pallas_call(
        pick_kernel,
        out_shape=outs,
        in_specs=[smem()] * 3 + [vm, vm],
        out_specs=[vm] * len(outs),
        compiler_params=params(),
        name="pick",
    )(me, slots, gids, *from_hbm(keys, values))


def gathered_kernel(x_ref, o_ref):
    o_ref[...] = jnp.sum(x_ref[...].astype(F32), axis=0).astype(BF)


def gathered(x):
    return pl.pallas_call(
        gathered_kernel,
        out_shape=jax.ShapeDtypeStruct((BLK, HALF), BF),
        compiler_params=params(),
        name="gathered",
    )(x)


def near_kernel(mine, below, above, two, three):
    added = mine[...].astype(F32) + below[...].astype(F32)
    two[...] = added.astype(BF)
    three[...] = (added + above[...].astype(F32)).astype(BF)


def near(mine, below, above):
    return pl.pallas_call(
        near_kernel,
        out_shape=[jax.ShapeDtypeStruct((BLK, HALF), BF)] * 2,
        compiler_params=params(),
        name="near",
    )(mine, below, above)


def relay_kernel(mine, below, above, out):
    total = (mine[...].astype(F32) + below[...].astype(F32) + above[...].astype(F32)).astype(BF)
    for j in range(CHUNKS):
        out[j] = total


def relay(mine, below, above):
    return pl.pallas_call(
        relay_kernel,
        out_shape=far((CHUNKS, BLK, HALF)),
        compiler_params=params(),
        name="relay",
    )(mine, below, above)


def gather_heads(where, dst, c, cols, own, pair, outer, rand, glob):
    inner = inner_block(where)
    dst[pl.ds(pl.multiple_of(inner * 192, 64), BLK), :] = pair[1, c, :, cols]
    dst[pl.ds(pl.multiple_of((1 - inner) * 192, 64), BLK), :] = outer[c, :, cols]
    dst[64:192, :] = own[:, cols]
    dst[256:384, :] = glob[0, c * TOK : (c + 1) * TOK, cols]
    dst[384:448, :] = pair[0, c, :, cols]
    for b in range(1, BITS):
        dst[384 + 64 * b : 448 + 64 * b, :] = rand[b - 1][c, :, cols]


def fill_bias(where, bias):
    lane = lax.broadcasted_iota(jnp.int32, (BLK, TOK), 1) // BLK
    for kb in range(12):
        if kb < 4:
            keep = jnp.logical_and(lane <= kb, lane >= kb - 2)
        elif kb < 6:
            keep = lane >= 0
        else:
            keep = lane == where[kb - 6]
        bias[kb * BLK : (kb + 1) * BLK, :] = jnp.where(keep, 0.0, -1e30).astype(F32)


def forward_kernel(where, q, k, v, pair, outer, *rest):
    rand, rest = rest[: BITS - 1], rest[BITS - 1 :]
    glob, perm, attn, stats, *ordered, ks, vs, bias, acc = rest
    step = pl.program_id(0)

    @pl.when(step == 0)
    def _():
        fill_bias(where, bias)

    for i in range(STEP):
        cols = slice(i * HEAD_DIM, (i + 1) * HEAD_DIM)
        gather_heads(where, ks.at[i], 0, cols, k, pair, outer, rand, glob)
        gather_heads(where, vs.at[i], 1, cols, v, pair, outer, rand, glob)
        scores = mm(ks[i], q[:, cols], ROWS) * SCALE + bias[...]
        top = jnp.max(scores, axis=0, keepdims=True)
        expd = jnp.exp(scores - top)
        inv = 1.0 / jnp.sum(expd, axis=0, keepdims=True)
        probs = (expd * inv).astype(BF)
        attn[:, cols] = mm(probs, vs[i], COLS).astype(BF)
        stats[i, 0:1, :] = top
        stats[i, 1:2, :] = inv

    part = mm(attn[...], perm[...], PLAIN)

    @pl.when(step == 0)
    def _():
        acc[...] = part

    @pl.when(step == HEADS // STEP - 1)
    def _():
        total = acc[...] + part
        for r in range(4):
            ordered[r][...] = total[:, r * 256 : (r + 1) * 256].astype(BF)


def head_specs():
    flat = pl.BlockSpec((TOK, WIDE), lambda h: (0, h))
    pair = pl.BlockSpec((2, BLK, WIDE), lambda h: (0, 0, h))
    both = pl.BlockSpec((2, TOK, WIDE), lambda h: (0, 0, h))
    half = pl.BlockSpec((1, 2 * TOK, WIDE), lambda h: (h, 0, 0))
    two = pl.BlockSpec((2, 2, BLK, WIDE), lambda h: (0, 0, 0, h))
    return flat, pair, both, half, two


def forward(where, q, k, v, pair, outer, rand, glob, perm):
    flat, block, both, half, two = head_specs()
    return pl.pallas_call(
        forward_kernel,
        grid=(HEADS // STEP,),
        in_specs=[smem(), flat, flat, flat, two]
        + [block] * BITS
        + [half, pl.BlockSpec((WIDE, WIDTH), lambda h: (h, 0))],
        out_specs=[
            flat,
            pl.BlockSpec((STEP, 8, TOK), lambda h: (h, 0, 0)),
        ]
        + [pl.BlockSpec((TOK, 256), lambda h: (0, 0))] * 4,
        out_shape=[
            far((TOK, WIDTH)),
            far((HEADS, 8, TOK), F32),
        ]
        + [jax.ShapeDtypeStruct((TOK, 256), BF)] * 4,
        scratch_shapes=[
            pltpu.VMEM((STEP, KEYS, HEAD_DIM), BF),
            pltpu.VMEM((STEP, KEYS, HEAD_DIM), BF),
            pltpu.VMEM((KEYS, TOK), F32),
            pltpu.VMEM((TOK, WIDTH), F32),
        ],
        compiler_params=params(dimension_semantics=("arbitrary",)),
        name="forward",
    )(where, q, k, v, pair, outer, *rand, glob, perm)


def backward_kernel(where, q, k, v, pair, outer, *rest):
    rand, rest = rest[: BITS - 1], rest[BITS - 1 :]
    low = inner_block(where) == 0
    glob, stats, *pieces, dq, down, dpair, douter = rest[:10]
    drand, rest = rest[10 : 9 + BITS], rest[9 + BITS :]
    dglob, ks, vs, bias, d_attns = rest

    step = pl.program_id(0)

    @pl.when(step == 0)
    def _():
        fill_bias(where, bias)
        for i in range(4):
            d_attns[i ^ where[13]] = pieces[i][...]

    for i in range(STEP):
        cols = slice(i * HEAD_DIM, (i + 1) * HEAD_DIM)
        gather_heads(where, ks.at[i], 0, cols, k, pair, outer, rand, glob)
        gather_heads(where, vs.at[i], 1, cols, v, pair, outer, rand, glob)
        d_attn = d_attns[step * (STEP // 2) + i // 2, :, i % 2 * HEAD_DIM : (i % 2 + 1) * HEAD_DIM]
        scores = mm(ks[i], q[:, cols], ROWS) * SCALE + bias[...]
        probs = jnp.exp(scores - stats[i, 0:1, :]) * stats[i, 1:2, :]
        probs_b = probs.astype(BF)
        dprob = mm(vs[i], d_attn, ROWS)
        delta = jnp.sum(dprob * probs, axis=0, keepdims=True)
        dscore = (probs * (dprob - delta) * SCALE).astype(BF)
        dq[:, cols] = mm(dscore, ks[i], COLS).astype(BF)
        for c, grad in ((0, mm(dscore, q[:, cols], PLAIN)), (1, mm(probs_b, d_attn, PLAIN))):
            before, after = grad[0:64], grad[192:256]
            dpair[0, c, :, cols] = grad[384:448].astype(BF)
            dpair[1, c, :, cols] = jnp.where(low, before, after).astype(BF)
            douter[c, :, cols] = jnp.where(low, after, before).astype(BF)
            down[c, :, cols] = grad[64:192]
            dglob[0, c * TOK : (c + 1) * TOK, cols] = grad[256:384].astype(BF)
            for b in range(1, BITS):
                drand[b - 1][c, :, cols] = grad[384 + 64 * b : 448 + 64 * b].astype(BF)


def backward(where, q, k, v, pair, outer, rand, glob, stats, pieces):
    flat, block, both, half, two = head_specs()
    out = far((2, BLK, WIDTH))
    outs = pl.pallas_call(
        backward_kernel,
        grid=(HEADS // STEP,),
        in_specs=[smem(), flat, flat, flat, two]
        + [block] * BITS
        + [half, pl.BlockSpec((STEP, 8, TOK), lambda h: (h, 0, 0))]
        + [pl.BlockSpec((TOK, 256), lambda h: (0, 0))] * 4,
        out_specs=[flat, both, two] + [block] * BITS + [half],
        out_shape=[far((TOK, WIDTH)), far((2, TOK, WIDTH), F32), far((2, 2, BLK, WIDTH))]
        + [out] * BITS
        + [far((2, 2 * TOK, HALF))],
        scratch_shapes=[
            pltpu.VMEM((STEP, KEYS, HEAD_DIM), BF),
            pltpu.VMEM((STEP, KEYS, HEAD_DIM), BF),
            pltpu.VMEM((KEYS, TOK), F32),
            pltpu.VMEM((4, TOK, 256), BF),
        ],
        compiler_params=params(dimension_semantics=("arbitrary",)),
        name="backward",
    )(where, *from_hbm(q, k, v, pair, outer, *rand, glob, stats), *pieces)
    return outs[:4], outs[4 : 3 + BITS], outs[3 + BITS]


def place_weights(where, parts, w, sems):
    copies = []
    for i, (rep, half) in enumerate([(0, 0), (1, 0), (2, 0), (2, 1), (3, 0), (3, 1)]):
        head = (rep ^ where[13]) * 2 + half
        rows = pl.ds(pl.multiple_of(head * HEAD_DIM, HEAD_DIM), parts[i].shape[0])
        copies.append(pltpu.make_async_copy(parts[i], w.at[rows, :], sems.at[i]))
    for copy in copies:
        copy.start()
    for copy in copies:
        copy.wait()


def project_kernel(w, *refs):
    for i in range(4):
        refs[4 + i][...] = mm(refs[i][...], w[...], ROWS).astype(BF)


def project(w, grads):
    return pl.pallas_call(
        project_kernel,
        out_shape=[jax.ShapeDtypeStruct((TOK, 256), BF)] * 4,
        compiler_params=params(),
        name="project",
    )(*from_hbm(w, *grads))


def layer_kernel(where, *refs):
    parts, (attn, out, w, sems) = refs[:PARTS], refs[PARTS:]
    place_weights(where, parts, w, sems)
    out[...] = mm(attn[...], w[...], PLAIN).astype(BF)


def weights_call(kernel, where, parts, rows, width, name):
    vm = pl.BlockSpec(memory_space=pltpu.VMEM)
    return pl.pallas_call(
        kernel,
        out_shape=far((TOK, width)),
        in_specs=[smem()] + [pl.BlockSpec(memory_space=pl.ANY)] * PARTS + [vm],
        out_specs=vm,
        scratch_shapes=[pltpu.VMEM((WIDTH, D), BF), pltpu.SemaphoreType.DMA((PARTS,))],
        compiler_params=params(),
        name=name,
    )(where, *from_hbm(*parts), rows)


def layer_of(where, parts, attn):
    return weights_call(layer_kernel, where, parts, attn, D, "layer")


def weight_kernel(*refs):
    cols, grads, (dglob, out) = refs[:4], refs[4:8], refs[8:]
    step = pl.program_id(0)

    @pl.when(step == 0)
    def _():
        out[...] = dglob[...]

    @pl.when(step > 0)
    def _():
        left = jnp.concatenate([ref[...] for ref in cols])
        right = jnp.concatenate([ref[...] for ref in grads])
        part = mm(left, right, COLS).astype(BF)
        for i in range(2):
            out[:, 32 * i : 32 * i + 32, :] = part[:, HALF * i : HALF * (i + 1)].reshape(
                CHUNKS, 32, HALF
            )


def weight_payload(cols, grads, dglob):
    return pl.pallas_call(
        weight_kernel,
        grid=(3,),
        in_specs=[pl.BlockSpec((TOK, 256), lambda i: (0, 0))] * 4
        + [pl.BlockSpec((TOK, WIDTH), lambda i: (0, jnp.maximum(i - 1, 0)))] * 4
        + [pl.BlockSpec((CHUNKS, BLK, HALF), lambda i: (0, 0, 0))],
        out_specs=pl.BlockSpec((CHUNKS, BLK, HALF), lambda i: (0, i, 0)),
        out_shape=far((CHUNKS, 192, HALF)),
        compiler_params=params(dimension_semantics=("arbitrary",)),
        name="weight",
    )(*cols, *from_hbm(*grads, dglob))


def halve(where, bit, total, keep, stage):
    rows = keep.shape[0] // 4
    side = (where[11] // (1 << bit)) % 2
    for part in range(4):
        lower = total[2 * rows * part : 2 * rows * part + rows, :]
        upper = total[2 * rows * part + rows : 2 * rows * (part + 1), :]
        keep[rows * part : rows * (part + 1), :] = jnp.where(side == 0, lower, upper)
        stage[rows * part : rows * (part + 1), :] = jnp.where(side == 0, upper, lower)


def first_kernel(bit, where, x, glob, keep, send, total, stage):
    added = jnp.sum(x[...].astype(F32), axis=0)
    glob[...] = added[0:BLK]
    send[0:BLK, :] = added[0:BLK].astype(BF)
    total[...] = added[BLK:]
    halve(where, bit, total, keep, stage)
    send[BLK:, :] = stage[...].astype(BF)


def fold_kernel(bit, where, glob, kept, came, glob_out, keep, send, total, stage):
    added = came[...].astype(F32)
    glob_out[...] = glob[...] + added[0:BLK]
    send[0:BLK, :] = glob_out[...].astype(BF)
    total[...] = kept[...] + added[BLK:]
    halve(where, bit, total, keep, stage)
    send[BLK:, :] = stage[...].astype(BF)


def last_kernel(where, glob, kept, came, out, weight, total):
    added = came[...].astype(F32)
    chunk = (glob[...] + added[0:BLK]).astype(BF)
    target = jnp.where(where[10] == 0, where[8], where[9])
    for j in range(CHUNKS):
        out[j] = jnp.where(target == j, chunk, jnp.zeros_like(chunk))
    total[...] = kept[...] + added[BLK:]
    for part in range(4):
        weight[:, part * HALF : (part + 1) * HALF] = total[4 * part : 4 * part + 4, :]


def fold_call(kernel, where, args, rows, name):
    vm = pl.BlockSpec(memory_space=pltpu.VMEM)
    return pl.pallas_call(
        kernel,
        out_shape=[
            jax.ShapeDtypeStruct((BLK, HALF), F32),
            jax.ShapeDtypeStruct((rows, HALF), F32),
            jax.ShapeDtypeStruct((BLK + rows, HALF), BF),
        ],
        in_specs=[smem()] + [vm] * len(args),
        out_specs=[vm] * 3,
        scratch_shapes=[pltpu.VMEM((2 * rows, HALF), F32), pltpu.VMEM((rows, HALF), F32)],
        compiler_params=params(),
        name=name,
    )(where, *args)


def first(where, x):
    return fold_call(lambda *refs: first_kernel(Z_BITS[0], *refs), where, (x,), 64, "first")


def fold(where, bit, glob, kept, came):
    rows = kept.shape[0] // 2
    return fold_call(lambda *refs: fold_kernel(bit, *refs), where, (glob, kept, came), rows, "fold")


def last(where, glob, kept, came):
    vm = pl.BlockSpec(memory_space=pltpu.VMEM)
    return pl.pallas_call(
        last_kernel,
        out_shape=[far((CHUNKS, BLK, HALF)), far((4, D), F32)],
        in_specs=[smem()] + [vm] * 3,
        out_specs=[vm] * 2,
        scratch_shapes=[pltpu.VMEM((16, HALF), F32)],
        compiler_params=params(),
        name="last",
    )(where, glob, kept, came)


def finish_kernel(where, own, pair, outer, *rest):
    rand, (glob, dk, dv, acc) = rest[: BITS - 1], rest[BITS - 1 :]

    def block(index):
        return pl.ds(pl.multiple_of(index * BLK, BLK), BLK)

    inner = inner_block(where)
    acc[...] = own[...]
    acc[:, block(inner), :] += pair[1].astype(F32)
    acc[:, block(1 - inner), :] += outer[...].astype(F32)
    acc[:, block(where[0]), :] += pair[0].astype(F32)
    for b in range(1, BITS):
        acc[:, block(where[b]), :] += rand[b - 1][...].astype(F32)
    for g in range(GLOB):
        here = where[6 + g]

        @pl.when(here >= 0)
        def _():
            rows = pl.ds(pl.multiple_of(jnp.maximum(here, 0) * BLK, BLK), BLK)
            acc[:, rows, :] += glob[0, :, g].astype(F32)

    dk[...] = acc[0].astype(BF)
    dv[...] = acc[1].astype(BF)


def finish(where, own, pair, outer, rand, glob):
    wide = 512
    block = pl.BlockSpec((2, BLK, wide), lambda i: (0, 0, i))
    two = pl.BlockSpec((2, 2, BLK, wide), lambda i: (0, 0, 0, i))
    flat = pl.BlockSpec((TOK, wide), lambda i: (0, i))
    return pl.pallas_call(
        finish_kernel,
        grid=(WIDTH // wide,),
        in_specs=[smem(), pl.BlockSpec((2, TOK, wide), lambda i: (0, 0, i)), two]
        + [block] * BITS
        + [pl.BlockSpec((1, 2, GLOB, BLK, wide), lambda i: (i, 0, 0, 0, 0))],
        out_specs=[flat, flat],
        out_shape=[far((TOK, WIDTH)), far((TOK, WIDTH))],
        scratch_shapes=[pltpu.VMEM((2, TOK, wide), F32)],
        compiler_params=params(dimension_semantics=("arbitrary",)),
        name="finish",
    )(where, *from_hbm(own, pair, outer, *rand), glob)


def feature_order(rep):
    new = jnp.arange(WIDTH, dtype=jnp.int32)
    stretch = ((new // 64) % 4) * 16 + (new // 32) % 2
    for i, bit in enumerate(Z_BITS):
        stretch = stretch + ((new // (16 >> i)) % 2) * (1 << bit)
    old = stretch * 16 + ((new // 256) ^ rep) * 4 + new % 4
    return (jnp.arange(WIDTH, dtype=jnp.int32)[:, None] == old[None, :]).astype(BF)


def together(*values):
    return lax.optimization_barrier(values)


def per_device(queries, keys, values, w_out, d_out, rand_slot, global_ids):
    q, k, v, grad_out = queries[0], keys[0], values[0], d_out[0]
    me = jnp.full((1,), lax.axis_index("seq"), jnp.int32)
    pair, outer, *chosen, picked = pick(me, rand_slot[0, 0], global_ids[0], k, v)
    rand = dict(zip(range(1, BITS), chosen))
    spread = trade(picked)
    picked, own_grad, slots, gids = together(picked, grad_out, rand_slot[0, 0], global_ids[0])
    where = where_of(slots, gids)
    grads = [grad_out, across(own_grad, 1), across(own_grad, 2)]
    order = feature_order(lax.axis_index("rep"))
    for b in FIRST:
        rand[b] = swapped(rand[b], b)
    spread, order, grads, pair, outer, rand, lower, upper = together(
        spread, order, grads, pair, outer, rand, w_out[:HEAD_DIM], w_out[HEAD_DIM:]
    )
    mine = gathered(spread)
    two, three = near(mine, along_z(mine, 1), along_z(mine, -1))
    two, three, outer = together(two, three, outer)
    below, above = along_z(three, 3), along_z(two, -3)
    outer = neighboured(outer)
    below, above, pair, grads, rand = together(below, above, pair, grads, rand)
    glob = trade(relay(three, below, above)).reshape(2, 2 * TOK, HALF)
    grads.append(across(grads[2], 1))
    pair = paired(pair)
    for b in THIRD:
        rand[b] = swapped(rand[b], b)
    pieces = project(w_out, grads)
    glob, pieces, pair, outer, rand = together(glob, pieces, pair, outer, rand)
    pieces = [pieces[0]] + [across(pieces[a], a) for a in range(1, 4)]
    rand = [rand[b] for b in range(1, BITS)]
    pair, outer, *rand = from_hbm(pair, outer, *rand)
    attn, stats, *ordered = forward(
        where, *from_hbm(q, k, v), pair, outer, rand, glob, *from_hbm(order)
    )
    cols = [ordered[0]] + [across(ordered[a], a) for a in range(1, 4)]
    (dq, down, pair, outer), drand, dglob = backward(
        where, q, k, v, pair, outer, rand, glob, stats, pieces
    )
    back = dict(zip(range(1, BITS), drand))
    cols, dglob = together(cols, dglob)
    payload = weight_payload(cols, grads, dglob.reshape(CHUNKS, BLK, HALF))
    payload, w_own = together(payload, w_out)
    payload = trade(payload)
    back[3] = swapped(back[3], 3)
    w_core = across(w_own, 1)
    payload, pair, outer, back, lower, upper, w_core = together(
        payload, pair, outer, back, lower, upper, w_core
    )
    parts = [w_out, w_core, across(lower, 2), beside(upper)]
    back[4] = swapped(back[4], 4)
    outer = neighboured(outer)
    glob_sum, keep, send = first(where, payload)
    for step, bit in enumerate(Z_BITS[1:]):
        came = swapped(send, Z_BITS[step])
        glob_sum, keep, send = fold(where, bit, glob_sum, keep, came)
    came = swapped(send, Z_BITS[2])
    came, pair, outer, back, parts = together(came, pair, outer, back, parts)
    parts += [across(parts[2], 1), across(parts[3], 1)]
    routed, weight_grad = last(where, glob_sum, keep, came)
    glob_total = trade(routed).reshape(2, 2, GLOB, BLK, HALF)
    pair = paired(pair)
    for b in THIRD:
        back[b] = swapped(back[b], b)
    back = [back[b] for b in range(1, BITS)]
    layer = layer_of(where, parts, attn)
    glob_total, layer = together(glob_total, layer)
    dk, dv = finish(where, down, pair, outer, back, glob_total)
    return (layer[None], dq[None], dk[None], dv[None], weight_grad)


def solution(mesh):
    return jax.shard_map(
        per_device,
        mesh=mesh,
        in_specs=(
            P("rep", "seq", None),
            P("rep", "seq", None),
            P("rep", "seq", None),
            P("rep", None),
            P("rep", "seq", None),
            P("rep", "seq", None),
            P("rep", None),
        ),
        out_specs=(
            P("rep", "seq", None),
            P("rep", "seq", None),
            P("rep", "seq", None),
            P("rep", "seq", None),
            P(("seq", "rep"), None),
        ),
        check_vma=False,
    )
```

```python
import jax
import jax.numpy as jnp
from jax import lax
from jax.experimental import pallas as pl
from jax.experimental.pallas import tpu as pltpu
from jax.sharding import PartitionSpec as P

HEADS = 8
HEAD_DIM = 128
BLK = 64
GLOB = 2
BITS = 6
TOK = 128
WIDTH = HEADS * HEAD_DIM
D = 2048
KEYS = 768
SCALE = HEAD_DIM ** (-0.5)
BF = jnp.bfloat16
F32 = jnp.float32
STEP = 4
WIDE = STEP * HEAD_DIM
ROWS = (((1,), (1,)), ((), ()))
COLS = (((0,), (0,)), ((), ()))
PLAIN = (((1,), (0,)), ((), ()))
VMEM_LIMIT = 20 * 1024 * 1024


def stretch_id(y, z, x):
    return y * 16 + z * 2 + x


YX_GROUPS = [[stretch_id(y, z, x) for y in range(4) for x in range(2)] for z in range(8)]
CHUNKS = 8
PARTS = 6
HALF = WIDTH // 2
Z_BITS = (1, 2, 3)
FIRST, THIRD = (3, 4, 5), (2, 1)


def mm(left, right, dims):
    return lax.dot_general(left, right, dims, preferred_element_type=F32)


def trade(value):
    return lax.all_to_all(value, "seq", 0, 0, axis_index_groups=YX_GROUPS, tiled=True)


def swapped(value, bit):
    return lax.ppermute(value, "seq", [(s, s ^ (1 << bit)) for s in range(64)])


def along_z(value, steps):
    pairs = [(s, s // 16 * 16 + (s // 2 + steps) % 8 * 2 + s % 2) for s in range(64)]
    return lax.ppermute(value, "seq", pairs)


def across(value, flip):
    return lax.ppermute(value, "rep", [(r, r ^ flip) for r in range(4)])


def beside(value):
    pairs = [(s * 4 + r, (s ^ 1) * 4 + (r ^ 2)) for s in range(64) for r in range(4)]
    return lax.ppermute(value, ("seq", "rep"), pairs)


def far(shape, dtype=BF):
    return pltpu.HBM(shape, dtype)


def from_hbm(*values):
    return [pltpu.with_memory_space_constraint(x, pltpu.HBM) for x in values]


def smem():
    return pl.BlockSpec(memory_space=pltpu.SMEM)


def params(**kw):
    return pltpu.CompilerParams(vmem_limit_bytes=VMEM_LIMIT, **kw)


def where_of(rand_slot, global_ids):
    me = lax.axis_index("seq")
    rep = lax.axis_index("rep")
    owner = global_ids // 2
    here = jnp.where(owner == me, global_ids % 2, -1)
    tail = jnp.stack([me % 2, me, rep, rep])
    return jnp.concatenate([rand_slot, here, (owner // 16) * 2 + owner % 2, tail]).astype(
        jnp.int32
    )


def paired(value):
    return swapped(value, 0)


def neighboured(value):
    return lax.ppermute(value, "seq", [(s, (s - 1 + s % 2 * 2) % 64) for s in range(64)])


def inner_block(where):
    return 1 - where[11] % 2


def pick_kernel(me_ref, slots, gids, k_ref, v_ref, pair, outer, *outs):
    def block(index):
        return pl.ds(pl.multiple_of(index * BLK, BLK), BLK)

    me = me_ref[0]
    inner = 1 - me % 2
    for c, src in enumerate((k_ref, v_ref)):
        pair[0, c] = src[block(slots[0]), :]
        pair[1, c] = src[block(inner), :]
        outer[c] = src[block(1 - inner), :]
        for b in range(1, BITS):
            outs[b - 1][c] = src[block(slots[b]), :]
    picked = outs[BITS - 1]
    for g in range(GLOB):
        here = jnp.where(gids[g] // 2 == me, gids[g] % 2, -1)
        rows = pl.ds(pl.multiple_of(jnp.maximum(here, 0) * BLK, BLK), BLK)
        for c, src in enumerate((k_ref, v_ref)):
            block = jnp.where(here >= 0, src[rows, :], jnp.zeros((BLK, WIDTH), BF))
            for half in range(2):
                picked[half * 4 + c * 2 + g] = block[:, half * HALF : (half + 1) * HALF]


def pick(me, slots, gids, keys, values):
    block = far((2, BLK, WIDTH))
    outs = [far((2, 2, BLK, WIDTH))] + [block] * BITS + [far((CHUNKS, BLK, HALF))]
    vm = pl.BlockSpec(memory_space=pltpu.VMEM)
    return pl.pallas_call(
        pick_kernel,
        out_shape=outs,
        in_specs=[smem()] * 3 + [vm, vm],
        out_specs=[vm] * len(outs),
        compiler_params=params(),
        name="pick",
    )(me, slots, gids, *from_hbm(keys, values))


def gathered_kernel(x_ref, o_ref):
    o_ref[...] = jnp.sum(x_ref[...].astype(F32), axis=0).astype(BF)


def gathered(x):
    return pl.pallas_call(
        gathered_kernel,
        out_shape=jax.ShapeDtypeStruct((BLK, HALF), BF),
        compiler_params=params(),
        name="gathered",
    )(x)


def near_kernel(mine, below, above, two, three):
    added = mine[...].astype(F32) + below[...].astype(F32)
    two[...] = added.astype(BF)
    three[...] = (added + above[...].astype(F32)).astype(BF)


def near(mine, below, above):
    return pl.pallas_call(
        near_kernel,
        out_shape=[jax.ShapeDtypeStruct((BLK, HALF), BF)] * 2,
        compiler_params=params(),
        name="near",
    )(mine, below, above)


def relay_kernel(mine, below, above, out):
    total = (mine[...].astype(F32) + below[...].astype(F32) + above[...].astype(F32)).astype(BF)
    for j in range(CHUNKS):
        out[j] = total


def relay(mine, below, above):
    return pl.pallas_call(
        relay_kernel,
        out_shape=far((CHUNKS, BLK, HALF)),
        compiler_params=params(),
        name="relay",
    )(mine, below, above)


def gather_heads(where, dst, c, cols, own, pair, outer, rand, glob):
    inner = inner_block(where)
    dst[pl.ds(pl.multiple_of(inner * 192, 64), BLK), :] = pair[1, c, :, cols]
    dst[pl.ds(pl.multiple_of((1 - inner) * 192, 64), BLK), :] = outer[c, :, cols]
    dst[64:192, :] = own[:, cols]
    dst[256:384, :] = glob[0, c * TOK : (c + 1) * TOK, cols]
    dst[384:448, :] = pair[0, c, :, cols]
    for b in range(1, BITS):
        dst[384 + 64 * b : 448 + 64 * b, :] = rand[b - 1][c, :, cols]


def fill_bias(where, bias):
    lane = lax.broadcasted_iota(jnp.int32, (BLK, TOK), 1) // BLK
    for kb in range(12):
        if kb < 4:
            keep = jnp.logical_and(lane <= kb, lane >= kb - 2)
        elif kb < 6:
            keep = lane >= 0
        else:
            keep = lane == where[kb - 6]
        bias[kb * BLK : (kb + 1) * BLK, :] = jnp.where(keep, 0.0, -1e30).astype(F32)


def forward_kernel(where, q, k, v, pair, outer, *rest):
    rand, rest = rest[: BITS - 1], rest[BITS - 1 :]
    glob, perm, attn, stats, *ordered, ks, vs, bias, acc = rest
    step = pl.program_id(0)

    @pl.when(step == 0)
    def _():
        fill_bias(where, bias)

    for i in range(STEP):
        cols = slice(i * HEAD_DIM, (i + 1) * HEAD_DIM)
        gather_heads(where, ks.at[i], 0, cols, k, pair, outer, rand, glob)
        gather_heads(where, vs.at[i], 1, cols, v, pair, outer, rand, glob)
        scores = mm(ks[i], q[:, cols], ROWS) * SCALE + bias[...]
        top = jnp.max(scores, axis=0, keepdims=True)
        expd = jnp.exp(scores - top)
        inv = 1.0 / jnp.sum(expd, axis=0, keepdims=True)
        probs = (expd * inv).astype(BF)
        attn[:, cols] = mm(probs, vs[i], COLS).astype(BF)
        stats[i, 0:1, :] = top
        stats[i, 1:2, :] = inv

    part = mm(attn[...], perm[...], PLAIN)

    @pl.when(step == 0)
    def _():
        acc[...] = part

    @pl.when(step == HEADS // STEP - 1)
    def _():
        total = acc[...] + part
        for r in range(4):
            ordered[r][...] = total[:, r * 256 : (r + 1) * 256].astype(BF)


def head_specs():
    flat = pl.BlockSpec((TOK, WIDE), lambda h: (0, h))
    pair = pl.BlockSpec((2, BLK, WIDE), lambda h: (0, 0, h))
    both = pl.BlockSpec((2, TOK, WIDE), lambda h: (0, 0, h))
    half = pl.BlockSpec((1, 2 * TOK, WIDE), lambda h: (h, 0, 0))
    two = pl.BlockSpec((2, 2, BLK, WIDE), lambda h: (0, 0, 0, h))
    return flat, pair, both, half, two


def forward(where, q, k, v, pair, outer, rand, glob, perm):
    flat, block, both, half, two = head_specs()
    return pl.pallas_call(
        forward_kernel,
        grid=(HEADS // STEP,),
        in_specs=[smem(), flat, flat, flat, two]
        + [block] * BITS
        + [half, pl.BlockSpec((WIDE, WIDTH), lambda h: (h, 0))],
        out_specs=[
            flat,
            pl.BlockSpec((STEP, 8, TOK), lambda h: (h, 0, 0)),
        ]
        + [pl.BlockSpec((TOK, 256), lambda h: (0, 0))] * 4,
        out_shape=[
            far((TOK, WIDTH)),
            far((HEADS, 8, TOK), F32),
        ]
        + [jax.ShapeDtypeStruct((TOK, 256), BF)] * 4,
        scratch_shapes=[
            pltpu.VMEM((STEP, KEYS, HEAD_DIM), BF),
            pltpu.VMEM((STEP, KEYS, HEAD_DIM), BF),
            pltpu.VMEM((KEYS, TOK), F32),
            pltpu.VMEM((TOK, WIDTH), F32),
        ],
        compiler_params=params(dimension_semantics=("arbitrary",)),
        name="forward",
    )(where, q, k, v, pair, outer, *rand, glob, perm)


def backward_kernel(where, q, k, v, pair, outer, *rest):
    rand, rest = rest[: BITS - 1], rest[BITS - 1 :]
    low = inner_block(where) == 0
    glob, stats, *pieces, dq, down, dpair, douter = rest[:10]
    drand, rest = rest[10 : 9 + BITS], rest[9 + BITS :]
    dglob, ks, vs, bias, d_attns = rest

    step = pl.program_id(0)

    @pl.when(step == 0)
    def _():
        fill_bias(where, bias)
        for i in range(4):
            d_attns[i ^ where[13]] = pieces[i][...]

    for i in range(STEP):
        cols = slice(i * HEAD_DIM, (i + 1) * HEAD_DIM)
        gather_heads(where, ks.at[i], 0, cols, k, pair, outer, rand, glob)
        gather_heads(where, vs.at[i], 1, cols, v, pair, outer, rand, glob)
        d_attn = d_attns[step * (STEP // 2) + i // 2, :, i % 2 * HEAD_DIM : (i % 2 + 1) * HEAD_DIM]
        scores = mm(ks[i], q[:, cols], ROWS) * SCALE + bias[...]
        probs = jnp.exp(scores - stats[i, 0:1, :]) * stats[i, 1:2, :]
        probs_b = probs.astype(BF)
        dprob = mm(vs[i], d_attn, ROWS)
        delta = jnp.sum(dprob * probs, axis=0, keepdims=True)
        dscore = (probs * (dprob - delta) * SCALE).astype(BF)
        dq[:, cols] = mm(dscore, ks[i], COLS).astype(BF)
        for c, grad in ((0, mm(dscore, q[:, cols], PLAIN)), (1, mm(probs_b, d_attn, PLAIN))):
            before, after = grad[0:64], grad[192:256]
            dpair[0, c, :, cols] = grad[384:448].astype(BF)
            dpair[1, c, :, cols] = jnp.where(low, before, after).astype(BF)
            douter[c, :, cols] = jnp.where(low, after, before).astype(BF)
            down[c, :, cols] = grad[64:192]
            dglob[0, c * TOK : (c + 1) * TOK, cols] = grad[256:384].astype(BF)
            for b in range(1, BITS):
                drand[b - 1][c, :, cols] = grad[384 + 64 * b : 448 + 64 * b].astype(BF)


def backward(where, q, k, v, pair, outer, rand, glob, stats, pieces):
    flat, block, both, half, two = head_specs()
    out = far((2, BLK, WIDTH))
    outs = pl.pallas_call(
        backward_kernel,
        grid=(HEADS // STEP,),
        in_specs=[smem(), flat, flat, flat, two]
        + [block] * BITS
        + [half, pl.BlockSpec((STEP, 8, TOK), lambda h: (h, 0, 0))]
        + [pl.BlockSpec((TOK, 256), lambda h: (0, 0))] * 4,
        out_specs=[flat, both, two] + [block] * BITS + [half],
        out_shape=[far((TOK, WIDTH)), far((2, TOK, WIDTH), F32), far((2, 2, BLK, WIDTH))]
        + [out] * BITS
        + [far((2, 2 * TOK, HALF))],
        scratch_shapes=[
            pltpu.VMEM((STEP, KEYS, HEAD_DIM), BF),
            pltpu.VMEM((STEP, KEYS, HEAD_DIM), BF),
            pltpu.VMEM((KEYS, TOK), F32),
            pltpu.VMEM((4, TOK, 256), BF),
        ],
        compiler_params=params(dimension_semantics=("arbitrary",)),
        name="backward",
    )(where, *from_hbm(q, k, v, pair, outer, *rand, glob, stats), *pieces)
    return outs[:4], outs[4 : 3 + BITS], outs[3 + BITS]


def place_weights(where, parts, w, sems):
    copies = []
    for i, (rep, half) in enumerate([(0, 0), (1, 0), (2, 0), (2, 1), (3, 0), (3, 1)]):
        head = (rep ^ where[13]) * 2 + half
        rows = pl.ds(pl.multiple_of(head * HEAD_DIM, HEAD_DIM), parts[i].shape[0])
        copies.append(pltpu.make_async_copy(parts[i], w.at[rows, :], sems.at[i]))
    for copy in copies:
        copy.start()
    for copy in copies:
        copy.wait()


def project_kernel(w, *refs):
    for i in range(4):
        refs[4 + i][...] = mm(refs[i][...], w[...], ROWS).astype(BF)


def project(w, grads):
    return pl.pallas_call(
        project_kernel,
        out_shape=[jax.ShapeDtypeStruct((TOK, 256), BF)] * 4,
        compiler_params=params(),
        name="project",
    )(*from_hbm(w, *grads))


def layer_kernel(where, *refs):
    parts, (attn, out, w, sems) = refs[:PARTS], refs[PARTS:]
    place_weights(where, parts, w, sems)
    out[...] = mm(attn[...], w[...], PLAIN).astype(BF)


def weights_call(kernel, where, parts, rows, width, name):
    vm = pl.BlockSpec(memory_space=pltpu.VMEM)
    return pl.pallas_call(
        kernel,
        out_shape=far((TOK, width)),
        in_specs=[smem()] + [pl.BlockSpec(memory_space=pl.ANY)] * PARTS + [vm],
        out_specs=vm,
        scratch_shapes=[pltpu.VMEM((WIDTH, D), BF), pltpu.SemaphoreType.DMA((PARTS,))],
        compiler_params=params(),
        name=name,
    )(where, *from_hbm(*parts), rows)


def layer_of(where, parts, attn):
    return weights_call(layer_kernel, where, parts, attn, D, "layer")


def weight_kernel(*refs):
    cols, grads, (dglob, out) = refs[:4], refs[4:8], refs[8:]
    step = pl.program_id(0)

    @pl.when(step == 0)
    def _():
        out[...] = dglob[...]

    @pl.when(step > 0)
    def _():
        left = jnp.concatenate([ref[...] for ref in cols])
        right = jnp.concatenate([ref[...] for ref in grads])
        part = mm(left, right, COLS).astype(BF)
        for i in range(2):
            out[:, 32 * i : 32 * i + 32, :] = part[:, HALF * i : HALF * (i + 1)].reshape(
                CHUNKS, 32, HALF
            )


def weight_payload(cols, grads, dglob):
    return pl.pallas_call(
        weight_kernel,
        grid=(3,),
        in_specs=[pl.BlockSpec((TOK, 256), lambda i: (0, 0))] * 4
        + [pl.BlockSpec((TOK, WIDTH), lambda i: (0, jnp.maximum(i - 1, 0)))] * 4
        + [pl.BlockSpec((CHUNKS, BLK, HALF), lambda i: (0, 0, 0))],
        out_specs=pl.BlockSpec((CHUNKS, BLK, HALF), lambda i: (0, i, 0)),
        out_shape=far((CHUNKS, 192, HALF)),
        compiler_params=params(dimension_semantics=("arbitrary",)),
        name="weight",
    )(*cols, *from_hbm(*grads, dglob))


def halve(where, bit, total, keep, stage):
    rows = keep.shape[0] // 4
    side = (where[11] // (1 << bit)) % 2
    for part in range(4):
        lower = total[2 * rows * part : 2 * rows * part + rows, :]
        upper = total[2 * rows * part + rows : 2 * rows * (part + 1), :]
        keep[rows * part : rows * (part + 1), :] = jnp.where(side == 0, lower, upper)
        stage[rows * part : rows * (part + 1), :] = jnp.where(side == 0, upper, lower)


def first_kernel(bit, where, x, glob, keep, send, total, stage):
    added = jnp.sum(x[...].astype(F32), axis=0)
    glob[...] = added[0:BLK]
    send[0:BLK, :] = added[0:BLK].astype(BF)
    total[...] = added[BLK:]
    halve(where, bit, total, keep, stage)
    send[BLK:, :] = stage[...].astype(BF)


def fold_kernel(bit, where, glob, kept, came, glob_out, keep, send, total, stage):
    added = came[...].astype(F32)
    glob_out[...] = glob[...] + added[0:BLK]
    send[0:BLK, :] = glob_out[...].astype(BF)
    total[...] = kept[...] + added[BLK:]
    halve(where, bit, total, keep, stage)
    send[BLK:, :] = stage[...].astype(BF)


def last_kernel(where, glob, kept, came, out, weight, total):
    added = came[...].astype(F32)
    chunk = (glob[...] + added[0:BLK]).astype(BF)
    target = jnp.where(where[10] == 0, where[8], where[9])
    for j in range(CHUNKS):
        out[j] = jnp.where(target == j, chunk, jnp.zeros_like(chunk))
    total[...] = kept[...] + added[BLK:]
    for part in range(4):
        weight[:, part * HALF : (part + 1) * HALF] = total[4 * part : 4 * part + 4, :]


def fold_call(kernel, where, args, rows, name):
    vm = pl.BlockSpec(memory_space=pltpu.VMEM)
    return pl.pallas_call(
        kernel,
        out_shape=[
            jax.ShapeDtypeStruct((BLK, HALF), F32),
            jax.ShapeDtypeStruct((rows, HALF), F32),
            jax.ShapeDtypeStruct((BLK + rows, HALF), BF),
        ],
        in_specs=[smem()] + [vm] * len(args),
        out_specs=[vm] * 3,
        scratch_shapes=[pltpu.VMEM((2 * rows, HALF), F32), pltpu.VMEM((rows, HALF), F32)],
        compiler_params=params(),
        name=name,
    )(where, *args)


def first(where, x):
    return fold_call(lambda *refs: first_kernel(Z_BITS[0], *refs), where, (x,), 64, "first")


def fold(where, bit, glob, kept, came):
    rows = kept.shape[0] // 2
    return fold_call(lambda *refs: fold_kernel(bit, *refs), where, (glob, kept, came), rows, "fold")


def last(where, glob, kept, came):
    vm = pl.BlockSpec(memory_space=pltpu.VMEM)
    return pl.pallas_call(
        last_kernel,
        out_shape=[far((CHUNKS, BLK, HALF)), far((4, D), F32)],
        in_specs=[smem()] + [vm] * 3,
        out_specs=[vm] * 2,
        scratch_shapes=[pltpu.VMEM((16, HALF), F32)],
        compiler_params=params(),
        name="last",
    )(where, glob, kept, came)


def finish_kernel(where, own, pair, outer, *rest):
    rand, (glob, dk, dv, acc) = rest[: BITS - 1], rest[BITS - 1 :]

    def block(index):
        return pl.ds(pl.multiple_of(index * BLK, BLK), BLK)

    inner = inner_block(where)
    acc[...] = own[...]
    acc[:, block(inner), :] += pair[1].astype(F32)
    acc[:, block(1 - inner), :] += outer[...].astype(F32)
    acc[:, block(where[0]), :] += pair[0].astype(F32)
    for b in range(1, BITS):
        acc[:, block(where[b]), :] += rand[b - 1][...].astype(F32)
    for g in range(GLOB):
        here = where[6 + g]

        @pl.when(here >= 0)
        def _():
            rows = pl.ds(pl.multiple_of(jnp.maximum(here, 0) * BLK, BLK), BLK)
            acc[:, rows, :] += glob[0, :, g].astype(F32)

    dk[...] = acc[0].astype(BF)
    dv[...] = acc[1].astype(BF)


def finish(where, own, pair, outer, rand, glob):
    wide = 512
    block = pl.BlockSpec((2, BLK, wide), lambda i: (0, 0, i))
    two = pl.BlockSpec((2, 2, BLK, wide), lambda i: (0, 0, 0, i))
    flat = pl.BlockSpec((TOK, wide), lambda i: (0, i))
    return pl.pallas_call(
        finish_kernel,
        grid=(WIDTH // wide,),
        in_specs=[smem(), pl.BlockSpec((2, TOK, wide), lambda i: (0, 0, i)), two]
        + [block] * BITS
        + [pl.BlockSpec((1, 2, GLOB, BLK, wide), lambda i: (i, 0, 0, 0, 0))],
        out_specs=[flat, flat],
        out_shape=[far((TOK, WIDTH)), far((TOK, WIDTH))],
        scratch_shapes=[pltpu.VMEM((2, TOK, wide), F32)],
        compiler_params=params(dimension_semantics=("arbitrary",)),
        name="finish",
    )(where, *from_hbm(own, pair, outer, *rand), glob)


def feature_order(rep):
    new = jnp.arange(WIDTH, dtype=jnp.int32)
    stretch = ((new // 64) % 4) * 16 + (new // 32) % 2
    for i, bit in enumerate(Z_BITS):
        stretch = stretch + ((new // (16 >> i)) % 2) * (1 << bit)
    old = stretch * 16 + ((new // 256) ^ rep) * 4 + new % 4
    return (jnp.arange(WIDTH, dtype=jnp.int32)[:, None] == old[None, :]).astype(BF)


def together(*values):
    return lax.optimization_barrier(values)


def per_device(queries, keys, values, w_out, d_out, rand_slot, global_ids):
    q, k, v, grad_out = queries[0], keys[0], values[0], d_out[0]
    me = jnp.full((1,), lax.axis_index("seq"), jnp.int32)
    pair, outer, *chosen, picked = pick(me, rand_slot[0, 0], global_ids[0], k, v)
    rand = dict(zip(range(1, BITS), chosen))
    spread = trade(picked)
    picked, own_grad, slots, gids = together(picked, grad_out, rand_slot[0, 0], global_ids[0])
    where = where_of(slots, gids)
    grads = [grad_out, across(own_grad, 1), across(own_grad, 2)]
    order = feature_order(lax.axis_index("rep"))
    for b in FIRST:
        rand[b] = swapped(rand[b], b)
    first_done = [rand[b] for b in FIRST]
    spread, first_done, order, grads, pair, outer, rand, lower, upper = together(
        spread, first_done, order, grads, pair, outer, rand, w_out[:HEAD_DIM], w_out[HEAD_DIM:]
    )
    rand.update(zip(FIRST, first_done))
    mine = gathered(spread)
    two, three = near(mine, along_z(mine, 1), along_z(mine, -1))
    two, three, outer = together(two, three, outer)
    below, above = along_z(three, 3), along_z(two, -3)
    outer = neighboured(outer)
    below, above, pair, grads, rand = together(below, above, pair, grads, rand)
    glob = trade(relay(three, below, above)).reshape(2, 2 * TOK, HALF)
    grads.append(across(grads[2], 1))
    pair = paired(pair)
    for b in THIRD:
        rand[b] = swapped(rand[b], b)
    pieces = project(w_out, grads)
    pieces = [pieces[0]] + [across(pieces[a], a) for a in range(1, 4)]
    third_done = [rand[b] for b in THIRD]
    glob, third_done, outer, pair, pieces, rand = together(
        glob, third_done, outer, pair, pieces, rand
    )
    rand.update(zip(THIRD, third_done))
    rand = [rand[b] for b in range(1, BITS)]
    pair, outer, *rand = from_hbm(pair, outer, *rand)
    attn, stats, *ordered = forward(
        where, *from_hbm(q, k, v), pair, outer, rand, glob, *from_hbm(order)
    )
    cols = [ordered[0]] + [across(ordered[a], a) for a in range(1, 4)]
    (dq, down, pair, outer), drand, dglob = backward(
        where, q, k, v, pair, outer, rand, glob, stats, pieces
    )
    back = dict(zip(range(1, BITS), drand))
    cols, dglob = together(cols, dglob)
    payload = weight_payload(cols, grads, dglob.reshape(CHUNKS, BLK, HALF))
    payload, w_own = together(payload, w_out)
    payload = trade(payload)
    back[3] = swapped(back[3], 3)
    w_core = across(w_own, 1)
    payload, pair, outer, back, lower, upper, w_core = together(
        payload, pair, outer, back, lower, upper, w_core
    )
    parts = [w_out, w_core, across(lower, 2), beside(upper)]
    back[4] = swapped(back[4], 4)
    outer = neighboured(outer)
    glob_sum, keep, send = first(where, payload)
    for step, bit in enumerate(Z_BITS[1:]):
        came = swapped(send, Z_BITS[step])
        glob_sum, keep, send = fold(where, bit, glob_sum, keep, came)
    came = swapped(send, Z_BITS[2])
    came, pair, outer, back, parts = together(came, pair, outer, back, parts)
    parts += [across(parts[2], 1), across(parts[3], 1)]
    routed, weight_grad = last(where, glob_sum, keep, came)
    glob_total = trade(routed).reshape(2, 2, GLOB, BLK, HALF)
    pair = paired(pair)
    for b in THIRD + (5,):
        back[b] = swapped(back[b], b)
    back = [back[b] for b in range(1, BITS)]
    layer = layer_of(where, parts, attn)
    glob_total, layer = together(glob_total, layer)
    dk, dv = finish(where, down, pair, outer, back, glob_total)
    return (layer[None], dq[None], dk[None], dv[None], weight_grad)


def solution(mesh):
    return jax.shard_map(
        per_device,
        mesh=mesh,
        in_specs=(
            P("rep", "seq", None),
            P("rep", "seq", None),
            P("rep", "seq", None),
            P("rep", None),
            P("rep", "seq", None),
            P("rep", "seq", None),
            P("rep", None),
        ),
        out_specs=(
            P("rep", "seq", None),
            P("rep", "seq", None),
            P("rep", "seq", None),
            P("rep", "seq", None),
            P(("seq", "rep"), None),
        ),
        check_vma=False,
    )
```
